32 devices in a mesh: dp: 4 (over x, core), tok: 8 (over z, y).
Axes of the slice: x: 2, y: 2, z: 4, core: 2. Of those that a mesh axis runs over, the one named last changes fastest.
Arguments:
- tokens: bfloat16 [8, 1024, 768], P('dp', 'tok'), may hold values from -6 to 6
- mask: int32 [8, 1024], P('dp', 'tok'), may hold values 0 or 1
- segments: int32 [8, 1024], P('dp', 'tok'), may hold values from 0 to 3, as said below
- replacement: float32 [768], replicated, may hold values from -6 to 6
- w_qkv: bfloat16 [768, 2, 2304], replicated, may hold values from -0.21875 to 0.21875
- w_out: bfloat16 [768, 2, 768], replicated, may hold values from -0.875 to 0.875
- w_in: bfloat16 [768, 2, 6144], replicated, may hold values from -0.21875 to 0.21875
- w_down: bfloat16 [3072, 2, 768], replicated, may hold values from -0.109375 to 0.109375
- ln_gain: float32 [2, 2, 768], replicated, may hold values from 0.5 to 1.5
- ln_bias: float32 [2, 2, 768], replicated, may hold values from -1 to 1
- cotangent: bfloat16 [8, 1024, 768], P('dp', 'tok'), may hold values from -6 to 6
Outputs:
- layer_out: bfloat16 [8, 1024, 768], P('dp', 'tok')
- grad_tokens: float32 [8, 1024, 768], P('dp', 'tok')
- grad_replacement: float32 [768], P('tok')
- grad_w_qkv: float32 [768, 2, 2304], P('tok')
- grad_w_out: float32 [768, 2, 768], P('tok')
- grad_w_in: float32 [768, 2, 6144], P('tok')
- grad_w_down: float32 [3072, 2, 768], P('tok')
- grad_gain: float32 [2, 2, 768], P(None, None, 'tok')
- grad_bias: float32 [2, 2, 768], P(None, None, 'tok')
The draws below stay inside these ranges and needn't reach their ends.
Inputs may be any that keep to these rules, and one draw needn't show every extreme that they name: `segments`: along each sequence the ids start at 0 and never fall. Each sequence holds either one document or exactly 4. In each aligned group of 2 sequences exactly one, at a place drawn from the seed, is a single document.
All inputs are finite; a program needn't handle non-finite values. No bound on the sum of `mask` on one device may be relied on, other than what follows from the above.
Results may differ from the reference program's by a relative error of at most 0.025.
Values may be sent and summed in bfloat16 or wider, within the bound.
No kernel may reach another device: no remote copies, remote signals or barrier semaphores. Data moves between devices by JAX's collectives and lax.ppermute only.
A program may use at most 384 MiB of HBM per device.

```python
import math
import jax
import jax.numpy as jnp
from jax import lax

D = 768
HEADS = 12
HEAD_DIM = 64
FF = 3072
LAYERS = 2
LEN = 1024
DOCS = 4
GROUP_SEQS = 2
SEQS = 8


def draw_segments(key, part):
    key = jax.random.fold_in(key, 7)
    cut_key, pick_key = jax.random.split(key)

    def one_row(row_key):
        shuffled = jax.random.permutation(row_key, LEN - 1)
        boundary = shuffled[:DOCS - 1] + 1
        position = jnp.arange(LEN, dtype=jnp.int32)
        return jnp.sum((position[:, None] >= boundary[None, :]).astype(jnp.int32), axis=1)
    labels = jax.vmap(one_row)(jax.random.split(cut_key, SEQS))
    chosen = jax.random.randint(pick_key, (SEQS // GROUP_SEQS,), 0, GROUP_SEQS)
    row_index = jnp.arange(SEQS, dtype=jnp.int32)
    single = row_index % GROUP_SEQS == chosen[row_index // GROUP_SEQS]
    return jnp.where(single[:, None], 0, labels).astype(jnp.int32)


def with_ends(values, own_key, smallest, top_value):
    index_at = [jax.random.randint(jax.random.fold_in(own_key, axis), (), 0, length) for axis, length in enumerate(values.shape)]
    widest = values.shape.index(max(values.shape))
    beside = index_at[:widest] + [(index_at[widest] + 1) % values.shape[widest]] + index_at[widest + 1:]
    return values.at[tuple(index_at)].set(smallest).at[tuple(beside)].set(top_value)


def steps_of(key, shape, shards, smallest, largest):
    level, own = 1.0, jax.random.fold_in(key, 6)
    for axis_at, blocks in shards:
        steps = jnp.exp(jax.random.uniform(jax.random.fold_in(own, axis_at), (blocks,), jnp.float32, smallest / len(shards), largest / len(shards)))
        level = level * jnp.repeat(steps, shape[axis_at] // blocks).reshape([-1 if axis == axis_at else 1 for axis in range(len(shape))])
    return level


def centred(stream_key, dims, deviation, limit, pieces=(), kind=jnp.bfloat16):
    drawn = deviation * jax.random.normal(stream_key, dims, jnp.float32)
    if pieces:
        drawn = drawn * steps_of(stream_key, dims, pieces, -0.22, 0.18)
    return jnp.clip(drawn, -limit, limit).astype(kind)


def setup_inputs(seed: int = 0) -> dict:
    splits = jax.random.split(jax.random.key(seed), 12)
    return {
        "tokens": centred(splits[0], (SEQS, LEN, D), 1.0, 6.0, ((0, 4), (1, 8))),
        "mask": with_ends((jax.random.randint(splits[1], (SEQS, LEN), 0, 10) < 3).astype(jnp.int32), jax.random.fold_in(splits[1], 1), 0, 1),
        "segments": draw_segments(jax.random.fold_in(splits[11], 71), 0),
        "replacement": centred(splits[3], (D,), 1.0, 6.0, (), jnp.float32),
        "w_qkv": centred(splits[4], (D, LAYERS, 3 * D), D ** -0.5, 0.21875),
        "w_out": centred(splits[5], (D, LAYERS, D), (D // 16) ** -0.5, 0.875),
        "w_in": centred(splits[6], (D, LAYERS, 2 * FF), D ** -0.5, 0.21875),
        "w_down": centred(splits[7], (FF, LAYERS, D), FF ** -0.5, 0.109375),
        "ln_gain": jnp.clip(1.0 + 0.1 * jax.random.normal(splits[8], (LAYERS, 2, D), jnp.float32), 0.5, 1.5),
        "ln_bias": centred(splits[9], (LAYERS, 2, D), 0.2, 1.0, (), jnp.float32),
        "cotangent": centred(splits[10], (SEQS, LEN, D), 1.0, 6.0, ((0, 4), (1, 8))),
    }


@jax.custom_vjp
def low(v):
    return lax.optimization_barrier(v.astype(jnp.bfloat16)).astype(jnp.float32)

@jax.custom_vjp
def low_back(v):
    return v

def low_keep(v):
    return (low(v), None)

def low_pass(kept, grad):
    return (grad,)

def back_keep(v):
    return (v, None)

def back_low(kept, grad):
    return (low(grad),)
low.defvjp(low_keep, low_pass)
low_back.defvjp(back_keep, back_low)

def hdot(left, right):
    return jnp.dot(left, right, precision=lax.Precision.HIGHEST, preferred_element_type=jnp.float32)

def alibi_slopes(head_count):
    head_index = jnp.arange(head_count, dtype=jnp.float32)
    return jnp.exp2(jnp.where(head_index < 8.0, -(head_index + 1.0), 7.5 - head_index))

def layer_norm(value, gain, bias):
    center = lax.optimization_barrier(jnp.mean(value, axis=-1, keepdims=True))
    shifted = value - center
    spread = lax.optimization_barrier(jnp.mean(shifted * shifted, axis=-1, keepdims=True))
    return shifted * lax.rsqrt(spread + 1e-12) * gain + bias

def gated_gelu(gate_up):
    half_cols = gate_up.shape[-1] // 2
    return jax.nn.gelu(gate_up[..., :half_cols], approximate=False) * gate_up[..., half_cols:]

def encode_sequence(params, seq_tokens, seq_mask, seq_labels):
    replace_vals, qkv_vals, out_vals, in_vals, down_vals, gain_vals, bias_vals = params
    current = jnp.where(seq_mask[:, None] == 1, replace_vals[None, :], seq_tokens)
    position = jnp.arange(LEN, dtype=jnp.float32)
    distance = jnp.abs(position[:, None] - position[None, :])
    same_doc = seq_labels[:, None] == seq_labels[None, :]
    slopes = alibi_slopes(HEADS)
    score_scale = 1.0 / math.sqrt(HEAD_DIM)
    for layer_index in range(LAYERS):
        flat_in = low(current)
        projected = low_back(low(hdot(flat_in, qkv_vals[:, layer_index])))
        queries = projected[:, :D].reshape(LEN, HEADS, HEAD_DIM)
        key_rows = projected[:, D:2 * D].reshape(LEN, HEADS, HEAD_DIM)
        value_rows = projected[:, 2 * D:].reshape(LEN, HEADS, HEAD_DIM)
        raw_scores = jnp.einsum('qhc,khc->hqk', queries, key_rows, precision=lax.Precision.HIGHEST)
        scores = low_back(raw_scores * score_scale) - slopes[:, None, None] * distance[None]
        scores = jnp.where(same_doc[None], scores, -jnp.inf)
        row_max = lax.optimization_barrier(jnp.max(scores, axis=-1, keepdims=True))
        weights_exp = jnp.exp(scores - row_max)
        probs_all = weights_exp / lax.optimization_barrier(jnp.sum(weights_exp, axis=-1, keepdims=True))
        context = jnp.einsum('hqk,khc->qhc', low(probs_all), value_rows, precision=lax.Precision.HIGHEST)
        context = low_back(low(context.reshape(LEN, D)))
        branch = low_back(hdot(context, out_vals[:, layer_index]))
        normed_one = layer_norm(current + branch, gain_vals[layer_index, 0], bias_vals[layer_index, 0])
        gate_up = low_back(hdot(low(normed_one), in_vals[:, layer_index]))
        feed_out = low_back(hdot(low(gated_gelu(gate_up)), down_vals[:, layer_index]))
        current = layer_norm(normed_one + feed_out, gain_vals[layer_index, 1], bias_vals[layer_index, 1])
    return current

def reference(tokens, mask, segments, replacement, w_qkv, w_out, w_in, w_down, ln_gain, ln_bias, cotangent):

    def forward(token_vals, replace_vals, qkv_vals, out_vals, in_vals, down_vals, gain_vals, bias_vals):
        params = (replace_vals, qkv_vals, out_vals, in_vals, down_vals, gain_vals, bias_vals)

        def one_sequence(seq_items):
            return encode_sequence(params, seq_items[0], seq_items[1], seq_items[2])
        return lax.map(jax.checkpoint(one_sequence), (token_vals, mask, segments))
    outputs, backward = jax.vjp(forward, tokens.astype(jnp.float32), replacement, w_qkv.astype(jnp.float32), w_out.astype(jnp.float32), w_in.astype(jnp.float32), w_down.astype(jnp.float32), ln_gain, ln_bias)
    gradients = backward(cotangent.astype(jnp.float32))
    return (outputs.astype(jnp.bfloat16), gradients[0], gradients[1], gradients[2], gradients[3], gradients[4], gradients[5], gradients[6], gradients[7])
```

```python
import math

import jax
import jax.numpy as jnp
from jax import lax
from jax.experimental import pallas as pl
from jax.experimental.pallas import tpu as pltpu
from jax.sharding import PartitionSpec as P

HEADS = 12
HEAD_DIM = 64
LAYERS = 2
LANES = 128
SCALE = 1.0 / math.sqrt(HEAD_DIM)
FAR = 1e30
BF16 = jnp.bfloat16
F32 = jnp.float32
VMEM_LIMIT = 56 << 20


def alibi_slopes(head_count):
    head_index = jnp.arange(head_count, dtype=jnp.float32)
    return jnp.exp2(jnp.where(head_index < 8.0, -(head_index + 1.0), 7.5 - head_index))


def layer_norm(value, gain, bias):
    center = jnp.mean(value, axis=-1, keepdims=True)
    shifted = value - center
    spread = jnp.mean(shifted * shifted, axis=-1, keepdims=True)
    return shifted * lax.rsqrt(spread + 1e-12) * gain + bias


def gated_gelu(gate_up):
    half_cols = gate_up.shape[-1] // 2
    return jax.nn.gelu(gate_up[..., :half_cols], approximate=False) * gate_up[..., half_cols:]


def dot(a, b, dims):
    return lax.dot_general(a, b, (dims, ((), ())), preferred_element_type=F32)


NN = ((1,), (0,))
NT = ((1,), (1,))
TN = ((0,), (0,))


def split_layers(weight):
    rows, _, cols = weight.shape
    row_block = 256
    col_block = next(c for c in (3072, 2304, 1152, 768) if cols % c == 0)

    def body(in_ref, out_ref):
        to_row = lax.broadcasted_iota(jnp.int32, (256, 256), 0)
        from_row = lax.broadcasted_iota(jnp.int32, (256, 256), 1)
        wanted = jnp.where(to_row < 128, 2 * to_row, 2 * to_row - 255)
        pick = jnp.where(from_row == wanted, 1.0, 0.0).astype(BF16)
        for part in range(row_block // 128):
            at = slice(part * 128, part * 128 + 128)
            mixed = in_ref[at].reshape(256, col_block)
            picked = dot(pick, mixed, NN).astype(BF16)
            out_ref[0, at] = picked[:128]
            out_ref[1, at] = picked[128:]

    return pl.pallas_call(
        body,
        grid=(rows // row_block, cols // col_block),
        in_specs=[pl.BlockSpec((row_block, 2, col_block), lambda i, j: (i, 0, j))],
        out_specs=pl.BlockSpec((2, row_block, col_block), lambda i, j: (0, i, j)),
        out_shape=jax.ShapeDtypeStruct((2, rows, cols), BF16),
        compiler_params=pltpu.CompilerParams(vmem_limit_bytes=VMEM_LIMIT),
        cost_estimate=pl.CostEstimate(
            flops=2 * 512 * rows * cols, bytes_accessed=8 * rows * cols, transcendentals=0
        ),
        name="split_layers",
    )(weight)


def attend_forward(qkv, far_dist, slopes):
    length, width = qkv.shape
    cols = width // 3
    heads = cols // HEAD_DIM
    block = 256

    def body(slope_ref, qkv_ref, dist_ref, ctx_ref, lse_ref):
        at = pl.ds(pl.multiple_of(pl.program_id(0) * block, block), block)
        dist = dist_ref[...]
        for h in range(heads):
            q = qkv_ref[at, h * 64 : h * 64 + 64]
            k = qkv_ref[:, cols + h * 64 : cols + h * 64 + 64]
            v = qkv_ref[:, 2 * cols + h * 64 : 2 * cols + h * 64 + 64]
            s = dot(k, q, NT) * SCALE - dist * slope_ref[h]
            top = jnp.max(s, axis=0, keepdims=True)
            e = jnp.exp(s - top)
            total = jnp.sum(e, axis=0, keepdims=True)
            ctx = dot(v, e.astype(BF16), TN) / total
            ctx_ref[:, h * 64 : h * 64 + 64] = ctx.T.astype(BF16)
            lse_ref[h : h + 1, :] = top + jnp.log(total)

    return pl.pallas_call(
        body,
        grid=(length // block,),
        in_specs=[
            pl.BlockSpec(memory_space=pltpu.SMEM),
            pl.BlockSpec((length, width), lambda i: (0, 0)),
            pl.BlockSpec((length, block), lambda i: (0, i)),
        ],
        out_specs=[
            pl.BlockSpec((block, cols), lambda i: (i, 0)),
            pl.BlockSpec((heads, block), lambda i: (0, i)),
        ],
        out_shape=[
            jax.ShapeDtypeStruct((length, cols), BF16),
            jax.ShapeDtypeStruct((heads, length), F32),
        ],
        compiler_params=pltpu.CompilerParams(vmem_limit_bytes=VMEM_LIMIT),
        cost_estimate=pl.CostEstimate(
            flops=16 * heads * length * length * HEAD_DIM,
            bytes_accessed=4 * length * length,
            transcendentals=heads * length * length,
        ),
        name="attend_forward",
    )(slopes, qkv, far_dist)


def attend_backward(qkv, ctx, ctx_grad, lse, far_dist, slopes):
    length, width = qkv.shape
    cols = width // 3
    heads = cols // HEAD_DIM
    block = 256

    def body(slope_ref, qkv_ref, ctx_ref, g_ref, lse_ref, dist_ref, out_ref, dk_ref, dv_ref):
        step = pl.program_id(0)
        at = pl.ds(pl.multiple_of(step * block, block), block)

        @pl.when(step == 0)
        def _():
            dk_ref[...] = jnp.zeros_like(dk_ref)
            dv_ref[...] = jnp.zeros_like(dv_ref)

        dist = dist_ref[...]
        for h in range(heads):
            mine = slice(h * 64, h * 64 + 64)
            q = qkv_ref[at, mine]
            k = qkv_ref[:, cols + h * 64 : cols + h * 64 + 64]
            v = qkv_ref[:, 2 * cols + h * 64 : 2 * cols + h * 64 + 64]
            g = g_ref[:, mine]
            inner = (g.astype(F32) * ctx_ref[:, mine].astype(F32)).T
            inner = jnp.sum(inner, axis=0, keepdims=True)
            s = dot(k, q, NT) * SCALE - dist * slope_ref[h]
            p = jnp.exp(s - lse_ref[h : h + 1, :])
            gp = dot(v, g, NT)
            gs = (p * (gp - inner)).astype(BF16)
            dv_ref[:, mine] += dot(p.astype(BF16), g, NN)
            dk_ref[:, mine] += dot(gs, q, NN)
            dq = dot(k, gs, TN) * SCALE
            out_ref[at, mine] = dq.T.astype(BF16)

        @pl.when(step == pl.num_programs(0) - 1)
        def _():
            out_ref[:, cols : 2 * cols] = (dk_ref[...] * SCALE).astype(BF16)
            out_ref[:, 2 * cols :] = dv_ref[...].astype(BF16)

    return pl.pallas_call(
        body,
        grid=(length // block,),
        in_specs=[
            pl.BlockSpec(memory_space=pltpu.SMEM),
            pl.BlockSpec((length, width), lambda i: (0, 0)),
            pl.BlockSpec((block, cols), lambda i: (i, 0)),
            pl.BlockSpec((block, cols), lambda i: (i, 0)),
            pl.BlockSpec((heads, block), lambda i: (0, i)),
            pl.BlockSpec((length, block), lambda i: (0, i)),
        ],
        out_specs=pl.BlockSpec((length, width), lambda i: (0, 0)),
        out_shape=jax.ShapeDtypeStruct((length, width), BF16),
        scratch_shapes=[pltpu.VMEM((length, cols), F32), pltpu.VMEM((length, cols), F32)],
        compiler_params=pltpu.CompilerParams(vmem_limit_bytes=VMEM_LIMIT),
        cost_estimate=pl.CostEstimate(
            flops=40 * heads * length * length * HEAD_DIM,
            bytes_accessed=4 * length * length,
            transcendentals=heads * length * length,
        ),
        name="attend_backward",
    )(slopes, qkv, ctx, ctx_grad, lse, far_dist)


def swap(value, axis, bit):
    return lax.ppermute(value, axis, [(i, i ^ (1 << bit)) for i in range(lax.axis_size(axis))])


def reduce_half(value, axis, bit, dim):
    mine = (lax.axis_index(axis) >> bit) & 1
    kept = lax.dynamic_index_in_dim(value, mine, dim, False)
    sent = lax.dynamic_index_in_dim(value, 1 - mine, dim, False)
    return (kept.astype(F32) + swap(sent, axis, bit).astype(F32)).astype(BF16)


def gather_pair(value, axis, bit, dim):
    mine = (lax.axis_index(axis) >> bit) & 1
    other = swap(value, axis, bit)
    low = jnp.where(mine == 0, value, other)
    high = jnp.where(mine == 0, other, value)
    return jnp.stack((low, high), axis=dim)


def bits_of(axis):
    return lax.axis_size(axis).bit_length() - 1


def reduce_tok(value):
    for bit in range(bits_of("tok")):
        count = value.shape[0]
        value = value.reshape(count // 2, 2, *value.shape[1:])
        value = reduce_half(value, "tok", bit, 1)
    return value[0]


def gather_dp(value):
    value = value[None]
    for bit in reversed(range(bits_of("dp"))):
        value = gather_pair(value, "dp", bit, 1)
        value = value.reshape(-1, *value.shape[2:])
    return value


def per_device(
    tokens, mask, segments, replacement, w_qkv, w_out, w_in, w_down, ln_gain, ln_bias, cotangent
):
    tok_devices = lax.axis_size("tok")
    dp_devices = lax.axis_size("dp")
    seq_count, local_len, width = tokens.shape
    sub = tok_devices // seq_count
    per_group = HEADS // sub
    cols = per_group * HEAD_DIM
    tok_count = seq_count * local_len
    full_len = local_len * tok_devices
    tok_place = lax.axis_index("tok")
    group = tok_place % sub
    apart = [[j + sub * k for k in range(seq_count)] for j in range(sub)]
    near = [[j + sub * k for j in range(sub)] for k in range(seq_count)]

    def regroup(value):
        return lax.all_to_all(value, "tok", 0, 0, axis_index_groups=apart)

    def spread(value):
        return lax.all_to_all(value, "tok", 0, 0, axis_index_groups=near)

    extra = jnp.zeros((seq_count, local_len, LANES), BF16)
    extra = extra.at[:, :, 0].set((mask == 1).astype(BF16))
    extra = extra.at[:, :, 1].set(segments.astype(BF16))
    mixed = regroup(jnp.concatenate((tokens, extra), axis=-1)).reshape(tok_count, -1)
    flags = mixed[:, width:]
    masked = flags[:, :1] == 1.0
    current = jnp.where(masked, replacement[None, :], mixed[:, :width].astype(F32))
    cot = regroup(cotangent).reshape(tok_count, width)

    wq = split_layers(w_qkv)
    wo = split_layers(w_out)
    wi = split_layers(w_in)
    wd = split_layers(w_down)
    wq_mine = lax.dynamic_index_in_dim(
        wq.reshape(LAYERS, width, 3, sub, cols), group, 3, False
    ).reshape(LAYERS, width, 3 * cols)
    slopes = lax.dynamic_slice_in_dim(alibi_slopes(HEADS), group * per_group, per_group, 0)
    place = jnp.arange(full_len, dtype=jnp.int32)
    place = place.reshape(seq_count, sub, local_len).transpose(1, 0, 2).reshape(full_len)
    far_dist = None
    stored = []
    for layer in range(LAYERS):
        flat_in = current.astype(BF16)
        sent = jnp.concatenate((flat_in, flags), axis=-1) if layer == 0 else flat_in
        flat_all = spread(jnp.broadcast_to(sent[None], (sub, *sent.shape)))
        flat_all = flat_all.reshape(full_len, -1)
        if layer == 0:
            labels = flat_all[:, width + 1].astype(F32)
            flat_all = flat_all[:, :width]
            far_dist = jnp.where(
                labels[:, None] == labels[None, :],
                jnp.abs(place[:, None] - place[None, :]).astype(F32),
                FAR,
            )
        qkv = dot(flat_all, wq_mine[layer], NN).astype(BF16)
        ctx_here, lse = attend_forward(qkv, far_dist, slopes)
        ctx = spread(ctx_here.reshape(sub, tok_count, cols))
        ctx = ctx.transpose(1, 0, 2).reshape(tok_count, width)
        summed = current + dot(ctx, wo[layer], NN)
        y1 = layer_norm(summed, ln_gain[layer, 0], ln_bias[layer, 0])
        y1l = y1.astype(BF16)
        gate_up = dot(y1l, wi[layer], NN)
        hidden = gated_gelu(gate_up).astype(BF16)
        z = y1 + dot(hidden, wd[layer], NN)
        lhs_all = lax.all_gather(jnp.concatenate((y1l, hidden), axis=-1), "dp", tiled=True)
        stored.append((flat_all, qkv, ctx_here, lse, ctx, summed, gate_up, z, lhs_all))
        current = layer_norm(z, ln_gain[layer, 1], ln_bias[layer, 1])
    layer_out = regroup(current.astype(BF16).reshape(seq_count, local_len, width))
    gradient = cot.astype(F32)
    outs = [None] * LAYERS
    small = []
    in_cols = wi.shape[2] // dp_devices
    down_cols = width // dp_devices
    ff = wd.shape[1]
    row_out = width // tok_devices
    row_down = ff // tok_devices
    for layer in reversed(range(LAYERS)):
        flat_all, qkv, ctx_here, lse, ctx, summed, gate_up, z, lhs_all = stored[layer]
        z_grad, gain_two, bias_two = jax.vjp(
            layer_norm, z, ln_gain[layer, 1], ln_bias[layer, 1]
        )[1](gradient)
        z_low = z_grad.astype(BF16)
        hidden_grad = dot(z_low, wd[layer], NT)
        gate_grad = jax.vjp(gated_gelu, gate_up)[1](hidden_grad)[0].astype(BF16)
        rhs = jnp.concatenate(
            (
                gate_grad.reshape(tok_count, dp_devices, in_cols),
                z_low.reshape(tok_count, dp_devices, down_cols),
            ),
            axis=-1,
        ).transpose(1, 0, 2)
        rhs_all = lax.all_to_all(rhs, "dp", 0, 0).reshape(dp_devices * tok_count, -1)
        y1_grad = z_grad + dot(gate_grad, wi[layer], NT)
        s_grad, gain_one, bias_one = jax.vjp(
            layer_norm, summed, ln_gain[layer, 0], ln_bias[layer, 0]
        )[1](y1_grad)
        small += [gain_one, gain_two, bias_one, bias_two]
        s_low = s_grad.astype(BF16)
        ctx_grad = dot(s_low, wo[layer], NT).astype(BF16)
        ctx_grad = spread(ctx_grad.reshape(tok_count, sub, cols).transpose(1, 0, 2))
        ctx_grad = ctx_grad.reshape(full_len, cols)
        head_grad = attend_backward(qkv, ctx_here, ctx_grad, lse, far_dist, slopes)
        g_in = dot(lhs_all[:, :width], rhs_all[:, :in_cols], TN).astype(BF16)
        g_down = dot(lhs_all[:, width:], rhs_all[:, in_cols:], TN).astype(BF16)
        g_in = reduce_tok(g_in.reshape(tok_devices, row_out, in_cols))
        g_down = reduce_tok(g_down.reshape(tok_devices, row_down, down_cols))
        g_in = gather_dp(g_in).transpose(1, 0, 2).reshape(row_out, -1)
        g_down = gather_dp(g_down).transpose(1, 0, 2).reshape(row_down, -1)
        g_qkv = dot(flat_all, head_grad, TN).astype(BF16)
        back = spread(head_grad.reshape(sub, tok_count, 3 * cols))
        back = back.reshape(sub, tok_count, 3, cols).transpose(1, 2, 0, 3).reshape(tok_count, -1)
        gradient = s_grad + dot(back, wq[layer], NT)
        g_qkv = g_qkv.reshape(seq_count, sub, row_out, 3 * cols)
        for bit in range(bits_of("dp")):
            g_qkv = g_qkv.reshape(seq_count, sub, -1, 2, g_qkv.shape[2] // 2, 3 * cols)
            g_qkv = reduce_half(g_qkv, "dp", bit, 3)
            g_qkv = g_qkv.reshape(seq_count, sub, -1, 3 * cols)
        for bit in range(bits_of("tok")):
            if (1 << bit) >= sub:
                g_qkv = g_qkv.reshape(-1, 2, *g_qkv.shape[1:])
                g_qkv = reduce_half(g_qkv, "tok", bit, 1)
        g_qkv = g_qkv[0]
        for bit in reversed(range(bits_of("dp"))):
            g_qkv = gather_pair(g_qkv, "dp", bit, 1).reshape(sub, -1, 3 * cols)
        g_qkv = spread(g_qkv).reshape(sub, row_out, 3, cols)
        g_qkv = g_qkv.transpose(1, 2, 0, 3).reshape(row_out, -1)
        g_out = dot(ctx, s_low, TN).astype(BF16).reshape(tok_devices, row_out, width)
        g_out = reduce_tok(g_out)
        for bit in range(bits_of("dp")):
            g_out = (g_out.astype(F32) + swap(g_out, "dp", bit).astype(F32)).astype(BF16)
        outs[layer] = tuple(v.astype(F32) for v in (g_qkv, g_out, g_in, g_down))
    grad_tokens = jnp.where(masked, 0.0, gradient).astype(BF16)
    grad_tokens = regroup(grad_tokens.reshape(seq_count, local_len, width)).astype(F32)
    small.append(jnp.sum(jnp.where(masked, gradient, 0.0), axis=0))
    small = lax.all_gather(jnp.stack(small, axis=0), ("dp", "tok"))
    small = jnp.sum(small, axis=0)
    small = lax.dynamic_slice_in_dim(small, tok_place * row_out, row_out, 1)
    by_layer = jnp.flip(small[: 4 * LAYERS].reshape(LAYERS, 2, 2, row_out), axis=0)
    return (
        layer_out,
        grad_tokens,
        small[-1],
        *(jnp.stack([outs[i][n] for i in range(LAYERS)], axis=1) for n in range(4)),
        by_layer[:, 0],
        by_layer[:, 1],
    )


def solution(mesh):
    in_specs = (
        P("dp", "tok", None),
        P("dp", "tok"),
        P("dp", "tok"),
        P(),
        P(),
        P(),
        P(),
        P(),
        P(),
        P(),
        P("dp", "tok", None),
    )
    out_specs = (
        P("dp", "tok", None),
        P("dp", "tok", None),
        P("tok"),
        P("tok", None, None),
        P("tok", None, None),
        P("tok", None, None),
        P("tok", None, None),
        P(None, None, "tok"),
        P(None, None, "tok"),
    )
    return jax.shard_map(
        per_device, mesh=mesh, in_specs=in_specs, out_specs=out_specs, check_vma=False
    )
```

```python
import math

import jax
import jax.numpy as jnp
from jax import lax
from jax.experimental import pallas as pl
from jax.experimental.pallas import tpu as pltpu
from jax.sharding import PartitionSpec as P

HEADS = 12
HEAD_DIM = 64
LAYERS = 2
LANES = 128
PACK = 384
SCALE = 1.0 / math.sqrt(HEAD_DIM)
FAR = 1e30
BF16 = jnp.bfloat16
F32 = jnp.float32
VMEM_LIMIT = 56 << 20
COST_TIMES = 4


def alibi_slopes(head_count):
    head_index = jnp.arange(head_count, dtype=jnp.float32)
    return jnp.exp2(jnp.where(head_index < 8.0, -(head_index + 1.0), 7.5 - head_index))


def dot(a, b, dims):
    return lax.dot_general(a, b, (dims, ((), ())), preferred_element_type=F32)


def cost(flops, bytes_accessed, transcendentals):
    return pl.CostEstimate(
        flops=COST_TIMES * flops,
        bytes_accessed=bytes_accessed,
        transcendentals=transcendentals,
    )


NN = ((1,), (0,))
NT = ((1,), (1,))
TN = ((0,), (0,))


def split_layers(weight):
    rows, _, cols = weight.shape
    row_block = 256
    col_block = next(c for c in (3072, 2304, 1152, 768) if cols % c == 0)

    def body(in_ref, out_ref):
        to_row = lax.broadcasted_iota(jnp.int32, (256, 256), 0)
        from_row = lax.broadcasted_iota(jnp.int32, (256, 256), 1)
        wanted = jnp.where(to_row < 128, 2 * to_row, 2 * to_row - 255)
        pick = jnp.where(from_row == wanted, 1.0, 0.0).astype(BF16)
        for part in range(row_block // 128):
            at = slice(part * 128, part * 128 + 128)
            mixed = in_ref[at].reshape(256, col_block)
            picked = dot(pick, mixed, NN).astype(BF16)
            out_ref[0, at] = picked[:128]
            out_ref[1, at] = picked[128:]

    return pl.pallas_call(
        body,
        grid=(rows // row_block, cols // col_block),
        in_specs=[pl.BlockSpec((row_block, 2, col_block), lambda i, j: (i, 0, j))],
        out_specs=pl.BlockSpec((2, row_block, col_block), lambda i, j: (0, i, j)),
        out_shape=jax.ShapeDtypeStruct((2, rows, cols), BF16),
        compiler_params=pltpu.CompilerParams(vmem_limit_bytes=VMEM_LIMIT),
        cost_estimate=cost(
            flops=2 * 512 * rows * cols, bytes_accessed=8 * rows * cols, transcendentals=0
        ),
        name="split_layers",
    )(weight)


def split_layers_by_group(weight, sub):
    rows, _, cols = weight.shape
    row_block = 256
    group_cols = cols // sub // 3

    def body(in_ref, out_ref):
        to_row = lax.broadcasted_iota(jnp.int32, (256, 256), 0)
        from_row = lax.broadcasted_iota(jnp.int32, (256, 256), 1)
        wanted = jnp.where(to_row < 128, 2 * to_row, 2 * to_row - 255)
        pick = jnp.where(from_row == wanted, 1.0, 0.0).astype(BF16)
        for part in range(row_block // 128):
            at = slice(part * 128, part * 128 + 128)
            picked = dot(pick, in_ref[at].reshape(256, cols), NN).astype(BF16)
            for j in range(sub):
                for n in range(3):
                    first = (n * sub + j) * group_cols
                    block = picked[:, first : first + group_cols]
                    to = slice(n * group_cols, n * group_cols + group_cols)
                    out_ref[0, j, at, to] = block[:128]
                    out_ref[1, j, at, to] = block[128:]

    return pl.pallas_call(
        body,
        grid=(rows // row_block,),
        in_specs=[pl.BlockSpec((row_block, 2, cols), lambda i: (i, 0, 0))],
        out_specs=pl.BlockSpec((2, sub, row_block, 3 * group_cols), lambda i: (0, 0, i, 0)),
        out_shape=jax.ShapeDtypeStruct((2, sub, rows, 3 * group_cols), BF16),
        compiler_params=pltpu.CompilerParams(vmem_limit_bytes=VMEM_LIMIT),
        cost_estimate=cost(
            flops=2 * 512 * rows * cols, bytes_accessed=8 * rows * cols, transcendentals=0
        ),
        name="split_qkv",
    )(weight)


def norm_parts(value):
    center = jnp.mean(value, axis=-1, keepdims=True)
    shifted = value - center
    inverse = lax.rsqrt(jnp.mean(shifted * shifted, axis=-1, keepdims=True) + 1e-12)
    return shifted * inverse, inverse


def norm_grad(grad, value, gain):
    normed, inverse = norm_parts(value)
    scaled = grad * gain
    one = jnp.mean(scaled, axis=-1, keepdims=True)
    two = jnp.mean(scaled * normed, axis=-1, keepdims=True)
    in_grad = inverse * (scaled - one - normed * two)
    gain_grad = jnp.sum(grad * normed, axis=0, keepdims=True)
    bias_grad = jnp.sum(grad, axis=0, keepdims=True)
    return in_grad, gain_grad, bias_grad


def feed_forward(layer, group, current, ctx, w_out, w_in, w_down, gain, bias):
    count, width = current.shape
    sub, cols = len(ctx), ctx[0].shape[0]
    ff = w_down.shape[1]
    chunk = 768
    steps = ff // chunk

    def body(group_ref, *refs):
        ctx_refs = refs[:sub]
        cur_ref, wo_ref, wg_ref, wu_ref, wd_ref, gain_ref, bias_ref = refs[sub : sub + 7]
        lhs_ref, a_ref, b_ref, sum_ref, z_ref, next_ref, low_ref = refs[sub + 7 : sub + 14]
        y1l_ref, acc_ref, held_ref = refs[sub + 14 :]
        step = pl.program_id(0)

        @pl.when(step == 0)
        def _():
            branch = jnp.zeros((count, width), F32)
            for r in range(sub):
                held_ref[jnp.bitwise_xor(group_ref[0], r)] = ctx_refs[r][...]
            for j in range(sub):
                part = held_ref[j]
                to = slice(j * cols, j * cols + cols)
                lhs_ref[:, width + ff + j * cols : width + ff + j * cols + cols] = (
                    part.astype(F32).T.astype(BF16)
                )
                branch += dot(part, wo_ref[0, to, :], TN)
            summed = cur_ref[...] + branch
            sum_ref[...] = summed
            normed, _ = norm_parts(summed)
            y1 = normed * gain_ref[layer, 0:1, :] + bias_ref[layer, 0:1, :]
            acc_ref[...] = y1
            y1l_ref[...] = y1.astype(BF16)
            lhs_ref[:, :width] = y1.astype(BF16)

        y1l = y1l_ref[...]
        gate = dot(y1l, wg_ref[0], NN)
        up = dot(y1l, wu_ref[0], NN)
        cdf = 0.5 * (1.0 + lax.erf(gate * (0.5**0.5)))
        density = jnp.exp(-0.5 * gate * gate) * (1.0 / math.sqrt(2.0 * math.pi))
        gelu = gate * cdf
        hidden = (gelu * up).astype(BF16)
        a_ref[...] = gelu.astype(BF16)
        b_ref[...] = (up * (cdf + gate * density)).astype(BF16)
        lhs_ref[:, pl.ds(pl.multiple_of(width + step * chunk, 128), chunk)] = hidden
        acc_ref[...] += dot(hidden, wd_ref[0], NN)

        @pl.when(step == steps - 1)
        def _():
            z = acc_ref[...]
            z_ref[...] = z
            normed, _ = norm_parts(z)
            out = normed * gain_ref[layer, 1:2, :] + bias_ref[layer, 1:2, :]
            next_ref[...] = out
            low_ref[...] = out.astype(BF16)

    whole = lambda *shape: pl.BlockSpec(shape, lambda i: (0,) * len(shape))
    return pl.pallas_call(
        body,
        grid=(steps,),
        in_specs=[
            pl.BlockSpec(memory_space=pltpu.SMEM),
            *[whole(cols, count)] * sub,
            whole(count, width),
            pl.BlockSpec((1, width, width), lambda i: (layer, 0, 0)),
            pl.BlockSpec((1, width, chunk), lambda i: (layer, 0, i)),
            pl.BlockSpec((1, width, chunk), lambda i: (layer, 0, steps + i)),
            pl.BlockSpec((1, chunk, width), lambda i: (layer, i, 0)),
            whole(*gain.shape),
            whole(*bias.shape),
        ],
        out_specs=[
            whole(count, ff + 2 * width),
            pl.BlockSpec((count, chunk), lambda i: (0, i)),
            pl.BlockSpec((count, chunk), lambda i: (0, i)),
            whole(count, width),
            whole(count, width),
            whole(count, width),
            whole(count, width),
        ],
        out_shape=[
            jax.ShapeDtypeStruct((count, ff + 2 * width), BF16),
            jax.ShapeDtypeStruct((count, ff), BF16),
            jax.ShapeDtypeStruct((count, ff), BF16),
            jax.ShapeDtypeStruct((count, width), F32),
            jax.ShapeDtypeStruct((count, width), F32),
            jax.ShapeDtypeStruct((count, width), F32),
            jax.ShapeDtypeStruct((count, width), BF16),
        ],
        scratch_shapes=[
            pltpu.VMEM((count, width), BF16),
            pltpu.VMEM((count, width), F32),
            pltpu.VMEM((sub, cols, count), BF16),
        ],
        compiler_params=pltpu.CompilerParams(vmem_limit_bytes=VMEM_LIMIT),
        cost_estimate=cost(
            flops=2 * count * width * (width + 3 * ff),
            bytes_accessed=6 * width * ff + 2 * width * width + count * (20 * width + 6 * ff),
            transcendentals=2 * count * ff,
        ),
        name="feed_forward",
    )(group, *ctx, current, w_out, w_in, w_in, w_down, gain, bias)


def feed_backward(layer, core, group, grad, z, summed, a, b, w_out, w_in, w_down, gain, sub):
    count, width = grad.shape
    ff = w_down.shape[1]
    cols = width // sub
    half = width // 2
    chunk = 768
    steps = ff // chunk

    def body(
        core_ref, group_ref, grad_ref, z_ref, sum_ref, a_ref, b_ref,
        wo_ref, wg_ref, wu_ref, wd_ref, gain_ref, mine_ref, send_ref, ga_ref, small_ref, *refs,
    ):
        gctx_refs = refs[:sub]
        gzl_ref, acc_ref, held_ref = refs[sub:]
        step = pl.program_id(0)
        first = core_ref[0] == 0

        def store(to, low, high):
            mine_ref[:, to] = jnp.where(first, low, high)
            send_ref[:, to] = jnp.where(first, high, low)

        @pl.when(step == 0)
        def _():
            gz, gain_grad, bias_grad = norm_grad(grad_ref[...], z_ref[...], gain_ref[layer, 1:2, :])
            small_ref[1:2, :] = gain_grad
            small_ref[3:4, :] = bias_grad
            acc_ref[...] = gz
            gzl = gz.astype(BF16)
            gzl_ref[...] = gzl
            store(slice(ff, ff + half), gz[:, :half].astype(BF16), gz[:, half:].astype(BF16))

        gzl = gzl_ref[...]
        ghid = dot(gzl, wd_ref[0], NT)
        ggate = (ghid * b_ref[...].astype(F32)).astype(BF16)
        gup = (ghid * a_ref[...].astype(F32)).astype(BF16)
        store(pl.ds(pl.multiple_of(step * chunk, 128), chunk), ggate, gup)
        acc_ref[...] += dot(ggate, wg_ref[0], NT) + dot(gup, wu_ref[0], NT)

        @pl.when(step == steps - 1)
        def _():
            ga, gain_grad, bias_grad = norm_grad(
                acc_ref[...], sum_ref[...], gain_ref[layer, 0:1, :]
            )
            small_ref[0:1, :] = gain_grad
            small_ref[2:3, :] = bias_grad
            ga_ref[...] = ga
            gal = ga.astype(BF16)
            store(slice(ff + half, ff + width), gal[:, :half], gal[:, half:])
            for j in range(sub):
                to = slice(j * cols, j * cols + cols)
                held_ref[j] = dot(wo_ref[0, to, :], gal, NT).astype(BF16)
            for r in range(sub):
                gctx_refs[r][...] = held_ref[jnp.bitwise_xor(group_ref[0], r)]

    whole = lambda *shape: pl.BlockSpec(shape, lambda i: (0,) * len(shape))
    return pl.pallas_call(
        body,
        grid=(steps,),
        in_specs=[
            pl.BlockSpec(memory_space=pltpu.SMEM),
            pl.BlockSpec(memory_space=pltpu.SMEM),
            whole(count, width),
            whole(count, width),
            whole(count, width),
            pl.BlockSpec((count, chunk), lambda i: (0, i)),
            pl.BlockSpec((count, chunk), lambda i: (0, i)),
            pl.BlockSpec((1, width, width), lambda i: (layer, 0, 0)),
            pl.BlockSpec((1, width, chunk), lambda i: (layer, 0, i)),
            pl.BlockSpec((1, width, chunk), lambda i: (layer, 0, steps + i)),
            pl.BlockSpec((1, chunk, width), lambda i: (layer, i, 0)),
            whole(*gain.shape),
        ],
        out_specs=[
            whole(count, ff + width),
            whole(count, ff + width),
            whole(count, width),
            whole(4, width),
            *[whole(cols, count)] * sub,
        ],
        out_shape=[
            jax.ShapeDtypeStruct((count, ff + width), BF16),
            jax.ShapeDtypeStruct((count, ff + width), BF16),
            jax.ShapeDtypeStruct((count, width), F32),
            jax.ShapeDtypeStruct((4, width), F32),
            *[jax.ShapeDtypeStruct((cols, count), BF16)] * sub,
        ],
        scratch_shapes=[
            pltpu.VMEM((count, width), BF16),
            pltpu.VMEM((count, width), F32),
            pltpu.VMEM((sub, cols, count), BF16),
        ],
        compiler_params=pltpu.CompilerParams(vmem_limit_bytes=VMEM_LIMIT),
        cost_estimate=cost(
            flops=2 * count * width * (width + 3 * ff),
            bytes_accessed=6 * width * ff + 2 * width * width + count * (24 * width + 8 * ff),
            transcendentals=0,
        ),
        name="feed_backward",
    )(core, group, grad, z, summed, a, b, w_out, w_in, w_in, w_down, gain)


def pair_grad_in(group, lhs, lhs_other, rhs, rhs_other, ff, tok_devices, sub, far):
    count = lhs.shape[0]
    width = rhs.shape[1] - ff
    rows = width // tok_devices
    seqs = tok_devices // sub
    chunk = 2 * PACK
    steps = ff // chunk
    first_steps = steps - far * PACK // chunk

    def body(group_ref, l1_ref, l2_ref, r1_ref, r2_ref, *refs):
        out_refs, last_ref, held_ref = refs[:sub], refs[sub], refs[sub + 1]
        step = pl.program_id(0)
        out = dot(l1_ref[...], r1_ref[...], TN) + dot(l2_ref[...], r2_ref[...], TN)

        @pl.when(step < first_steps)
        def _():
            for t in range(tok_devices):
                held_ref[t % sub, t // sub] = out[t * rows : t * rows + rows].astype(BF16)
            for r in range(sub):
                out_refs[r][...] = held_ref[jnp.bitwise_xor(group_ref[0], r)]

        @pl.when(step >= first_steps)
        def _():
            for t in range(tok_devices):
                part = out[t * rows : t * rows + rows].astype(BF16)
                for f in range(2):
                    last_ref[t, f] = part[:, f * PACK : f * PACK + PACK]

    return pl.pallas_call(
        body,
        grid=(steps,),
        in_specs=[
            pl.BlockSpec(memory_space=pltpu.SMEM),
            pl.BlockSpec((count, width), lambda i: (0, 0)),
            pl.BlockSpec((count, width), lambda i: (0, 0)),
            pl.BlockSpec((count, chunk), lambda i: (0, i)),
            pl.BlockSpec((count, chunk), lambda i: (0, i)),
        ],
        out_specs=[
            *[pl.BlockSpec((seqs, rows, chunk), lambda i: (0, 0, jnp.minimum(i, first_steps - 1)))]
            * sub,
            pl.BlockSpec(
                (tok_devices, 2, rows, PACK), lambda i: (0, jnp.maximum(i - first_steps, 0), 0, 0)
            ),
        ],
        out_shape=[
            *[jax.ShapeDtypeStruct((seqs, rows, ff - far * PACK), BF16)] * sub,
            jax.ShapeDtypeStruct((tok_devices, far, rows, PACK), BF16),
        ],
        scratch_shapes=[pltpu.VMEM((sub, seqs, rows, chunk), BF16)],
        compiler_params=pltpu.CompilerParams(vmem_limit_bytes=VMEM_LIMIT),
        cost_estimate=cost(
            flops=4 * count * width * ff,
            bytes_accessed=2 * width * ff + 4 * count * (width + ff),
            transcendentals=0,
        ),
        name="pair_grad_in",
    )(group, lhs, lhs_other, rhs, rhs_other)


def pair_grad_down(lhs, lhs_other, rhs, rhs_other, ff):
    count = lhs.shape[0]
    width = rhs.shape[1] - ff
    half = width // 2
    chunk = 768
    down = ff // chunk

    def body(l1_ref, l2_ref, r1_ref, r2_ref, out_ref):
        out = dot(l1_ref[...], r1_ref[...], TN) + dot(l2_ref[...], r2_ref[...], TN)
        out_ref[...] = out.astype(BF16)

    left = pl.BlockSpec((count, chunk), lambda i: (0, 1 + i))
    right = pl.BlockSpec((count, half), lambda i: (0, ff // half + jnp.where(i < down, 0, 1)))
    return pl.pallas_call(
        body,
        grid=(down + 1,),
        in_specs=[left, left, right, right],
        out_specs=pl.BlockSpec((chunk, half), lambda i: (i, 0)),
        out_shape=jax.ShapeDtypeStruct((ff + width, half), BF16),
        compiler_params=pltpu.CompilerParams(vmem_limit_bytes=VMEM_LIMIT),
        cost_estimate=cost(
            flops=4 * count * half * (ff + width),
            bytes_accessed=(ff + width) * (width + 4 * count) + 8 * count * width,
            transcendentals=0,
        ),
        name="pair_grad_down",
    )(lhs, lhs_other, rhs, rhs_other)


def input_grad(layer, group, ga, back, w_qkv):
    sub = len(back)
    cols, count = back[0].shape
    width = ga.shape[1]

    def body(group_ref, ga_ref, w_ref, *refs):
        back_refs, out_ref, acc_ref = refs[:sub], refs[sub], refs[sub + 1]
        step = pl.program_id(0)

        @pl.when(step == 0)
        def _():
            acc_ref[...] = jnp.zeros_like(acc_ref)

        for r in range(sub):

            @pl.when(step == r)
            def _():
                acc_ref[...] += dot(w_ref[0, 0], back_refs[r][...], NN)

        @pl.when(step == sub - 1)
        def _():
            out_ref[...] = ga_ref[...] + acc_ref[...].T

    return pl.pallas_call(
        body,
        grid_spec=pltpu.PrefetchScalarGridSpec(
            num_scalar_prefetch=1,
            grid=(sub,),
            in_specs=[
                pl.BlockSpec((count, width), lambda i, g: (0, 0)),
                pl.BlockSpec(
                    (1, 1, width, cols), lambda i, g: (layer, jnp.bitwise_xor(g[0], i), 0, 0)
                ),
                *[pl.BlockSpec((cols, count), lambda i, g: (0, 0))] * sub,
            ],
            out_specs=pl.BlockSpec((count, width), lambda i, g: (0, 0)),
            scratch_shapes=[pltpu.VMEM((width, count), F32)],
        ),
        out_shape=jax.ShapeDtypeStruct((count, width), F32),
        compiler_params=pltpu.CompilerParams(vmem_limit_bytes=VMEM_LIMIT),
        cost_estimate=cost(
            flops=2 * count * width * cols * sub,
            bytes_accessed=2 * sub * cols * (width + count) + 8 * count * width,
            transcendentals=0,
        ),
        name="input_grad",
    )(group, ga, w_qkv, *back)


def project(layer, group, parts, w_qkv):
    sub = len(parts)
    count = parts[0].shape[0]
    width, cols = w_qkv.shape[2:]

    def body(group_ref, w_ref, *refs):
        out_ref = refs[sub]
        for r in range(sub):
            out_ref[r * count : r * count + count, :] = dot(
                refs[r][...], w_ref[0, 0], NN
            ).astype(BF16)

    return pl.pallas_call(
        body,
        grid_spec=pltpu.PrefetchScalarGridSpec(
            num_scalar_prefetch=1,
            grid=(1,),
            in_specs=[
                pl.BlockSpec((1, 1, width, cols), lambda i, g: (layer, g[0], 0, 0)),
                *[pl.BlockSpec((count, width), lambda i, g: (0, 0))] * sub,
            ],
            out_specs=pl.BlockSpec((sub * count, cols), lambda i, g: (0, 0)),
        ),
        out_shape=jax.ShapeDtypeStruct((sub * count, cols), BF16),
        compiler_params=pltpu.CompilerParams(vmem_limit_bytes=VMEM_LIMIT),
        cost_estimate=cost(
            flops=2 * sub * count * width * cols,
            bytes_accessed=2 * (width * cols + sub * count * (width + cols)),
            transcendentals=0,
        ),
        name="project",
    )(group, w_qkv, *parts)


def qkv_grad(parts, grads, width, tok_devices, dp_devices):
    sub = len(parts)
    count = parts[0].shape[0]
    cols = grads[0].shape[0]
    rows = width // tok_devices
    few = rows // dp_devices

    def body(*refs):
        out_ref = refs[2 * sub]
        acc = jnp.zeros((cols, width), F32)
        for r in range(sub):
            acc += dot(refs[sub + r][...], refs[r][...], NN)
        acc = acc.T
        for t in range(tok_devices):
            for q in range(dp_devices):
                first = t * rows + q * few
                out_ref[q, t] = acc[first : first + few].astype(BF16)

    return pl.pallas_call(
        body,
        grid=(1,),
        in_specs=[
            *[pl.BlockSpec((count, width), lambda i: (0, 0))] * sub,
            *[pl.BlockSpec((cols, count), lambda i: (0, 0))] * sub,
        ],
        out_specs=pl.BlockSpec((dp_devices, tok_devices, few, cols), lambda i: (0, 0, 0, 0)),
        out_shape=jax.ShapeDtypeStruct((dp_devices, tok_devices, few, cols), BF16),
        compiler_params=pltpu.CompilerParams(vmem_limit_bytes=VMEM_LIMIT),
        cost_estimate=cost(
            flops=2 * sub * count * width * cols,
            bytes_accessed=2 * (width * cols + sub * count * (width + cols)),
            transcendentals=0,
        ),
        name="qkv_grad",
    )(*parts, *grads)


def attend_forward(qkv, far_dist, slopes, sub):
    length, width = qkv.shape
    cols = width // 3
    heads = cols // HEAD_DIM
    count = length // sub
    block = 256
    per = count // block

    def body(slope_ref, qkv_ref, dist_ref, *refs):
        ctx_refs, lse_ref, held_ref = refs[:sub], refs[sub], refs[sub + 1]
        step = pl.program_id(0)
        at = pl.ds(pl.multiple_of(step * block, block), block)
        dist = dist_ref[...]
        for h in range(heads):
            q = qkv_ref[at, h * 64 : h * 64 + 64]
            k = qkv_ref[:, cols + h * 64 : cols + h * 64 + 64]
            v = qkv_ref[:, 2 * cols + h * 64 : 2 * cols + h * 64 + 64]
            s = dot(k, q, NT) * SCALE - dist * slope_ref[h]
            top = jnp.max(s, axis=0, keepdims=True)
            e = jnp.exp(s - top)
            total = jnp.sum(e, axis=0, keepdims=True)
            ctx = dot(v, e.astype(BF16), TN) / total
            held_ref[h * 64 : h * 64 + 64, :] = ctx.astype(BF16)
            lse_ref[h : h + 1, :] = top + jnp.log(total)
        for i in range(length // block):

            @pl.when(step == i)
            def _():
                first = i % per * block
                ctx_refs[i // per][:, first : first + block] = held_ref[...]

    return pl.pallas_call(
        body,
        grid=(length // block,),
        in_specs=[
            pl.BlockSpec(memory_space=pltpu.SMEM),
            pl.BlockSpec((length, width), lambda i: (0, 0)),
            pl.BlockSpec((length, block), lambda i: (0, i)),
        ],
        out_specs=[
            *[pl.BlockSpec((cols, count), lambda i: (0, 0))] * sub,
            pl.BlockSpec((heads, block), lambda i: (0, i)),
        ],
        out_shape=[
            *[jax.ShapeDtypeStruct((cols, count), BF16)] * sub,
            jax.ShapeDtypeStruct((heads, length), F32),
        ],
        scratch_shapes=[pltpu.VMEM((cols, block), BF16)],
        compiler_params=pltpu.CompilerParams(vmem_limit_bytes=VMEM_LIMIT),
        cost_estimate=cost(
            flops=16 * heads * length * length * HEAD_DIM,
            bytes_accessed=4 * length * length,
            transcendentals=heads * length * length,
        ),
        name="attend_forward",
    )(slopes, qkv, far_dist)


def attend_backward(qkv, ctx, ctx_grad, lse, far_dist, slopes):
    length, width = qkv.shape
    sub = len(ctx)
    cols = width // 3
    heads = cols // HEAD_DIM
    count = length // sub
    block = 256
    per = count // block

    def body(slope_ref, qkv_ref, lse_ref, dist_ref, *refs):
        ctx_refs, g_refs, out_refs = refs[:sub], refs[sub : 2 * sub], refs[2 * sub : 3 * sub]
        dk_ref, dv_ref, dq_ref, held_ref, inner_ref = refs[3 * sub :]
        step = pl.program_id(0)
        at = pl.ds(pl.multiple_of(step * block, block), block)

        @pl.when(step == 0)
        def _():
            dk_ref[...] = jnp.zeros_like(dk_ref)
            dv_ref[...] = jnp.zeros_like(dv_ref)
            for r in range(sub):
                g = g_refs[r][...]
                both = g.astype(F32) * ctx_refs[r][...].astype(F32)
                for p in range(per):
                    of = slice(p * block, p * block + block)
                    held_ref[r * per + p] = g[:, of]
                    for h in range(heads):
                        inner_ref[r * per + p, h : h + 1, :] = jnp.sum(
                            both[h * 64 : h * 64 + 64, of], axis=0, keepdims=True
                        )

        dist = dist_ref[...]
        for h in range(heads):
            mine = slice(h * 64, h * 64 + 64)
            q = qkv_ref[at, mine]
            k = qkv_ref[:, cols + h * 64 : cols + h * 64 + 64]
            v = qkv_ref[:, 2 * cols + h * 64 : 2 * cols + h * 64 + 64]
            g = held_ref[step, mine, :]
            s = dot(k, q, NT) * SCALE - dist * slope_ref[h]
            p = jnp.exp(s - lse_ref[h : h + 1, :])
            gp = dot(v, g, NN)
            gs = (p * (gp - inner_ref[step, h : h + 1, :])).astype(BF16)
            dv_ref[:, mine] += dot(p.astype(BF16), g, NT)
            dk_ref[:, mine] += dot(gs, q, NN)
            dq_ref[step, mine, :] = (dot(k, gs, TN) * SCALE).astype(BF16)

        @pl.when(step == pl.num_programs(0) - 1)
        def _():
            for r in range(sub):
                of = slice(r * count, r * count + count)
                for p in range(per):
                    out_refs[r][:cols, p * block : p * block + block] = dq_ref[r * per + p]
                out_refs[r][cols : 2 * cols, :] = (dk_ref[of, :] * SCALE).T.astype(BF16)
                out_refs[r][2 * cols :, :] = dv_ref[of, :].T.astype(BF16)

    return pl.pallas_call(
        body,
        grid=(length // block,),
        in_specs=[
            pl.BlockSpec(memory_space=pltpu.SMEM),
            pl.BlockSpec((length, width), lambda i: (0, 0)),
            pl.BlockSpec((heads, block), lambda i: (0, i)),
            pl.BlockSpec((length, block), lambda i: (0, i)),
            *[pl.BlockSpec((cols, count), lambda i: (0, 0))] * (2 * sub),
        ],
        out_specs=[pl.BlockSpec((width, count), lambda i: (0, 0))] * sub,
        out_shape=[jax.ShapeDtypeStruct((width, count), BF16)] * sub,
        scratch_shapes=[
            pltpu.VMEM((length, cols), F32),
            pltpu.VMEM((length, cols), F32),
            pltpu.VMEM((length // block, cols, block), BF16),
            pltpu.VMEM((length // block, cols, block), BF16),
            pltpu.VMEM((length // block, heads, block), F32),
        ],
        compiler_params=pltpu.CompilerParams(vmem_limit_bytes=VMEM_LIMIT),
        cost_estimate=cost(
            flops=20 * heads * length * length * HEAD_DIM,
            bytes_accessed=4 * length * length,
            transcendentals=heads * length * length,
        ),
        name="attend_backward",
    )(slopes, qkv, lse, far_dist, *ctx, *ctx_grad)


def pack_columns(*values):
    parts = []
    for value in values:
        parts += [value[..., i : i + PACK] for i in range(0, value.shape[-1], PACK)]
    return jnp.concatenate(parts, axis=-2)


def unpack_plan(width, ff, tok_devices, dp_devices):
    far = dp_devices // 2
    half = width // 2
    row_out, row_down = width // tok_devices, ff // tok_devices
    plan = []
    for device in range(dp_devices):
        at, core = device // 2, device % 2
        pieces = []
        first_cols = ff - far * PACK
        for i in range(0, first_cols // far, PACK):
            pieces.append((2, 0, core * ff + at * (first_cols // far) + i, row_out))
        pieces.append((3, at * (row_down // far), core * half, row_down // far))
        pieces.append((1, at * (row_out // far), core * half, row_out // far))
        pieces.append((2, 0, core * ff + first_cols + at * PACK, row_out))
        for i in range(0, 3 * width, PACK):
            pieces.append((0, device * (row_out // dp_devices), i, row_out // dp_devices))
        plan.append(pieces)
    return plan


def assemble(packed, width, ff, tok_devices, dp_devices):
    row_out, row_down = width // tok_devices, ff // tok_devices
    plan = unpack_plan(width, ff, tok_devices, dp_devices)
    shapes = [
        (row_out, LAYERS, 3 * width),
        (row_out, LAYERS, width),
        (row_out, LAYERS, 2 * ff),
        (row_down, LAYERS, width),
    ]
    if row_out // dp_devices % 8:
        outs = [jnp.zeros(shape, F32) for shape in shapes]
        for layer in range(LAYERS):
            for device in range(dp_devices):
                row = 0
                for out, to_row, to_col, count in plan[device]:
                    piece = packed[layer][device, row : row + count].astype(F32)
                    outs[out] = (
                        outs[out].at[to_row : to_row + count, layer, to_col : to_col + PACK]
                    ).set(piece)
                    row += count
        return outs

    def body(*refs):
        in_refs, out_refs = refs[:LAYERS], refs[LAYERS:]
        for layer in range(LAYERS):
            for device in range(dp_devices):
                row = 0
                for out, to_row, to_col, count in plan[device]:
                    piece = in_refs[layer][device, row : row + count, :].astype(F32)
                    out_refs[out][
                        to_row : to_row + count, layer, to_col : to_col + PACK
                    ] = piece
                    row += count

    return pl.pallas_call(
        body,
        out_shape=[jax.ShapeDtypeStruct(shape, F32) for shape in shapes],
        compiler_params=pltpu.CompilerParams(vmem_limit_bytes=VMEM_LIMIT),
        name="assemble",
    )(*packed)


def swap(value, axis, bit):
    return lax.ppermute(value, axis, [(i, i ^ (1 << bit)) for i in range(lax.axis_size(axis))])


def bit_of(axis, bit):
    return (lax.axis_index(axis) >> bit) & 1


def bits_of(axis):
    return lax.axis_size(axis).bit_length() - 1


def add_up(*values):
    total = values[0].astype(F32)
    for value in values[1:]:
        total = total + value.astype(F32)
    return total.astype(BF16)


def reduce_half(value, axis, bit, dim):
    mine = bit_of(axis, bit)
    half = value.shape[dim] // 2
    kept = lax.dynamic_slice_in_dim(value, mine * half, half, dim)
    sent = lax.dynamic_slice_in_dim(value, (1 - mine) * half, half, dim)
    return add_up(kept, swap(sent, axis, bit))


def gather_pair(value, axis, bit, dim):
    mine = bit_of(axis, bit)
    other = swap(value, axis, bit)
    low = jnp.where(mine == 0, value, other)
    high = jnp.where(mine == 0, other, value)
    return jnp.stack((low, high), axis=dim)


def pin(*values):
    return lax.optimization_barrier(values)


def gather_dp(value):
    value = value[None]
    for bit in reversed(range(bits_of("dp"))):
        value = gather_pair(value, "dp", bit, 1)
        value = value.reshape(-1, *value.shape[2:])
    return value


def far_bits(sub):
    return [bit for bit in reversed(range(bits_of("tok"))) if (1 << bit) >= sub]


def per_device(
    tokens, mask, segments, replacement, w_qkv, w_out, w_in, w_down, ln_gain, ln_bias, cotangent
):
    tok_devices = lax.axis_size("tok")
    dp_devices = lax.axis_size("dp")
    seq_count, local_len, width = tokens.shape
    ff = w_down.shape[0]
    sub = tok_devices // seq_count
    per_group = HEADS // sub
    cols = per_group * HEAD_DIM
    tok_count = seq_count * local_len
    full_len = local_len * tok_devices
    tok_place = lax.axis_index("tok")
    group = tok_place % sub
    place_of = group.reshape(1)
    core = bit_of("dp", 0).reshape(1)
    near = [[j + sub * k for j in range(sub)] for k in range(seq_count)]

    def regroup(value):
        place = tok_place // sub
        parts = [lax.dynamic_index_in_dim(value, place, 0, False)]
        for r in range(1, seq_count):
            part = lax.dynamic_index_in_dim(value, place ^ r, 0, False)
            to = [(i, i ^ (r * sub)) for i in range(tok_devices)]
            parts.append(lax.ppermute(part, "tok", to))
        if seq_count == 2:
            low = jnp.where(place == 0, parts[0], parts[1])
            return jnp.stack((low, jnp.where(place == 0, parts[1], parts[0])))
        return jnp.stack(parts)[jnp.arange(seq_count) ^ place]

    def spread(value):
        return lax.all_to_all(value, "tok", 0, 0, axis_index_groups=near)

    near_pairs = [[(i, i ^ r) for i in range(tok_devices)] for r in range(1, sub)]

    def deal(parts):
        return [
            parts[0],
            *(lax.ppermute(p, "tok", to) for p, to in zip(parts[1:], near_pairs)),
        ]

    extra = jnp.zeros((seq_count, local_len, LANES), BF16)
    extra = extra.at[:, :, 0].set((mask == 1).astype(BF16))
    extra = extra.at[:, :, 1].set(segments.astype(BF16))
    mixed = regroup(jnp.concatenate((tokens, extra), axis=-1)).reshape(tok_count, -1)
    wq = split_layers_by_group(w_qkv, sub)
    wo = split_layers(w_out)
    mixed, wq, wo = pin(mixed, wq, wo)
    flags = mixed[:, width:]
    masked = flags[:, :1] == 1.0
    current = jnp.where(masked, replacement[None, :], mixed[:, :width].astype(F32))
    flat_in = current.astype(BF16)

    wi = split_layers(w_in)
    wd = split_layers(w_down)
    slopes = lax.dynamic_slice_in_dim(alibi_slopes(HEADS), group * per_group, per_group, 0)
    order = jnp.arange(sub, dtype=jnp.int32) ^ group
    place = (
        (jnp.arange(seq_count, dtype=jnp.int32)[None, :, None] * sub + order[:, None, None])
        * local_len
        + jnp.arange(local_len, dtype=jnp.int32)[None, None, :]
    ).reshape(full_len)
    far_dist = None
    stored = []
    for layer in range(LAYERS):
        sent = jnp.concatenate((flat_in, flags), axis=-1) if layer == 0 else flat_in
        parts = deal([sent] * sub)
        if layer == 0:
            *parts, wi = pin(*parts, wi)
            labels = jnp.concatenate([p[:, width + 1] for p in parts]).astype(F32)
            far_dist = jnp.where(
                labels[:, None] == labels[None, :],
                jnp.abs(place[:, None] - place[None, :]).astype(F32),
                FAR,
            )
        else:
            *parts, stored[0]["lhs_other"] = pin(*parts, stored[0]["lhs_other"])
        qkv = project(layer, place_of, parts, wq)
        *ctx_here, lse = attend_forward(qkv, far_dist, slopes, sub)
        ctx = deal(ctx_here)
        if layer == 0:
            *ctx, wd = pin(*ctx, wd)
        else:
            *ctx, cot = pin(*ctx, regroup(cotangent))
        lhs, a, b, summed, z, current, flat_in = feed_forward(
            layer, place_of, current, ctx, wo, wi, wd, ln_gain, ln_bias
        )
        stored.append(
            {
                "attend": (parts, qkv, ctx_here, lse),
                "feed": (z, summed, a, b),
                "lhs": lhs,
                "lhs_other": swap(lhs, "dp", 0),
            }
        )
    layer_out = flat_in.reshape(seq_count, local_len, width)
    gradient = cot.reshape(tok_count, width).astype(F32)
    small = []
    row_out = width // tok_devices
    row_down = ff // tok_devices
    half = width // 2
    x_bits = list(reversed(range(1, bits_of("dp"))))
    far = dp_devices // 2

    def near_sum(parts):
        return add_up(*deal(parts))

    def x_sum_rows(arrays):
        for bit in x_bits:
            at = bit_of("dp", bit)
            picked = []
            for choice in (at, 1 - at):
                picked.append(
                    jnp.concatenate(
                        [
                            lax.dynamic_slice_in_dim(
                                v, choice * (v.shape[1] // 2), v.shape[1] // 2, 1
                            )
                            for v in arrays
                        ],
                        axis=1,
                    )
                )
            total = add_up(picked[0], swap(picked[1], "dp", bit))
            ends = [v.shape[1] // 2 for v in arrays]
            arrays = []
            for end in ends:
                first = sum(v.shape[1] for v in arrays)
                arrays.append(total[:, first : first + end])
        return total

    def x_sum_columns(value):
        for bit in x_bits:
            value = reduce_half(value, "dp", bit, value.ndim - 1)
        return value

    def far_sum(value):
        for bit in far_bits(sub):
            value = reduce_half(value, "tok", bit, 0)
        return value[0]

    def by_place(value):
        return value.reshape(seq_count, sub, *value.shape[1:]).swapaxes(0, 1)

    def spread_sum(value):
        return add_up(*spread(by_place(value)))

    def deal_sum(value):
        value = by_place(value)
        return near_sum(
            [lax.dynamic_index_in_dim(value, group ^ r, 0, False) for r in range(sub)]
        )

    def dp_sum(value):
        value = add_up(*lax.all_to_all(value, "dp", 0, 0))
        return value.reshape(seq_count, sub, -1, 3 * cols)

    def by_head(value):
        value = spread(value.swapaxes(0, 1)).reshape(sub, seq_count, -1, 3, cols)
        return value.transpose(1, 2, 3, 0, 4).reshape(seq_count, -1, 3 * width)

    packed = [None] * LAYERS
    before = None
    for layer in reversed(range(LAYERS)):
        parts, qkv, ctx_here, lse = stored[layer]["attend"]
        z, summed, a, b = stored[layer]["feed"]
        lhs, lhs_other = stored[layer]["lhs"], stored[layer]["lhs_other"]
        mine, send, ga, small_part, *gctx = feed_backward(
            layer, core, place_of, gradient, z, summed, a, b, wo, wi, wd, ln_gain, sub
        )
        small.insert(0, small_part)
        if before is not None:
            mine, first, last, qkv_dp, layer_out = pin(
                mine,
                near_sum(before["first"]),
                x_sum_rows(before["rest"]),
                dp_sum(before["qkv"]),
                regroup(layer_out),
            )
            last = jnp.concatenate((before["down"], last), axis=1)
        other = swap(send, "dp", 0)
        ctx_grad = deal(gctx)
        g_down = pair_grad_down(lhs, lhs_other, mine, other, ff)
        *g_first, g_last = pair_grad_in(
            place_of, lhs, lhs_other, mine, other, ff, tok_devices, sub, far
        )
        done = (*ctx_grad, g_down, g_last, *g_first)
        if before is not None:
            done += (x_sum_columns(first), by_head(qkv_dp), last)
        done = pin(*done)
        ctx_grad, g_down, g_last = done[:sub], done[sub], done[sub + 1]
        g_first = done[sub + 2 : 2 * sub + 2]
        g_out = g_down[ff:].reshape(tok_devices, row_out, half)
        g_down = g_down[:ff].reshape(tok_devices, row_down, half)
        g_last = g_last.reshape(tok_devices, far * row_out, PACK)
        head_grad = attend_backward(qkv, ctx_here, ctx_grad, lse, far_dist, slopes)
        if before is not None:
            first, qkv_dp, last = done[2 * sub + 2 :]
            both = pin(
                *head_grad,
                spread_sum(last),
                near_sum(g_first),
                x_sum_rows((g_down, g_out, g_last)),
            )
            head_grad, (last, g_first, g_last) = both[:sub], both[sub:]
            g_qkv = dp_sum(qkv_grad(parts, head_grad, width, tok_devices, dp_devices))
            before_all = pack_columns(first, last, qkv_dp)
            both = pin(
                *head_grad, g_qkv, x_sum_columns(g_first), deal_sum(g_last), far_sum(before_all)
            )
            head_grad, (g_qkv, g_first, g_last, before_all) = both[:sub], both[sub:]
            packed[layer + 1] = lax.all_gather(before_all, "dp")
            back = deal(head_grad)
            packed[layer] = gather_dp(far_sum(pack_columns(g_first, g_last, by_head(g_qkv))))
        else:
            g_qkv = qkv_grad(parts, head_grad, width, tok_devices, dp_devices)
            both = pin(*deal(head_grad), g_qkv, x_sum_rows((g_down,)), g_out, g_last, *g_first)
            back, (g_qkv, g_down, g_out, g_last) = both[:sub], both[sub : sub + 4]
            before = {
                "first": both[sub + 4 :],
                "down": g_down,
                "rest": (g_out, g_last),
                "qkv": g_qkv,
            }
        gradient = input_grad(layer, place_of, ga, back, wq)
    grad_tokens = jnp.where(masked, 0.0, gradient).astype(BF16)
    grad_tokens = regroup(grad_tokens.reshape(seq_count, local_len, width)).astype(F32)
    small.append(jnp.sum(jnp.where(masked, gradient, 0.0), axis=0, keepdims=True))
    small = jnp.concatenate(small, axis=0).reshape(-1, tok_devices, row_out).transpose(1, 0, 2)
    small = jnp.sum(lax.all_to_all(small, "tok", 0, 0), axis=0)
    for bit in range(bits_of("dp")):
        small = small + swap(small, "dp", bit)
    by_layer = small[: 4 * LAYERS].reshape(LAYERS, 2, 2, row_out)
    return (
        layer_out,
        grad_tokens,
        small[-1],
        *assemble(packed, width, ff, tok_devices, dp_devices),
        by_layer[:, 0],
        by_layer[:, 1],
    )


def solution(mesh):
    in_specs = (
        P("dp", "tok", None),
        P("dp", "tok"),
        P("dp", "tok"),
        P(),
        P(),
        P(),
        P(),
        P(),
        P(),
        P(),
        P("dp", "tok", None),
    )
    out_specs = (
        P("dp", "tok", None),
        P("dp", "tok", None),
        P("tok"),
        P("tok", None, None),
        P("tok", None, None),
        P("tok", None, None),
        P("tok", None, None),
        P(None, None, "tok"),
        P(None, None, "tok"),
    )
    return jax.shard_map(
        per_device, mesh=mesh, in_specs=in_specs, out_specs=out_specs, check_vma=False
    )
```

```python
import functools
import math

import jax
import jax.numpy as jnp
from jax import lax
from jax.experimental import pallas as pl
from jax.experimental.pallas import tpu as pltpu
from jax.sharding import PartitionSpec as P

HEADS = 12
HEAD_DIM = 64
LAYERS = 2
LANES = 128
PACK = 384
SCALE = 1.0 / math.sqrt(HEAD_DIM)
FAR = 1e30
BF16 = jnp.bfloat16
F32 = jnp.float32
VMEM_LIMIT = 56 << 20
COST_TIMES = 4


def alibi_slopes(head_count):
    head_index = jnp.arange(head_count, dtype=jnp.float32)
    return jnp.exp2(jnp.where(head_index < 8.0, -(head_index + 1.0), 7.5 - head_index))


def dot(a, b, dims):
    return lax.dot_general(a, b, (dims, ((), ())), preferred_element_type=F32)


def cost(flops, bytes_accessed, transcendentals):
    return pl.CostEstimate(
        flops=COST_TIMES * flops,
        bytes_accessed=bytes_accessed,
        transcendentals=transcendentals,
    )


NN = ((1,), (0,))
NT = ((1,), (1,))
TN = ((0,), (0,))


def split_layers(weight):
    rows, _, cols = weight.shape
    row_block = 256
    col_block = next(c for c in (3072, 2304, 1152, 768) if cols % c == 0)

    def body(in_ref, out_ref):
        to_row = lax.broadcasted_iota(jnp.int32, (256, 256), 0)
        from_row = lax.broadcasted_iota(jnp.int32, (256, 256), 1)
        wanted = jnp.where(to_row < 128, 2 * to_row, 2 * to_row - 255)
        pick = jnp.where(from_row == wanted, 1.0, 0.0).astype(BF16)
        for part in range(row_block // 128):
            at = slice(part * 128, part * 128 + 128)
            mixed = in_ref[at].reshape(256, col_block)
            picked = dot(pick, mixed, NN).astype(BF16)
            out_ref[0, at] = picked[:128]
            out_ref[1, at] = picked[128:]

    return pl.pallas_call(
        body,
        grid=(rows // row_block, cols // col_block),
        in_specs=[pl.BlockSpec((row_block, 2, col_block), lambda i, j: (i, 0, j))],
        out_specs=pl.BlockSpec((2, row_block, col_block), lambda i, j: (0, i, j)),
        out_shape=jax.ShapeDtypeStruct((2, rows, cols), BF16),
        compiler_params=pltpu.CompilerParams(vmem_limit_bytes=VMEM_LIMIT),
        cost_estimate=cost(
            flops=2 * 512 * rows * cols, bytes_accessed=8 * rows * cols, transcendentals=0
        ),
        name="split_layers",
    )(weight)


def split_layers_by_group(weight, sub):
    rows, _, cols = weight.shape
    row_block = 256
    group_cols = cols // sub // 3

    def body(in_ref, out_ref):
        to_row = lax.broadcasted_iota(jnp.int32, (256, 256), 0)
        from_row = lax.broadcasted_iota(jnp.int32, (256, 256), 1)
        wanted = jnp.where(to_row < 128, 2 * to_row, 2 * to_row - 255)
        pick = jnp.where(from_row == wanted, 1.0, 0.0).astype(BF16)
        for part in range(row_block // 128):
            at = slice(part * 128, part * 128 + 128)
            picked = dot(pick, in_ref[at].reshape(256, cols), NN).astype(BF16)
            for j in range(sub):
                for n in range(3):
                    first = (n * sub + j) * group_cols
                    block = picked[:, first : first + group_cols]
                    to = slice(n * group_cols, n * group_cols + group_cols)
                    out_ref[0, j, at, to] = block[:128]
                    out_ref[1, j, at, to] = block[128:]

    return pl.pallas_call(
        body,
        grid=(rows // row_block,),
        in_specs=[pl.BlockSpec((row_block, 2, cols), lambda i: (i, 0, 0))],
        out_specs=pl.BlockSpec((2, sub, row_block, 3 * group_cols), lambda i: (0, 0, i, 0)),
        out_shape=jax.ShapeDtypeStruct((2, sub, rows, 3 * group_cols), BF16),
        compiler_params=pltpu.CompilerParams(vmem_limit_bytes=VMEM_LIMIT),
        cost_estimate=cost(
            flops=2 * 512 * rows * cols, bytes_accessed=8 * rows * cols, transcendentals=0
        ),
        name="split_qkv",
    )(weight)


def norm_parts(value):
    center = jnp.mean(value, axis=-1, keepdims=True)
    shifted = value - center
    inverse = lax.rsqrt(jnp.mean(shifted * shifted, axis=-1, keepdims=True) + 1e-12)
    return shifted * inverse, inverse


def norm_grad(grad, value, gain):
    normed, inverse = norm_parts(value)
    scaled = grad * gain
    one = jnp.mean(scaled, axis=-1, keepdims=True)
    two = jnp.mean(scaled * normed, axis=-1, keepdims=True)
    in_grad = inverse * (scaled - one - normed * two)
    gain_grad = jnp.sum(grad * normed, axis=0, keepdims=True)
    bias_grad = jnp.sum(grad, axis=0, keepdims=True)
    return in_grad, gain_grad, bias_grad


def feed_forward(layer, group, current, ctx, w_out, w_in, w_down, gain, bias):
    count, width = current.shape
    sub, cols = len(ctx), ctx[0].shape[0]
    ff = w_down.shape[1]
    chunk = 768
    steps = ff // chunk

    def body(group_ref, *refs):
        ctx_refs = refs[:sub]
        cur_ref, wo_ref, wg_ref, wu_ref, wd_ref, gain_ref, bias_ref = refs[sub : sub + 7]
        lhs_ref, a_ref, b_ref, sum_ref, z_ref, next_ref, low_ref = refs[sub + 7 : sub + 14]
        y1l_ref, acc_ref, held_ref = refs[sub + 14 :]
        step = pl.program_id(0)

        @pl.when(step == 0)
        def _():
            branch = jnp.zeros((count, width), F32)
            for r in range(sub):
                held_ref[jnp.bitwise_xor(group_ref[0], r)] = ctx_refs[r][...]
            for j in range(sub):
                part = held_ref[j]
                to = slice(j * cols, j * cols + cols)
                lhs_ref[:, width + ff + j * cols : width + ff + j * cols + cols] = (
                    part.astype(F32).T.astype(BF16)
                )
                branch += dot(part, wo_ref[0, to, :], TN)
            summed = cur_ref[...] + branch
            sum_ref[...] = summed
            normed, _ = norm_parts(summed)
            y1 = normed * gain_ref[layer, 0:1, :] + bias_ref[layer, 0:1, :]
            acc_ref[...] = y1
            y1l_ref[...] = y1.astype(BF16)
            lhs_ref[:, :width] = y1.astype(BF16)

        y1l = y1l_ref[...]
        gate = dot(y1l, wg_ref[0], NN)
        up = dot(y1l, wu_ref[0], NN)
        cdf = 0.5 * (1.0 + lax.erf(gate * (0.5**0.5)))
        density = jnp.exp(-0.5 * gate * gate) * (1.0 / math.sqrt(2.0 * math.pi))
        gelu = gate * cdf
        hidden = (gelu * up).astype(BF16)
        a_ref[...] = gelu.astype(BF16)
        b_ref[...] = (up * (cdf + gate * density)).astype(BF16)
        lhs_ref[:, pl.ds(pl.multiple_of(width + step * chunk, 128), chunk)] = hidden
        acc_ref[...] += dot(hidden, wd_ref[0], NN)

        @pl.when(step == steps - 1)
        def _():
            z = acc_ref[...]
            z_ref[...] = z
            normed, _ = norm_parts(z)
            out = normed * gain_ref[layer, 1:2, :] + bias_ref[layer, 1:2, :]
            next_ref[...] = out
            low_ref[...] = out.astype(BF16)

    whole = lambda *shape: pl.BlockSpec(shape, lambda i: (0,) * len(shape))
    return pl.pallas_call(
        body,
        grid=(steps,),
        in_specs=[
            pl.BlockSpec(memory_space=pltpu.SMEM),
            *[whole(cols, count)] * sub,
            whole(count, width),
            pl.BlockSpec((1, width, width), lambda i: (layer, 0, 0)),
            pl.BlockSpec((1, width, chunk), lambda i: (layer, 0, i)),
            pl.BlockSpec((1, width, chunk), lambda i: (layer, 0, steps + i)),
            pl.BlockSpec((1, chunk, width), lambda i: (layer, i, 0)),
            whole(*gain.shape),
            whole(*bias.shape),
        ],
        out_specs=[
            whole(count, ff + 2 * width),
            pl.BlockSpec((count, chunk), lambda i: (0, i)),
            pl.BlockSpec((count, chunk), lambda i: (0, i)),
            whole(count, width),
            whole(count, width),
            whole(count, width),
            whole(count, width),
        ],
        out_shape=[
            jax.ShapeDtypeStruct((count, ff + 2 * width), BF16),
            jax.ShapeDtypeStruct((count, ff), BF16),
            jax.ShapeDtypeStruct((count, ff), BF16),
            jax.ShapeDtypeStruct((count, width), F32),
            jax.ShapeDtypeStruct((count, width), F32),
            jax.ShapeDtypeStruct((count, width), F32),
            jax.ShapeDtypeStruct((count, width), BF16),
        ],
        scratch_shapes=[
            pltpu.VMEM((count, width), BF16),
            pltpu.VMEM((count, width), F32),
            pltpu.VMEM((sub, cols, count), BF16),
        ],
        compiler_params=pltpu.CompilerParams(vmem_limit_bytes=VMEM_LIMIT),
        cost_estimate=cost(
            flops=2 * count * width * (width + 3 * ff),
            bytes_accessed=6 * width * ff + 2 * width * width + count * (20 * width + 6 * ff),
            transcendentals=2 * count * ff,
        ),
        name="feed_forward",
    )(group, *ctx, current, w_out, w_in, w_in, w_down, gain, bias)


def feed_backward(layer, core, group, grad, z, summed, a, b, w_out, w_in, w_down, gain, sub):
    count, width = grad.shape
    ff = w_down.shape[1]
    cols = width // sub
    half = width // 2
    chunk = 768
    steps = ff // chunk

    def body(
        core_ref, group_ref, grad_ref, z_ref, sum_ref, a_ref, b_ref,
        wo_ref, wg_ref, wu_ref, wd_ref, gain_ref, mine_ref, send_ref, ga_ref, small_ref, *refs,
    ):
        gctx_refs = refs[:sub]
        gzl_ref, acc_ref, held_ref = refs[sub:]
        step = pl.program_id(0)
        first = core_ref[0] == 0

        def store(to, low, high):
            mine_ref[:, to] = jnp.where(first, low, high)
            send_ref[:, to] = jnp.where(first, high, low)

        @pl.when(step == 0)
        def _():
            gz, gain_grad, bias_grad = norm_grad(grad_ref[...], z_ref[...], gain_ref[layer, 1:2, :])
            small_ref[1:2, :] = gain_grad
            small_ref[3:4, :] = bias_grad
            acc_ref[...] = gz
            gzl = gz.astype(BF16)
            gzl_ref[...] = gzl
            store(slice(ff, ff + half), gz[:, :half].astype(BF16), gz[:, half:].astype(BF16))

        gzl = gzl_ref[...]
        ghid = dot(gzl, wd_ref[0], NT)
        ggate = (ghid * b_ref[...].astype(F32)).astype(BF16)
        gup = (ghid * a_ref[...].astype(F32)).astype(BF16)
        store(pl.ds(pl.multiple_of(step * chunk, 128), chunk), ggate, gup)
        acc_ref[...] += dot(ggate, wg_ref[0], NT) + dot(gup, wu_ref[0], NT)

        @pl.when(step == steps - 1)
        def _():
            ga, gain_grad, bias_grad = norm_grad(
                acc_ref[...], sum_ref[...], gain_ref[layer, 0:1, :]
            )
            small_ref[0:1, :] = gain_grad
            small_ref[2:3, :] = bias_grad
            ga_ref[...] = ga
            gal = ga.astype(BF16)
            store(slice(ff + half, ff + width), gal[:, :half], gal[:, half:])
            for j in range(sub):
                to = slice(j * cols, j * cols + cols)
                held_ref[j] = dot(wo_ref[0, to, :], gal, NT).astype(BF16)
            for r in range(sub):
                gctx_refs[r][...] = held_ref[jnp.bitwise_xor(group_ref[0], r)]

    whole = lambda *shape: pl.BlockSpec(shape, lambda i: (0,) * len(shape))
    return pl.pallas_call(
        body,
        grid=(steps,),
        in_specs=[
            pl.BlockSpec(memory_space=pltpu.SMEM),
            pl.BlockSpec(memory_space=pltpu.SMEM),
            whole(count, width),
            whole(count, width),
            whole(count, width),
            pl.BlockSpec((count, chunk), lambda i: (0, i)),
            pl.BlockSpec((count, chunk), lambda i: (0, i)),
            pl.BlockSpec((1, width, width), lambda i: (layer, 0, 0)),
            pl.BlockSpec((1, width, chunk), lambda i: (layer, 0, i)),
            pl.BlockSpec((1, width, chunk), lambda i: (layer, 0, steps + i)),
            pl.BlockSpec((1, chunk, width), lambda i: (layer, i, 0)),
            whole(*gain.shape),
        ],
        out_specs=[
            whole(count, ff + width),
            whole(count, ff + width),
            whole(count, width),
            whole(4, width),
            *[whole(cols, count)] * sub,
        ],
        out_shape=[
            jax.ShapeDtypeStruct((count, ff + width), BF16),
            jax.ShapeDtypeStruct((count, ff + width), BF16),
            jax.ShapeDtypeStruct((count, width), F32),
            jax.ShapeDtypeStruct((4, width), F32),
            *[jax.ShapeDtypeStruct((cols, count), BF16)] * sub,
        ],
        scratch_shapes=[
            pltpu.VMEM((count, width), BF16),
            pltpu.VMEM((count, width), F32),
            pltpu.VMEM((sub, cols, count), BF16),
        ],
        compiler_params=pltpu.CompilerParams(vmem_limit_bytes=VMEM_LIMIT),
        cost_estimate=cost(
            flops=2 * count * width * (width + 3 * ff),
            bytes_accessed=6 * width * ff + 2 * width * width + count * (24 * width + 8 * ff),
            transcendentals=0,
        ),
        name="feed_backward",
    )(core, group, grad, z, summed, a, b, w_out, w_in, w_in, w_down, gain)


def pair_grads(group, side, lhs, lhs_other, rhs, rhs_other, ff, tok_devices, sub, far, early):
    count = lhs.shape[0]
    width = rhs.shape[1] - ff
    half = width // 2
    rows, rows_down = width // tok_devices, ff // tok_devices
    seqs = tok_devices // sub
    chunk = 2 * PACK
    steps_in, steps_down = ff // chunk, ff // chunk
    first_steps = steps_in - far * PACK // chunk
    ends = [0, 1, first_steps] if early else [0, first_steps]
    spans = list(zip(ends[:-1], ends[1:]))
    split = far // 2
    half_down, half_out = rows_down // 2, rows // 2

    def body(group_ref, side_ref, l1_ref, l2_ref, r1_ref, r2_ref, h1_ref, h2_ref, *refs):
        out_refs = refs[: len(spans) * sub]
        keep_ref, send_ref, keep_in_ref, send_in_ref, held_ref = refs[len(spans) * sub :]
        step = pl.program_id(0)
        low_side = side_ref[0] == 0

        def store(t, at, low, high):
            keep_ref[t, at] = jnp.where(low_side, low, high).astype(BF16)
            send_ref[t, at] = jnp.where(low_side, high, low).astype(BF16)

        @pl.when(step < steps_in)
        def _():
            out = dot(l1_ref[...], r1_ref[...], TN) + dot(l2_ref[...], r2_ref[...], TN)

            @pl.when(step < first_steps)
            def _():
                for t in range(tok_devices):
                    held_ref[t % sub, t // sub] = out[t * rows : t * rows + rows].astype(BF16)

            for n, (begin, end) in enumerate(spans):

                @pl.when((step >= begin) & (step < end))
                def _():
                    for r in range(sub):
                        out_refs[n * sub + r][...] = held_ref[jnp.bitwise_xor(group_ref[0], r)]

            for f in range(2):
                block = 2 * (step - first_steps) + f
                here = block // split == side_ref[0]
                to = block % split
                for wanted, ref in ((here, keep_in_ref), (jnp.logical_not(here), send_in_ref)):

                    @pl.when((step >= first_steps) & wanted)
                    def _():
                        for t in range(tok_devices):
                            part = out[t * rows : t * rows + rows, f * PACK : f * PACK + PACK]
                            ref[t, to] = part.astype(BF16)

        @pl.when(step >= steps_in)
        def _():
            out = dot(l1_ref[...], h1_ref[...], TN) + dot(l2_ref[...], h2_ref[...], TN)
            each = chunk // rows_down

            @pl.when(step < steps_in + steps_down)
            def _():
                for i in range(each):
                    low = out[i * rows_down : i * rows_down + half_down]
                    high = out[i * rows_down + half_down : (i + 1) * rows_down]
                    store((step - steps_in) * each + i, slice(0, half_down), low, high)

            @pl.when(step == steps_in + steps_down)
            def _():
                for t in range(tok_devices):
                    low = out[t * rows : t * rows + half_out]
                    high = out[t * rows + half_out : (t + 1) * rows]
                    store(t, slice(half_down, half_down + half_out), low, high)

    left = pl.BlockSpec((count, chunk), lambda i: (0, jnp.maximum(i - steps_in + 1, 0)))
    right = pl.BlockSpec((count, chunk), lambda i: (0, jnp.minimum(i, steps_in - 1)))
    halves = pl.BlockSpec(
        (count, half), lambda i: (0, ff // half + jnp.where(i < steps_in + steps_down, 0, 1))
    )
    kept = (tok_devices, half_down + half_out, half)
    kept_in = (tok_devices, split, rows, PACK)
    whole = lambda *shape: pl.BlockSpec(shape, lambda i: (0,) * len(shape))
    return pl.pallas_call(
        body,
        grid=(steps_in + steps_down + 1,),
        in_specs=[
            pl.BlockSpec(memory_space=pltpu.SMEM),
            pl.BlockSpec(memory_space=pltpu.SMEM),
            left,
            left,
            right,
            right,
            halves,
            halves,
        ],
        out_specs=[
            *[
                pl.BlockSpec(
                    (seqs, rows, chunk),
                    functools.partial(
                        lambda begin, end, i: (0, 0, jnp.clip(i - begin, 0, end - begin - 1)),
                        begin,
                        end,
                    ),
                )
                for begin, end in spans
                for _ in range(sub)
            ],
            whole(*kept),
            whole(*kept),
            whole(*kept_in),
            whole(*kept_in),
        ],
        out_shape=[
            *[
                jax.ShapeDtypeStruct((seqs, rows, (end - begin) * chunk), BF16)
                for begin, end in spans
                for _ in range(sub)
            ],
            jax.ShapeDtypeStruct(kept, BF16),
            jax.ShapeDtypeStruct(kept, BF16),
            jax.ShapeDtypeStruct(kept_in, BF16),
            jax.ShapeDtypeStruct(kept_in, BF16),
        ],
        scratch_shapes=[pltpu.VMEM((sub, seqs, rows, chunk), BF16)],
        compiler_params=pltpu.CompilerParams(vmem_limit_bytes=VMEM_LIMIT),
        cost_estimate=cost(
            flops=8 * count * width * ff,
            bytes_accessed=4 * width * ff + 8 * count * (width + ff),
            transcendentals=0,
        ),
        name="pair_grads",
    )(group, side, lhs, lhs_other, rhs, rhs_other, rhs, rhs_other)


def input_grad(layer, group, ga, back, w_qkv):
    sub = len(back)
    cols, count = back[0].shape
    width = ga.shape[1]

    def body(group_ref, ga_ref, w_ref, *refs):
        back_refs, out_ref, acc_ref = refs[:sub], refs[sub], refs[sub + 1]
        step = pl.program_id(0)

        @pl.when(step == 0)
        def _():
            acc_ref[...] = jnp.zeros_like(acc_ref)

        for r in range(sub):

            @pl.when(step == r)
            def _():
                acc_ref[...] += dot(w_ref[0, 0], back_refs[r][...], NN)

        @pl.when(step == sub - 1)
        def _():
            out_ref[...] = ga_ref[...] + acc_ref[...].T

    return pl.pallas_call(
        body,
        grid_spec=pltpu.PrefetchScalarGridSpec(
            num_scalar_prefetch=1,
            grid=(sub,),
            in_specs=[
                pl.BlockSpec((count, width), lambda i, g: (0, 0)),
                pl.BlockSpec(
                    (1, 1, width, cols), lambda i, g: (layer, jnp.bitwise_xor(g[0], i), 0, 0)
                ),
                *[pl.BlockSpec((cols, count), lambda i, g: (0, 0))] * sub,
            ],
            out_specs=pl.BlockSpec((count, width), lambda i, g: (0, 0)),
            scratch_shapes=[pltpu.VMEM((width, count), F32)],
        ),
        out_shape=jax.ShapeDtypeStruct((count, width), F32),
        compiler_params=pltpu.CompilerParams(vmem_limit_bytes=VMEM_LIMIT),
        cost_estimate=cost(
            flops=2 * count * width * cols * sub,
            bytes_accessed=2 * sub * cols * (width + count) + 8 * count * width,
            transcendentals=0,
        ),
        name="input_grad",
    )(group, ga, w_qkv, *back)


def project(layer, group, parts, w_qkv):
    sub = len(parts)
    count = parts[0].shape[0]
    width, cols = w_qkv.shape[2:]

    def body(group_ref, w_ref, *refs):
        out_ref = refs[sub]
        for r in range(sub):
            out_ref[r * count : r * count + count, :] = dot(
                refs[r][...], w_ref[0, 0], NN
            ).astype(BF16)

    return pl.pallas_call(
        body,
        grid_spec=pltpu.PrefetchScalarGridSpec(
            num_scalar_prefetch=1,
            grid=(1,),
            in_specs=[
                pl.BlockSpec((1, 1, width, cols), lambda i, g: (layer, g[0], 0, 0)),
                *[pl.BlockSpec((count, width), lambda i, g: (0, 0))] * sub,
            ],
            out_specs=pl.BlockSpec((sub * count, cols), lambda i, g: (0, 0)),
        ),
        out_shape=jax.ShapeDtypeStruct((sub * count, cols), BF16),
        compiler_params=pltpu.CompilerParams(vmem_limit_bytes=VMEM_LIMIT),
        cost_estimate=cost(
            flops=2 * sub * count * width * cols,
            bytes_accessed=2 * (width * cols + sub * count * (width + cols)),
            transcendentals=0,
        ),
        name="project",
    )(group, w_qkv, *parts)


def qkv_grad(parts, grads, width, tok_devices, dp_devices):
    sub = len(parts)
    count = parts[0].shape[0]
    cols = grads[0].shape[0]
    rows = width // tok_devices
    few = rows // dp_devices

    def body(*refs):
        qkv_grad_body(refs[:sub], refs[sub : 2 * sub], refs[2 * sub], rows, few)

    shape = (dp_devices, tok_devices, few, cols)
    return pl.pallas_call(
        body,
        grid=(1,),
        in_specs=[
            *[pl.BlockSpec((count, width), lambda i: (0, 0))] * sub,
            *[pl.BlockSpec((cols, count), lambda i: (0, 0))] * sub,
        ],
        out_specs=pl.BlockSpec(shape, lambda i: (0, 0, 0, 0)),
        out_shape=jax.ShapeDtypeStruct(shape, BF16),
        compiler_params=pltpu.CompilerParams(vmem_limit_bytes=VMEM_LIMIT),
        cost_estimate=pl.CostEstimate(flops=1 << 20, bytes_accessed=1 << 10, transcendentals=0),
        name="qkv_grad",
    )(*parts, *grads)


def qkv_grad_body(part_refs, grad_refs, out_ref, rows, few):
    cols, width = grad_refs[0].shape[0], part_refs[0].shape[1]
    acc = jnp.zeros((cols, width), F32)
    for part_ref, grad_ref in zip(part_refs, grad_refs):
        acc += dot(grad_ref[...], part_ref[...], NN)
    acc = acc.T
    dp_devices, tok_devices = out_ref.shape[:2]
    for t in range(tok_devices):
        for q in range(dp_devices):
            first = t * rows + q * few
            out_ref[q, t, :few, :] = acc[first : first + few].astype(BF16)


def last_grads(group, small, masks, parts, grads, ga, w_qkv, tok_devices, dp_devices):
    sub = len(grads)
    cols, count = grads[0].shape
    width = ga.shape[1]
    rows = width // tok_devices
    few = rows // dp_devices

    def twice(value):
        high = value.astype(BF16)
        return high, (value - high.astype(F32)).astype(BF16)

    def body(group_ref, mask_ref, ga_ref, w_ref, small_ref, *refs):
        part_refs, grad_refs, out_ref = refs[:sub], refs[sub : 2 * sub], refs[2 * sub]
        qkv_grad_body(part_refs, grad_refs, out_ref, rows, few)
        total = jnp.zeros((16, cols), F32)
        for r in range(sub):
            total += dot(mask_ref[r], grad_refs[r][...], NT)
        mask_sum = jnp.zeros((16, width), F32)
        for part in twice(total):
            mask_sum += dot(part, w_ref[0, 0], NT)
        for part in twice(ga_ref[...]):
            mask_sum += dot(mask_ref[0], part, NN)
        values = small_ref[...]
        for t in range(tok_devices):
            for q in range(dp_devices):
                of = slice(t * rows + q * few, t * rows + q * few + few)
                row = jnp.concatenate(
                    (
                        jnp.pad(values[:, of], ((0, 0), (0, LANES - few))),
                        jnp.pad(mask_sum[:8, of], ((0, 0), (0, cols - LANES - few))),
                    ),
                    axis=1,
                )
                out_ref[q, t, few:, :] = row.astype(BF16)

    whole = lambda *shape: pl.BlockSpec(shape, lambda i, g: (0,) * len(shape))
    shape = (dp_devices, tok_devices, few + 8, cols)
    return pl.pallas_call(
        body,
        grid_spec=pltpu.PrefetchScalarGridSpec(
            num_scalar_prefetch=1,
            grid=(1,),
            in_specs=[
                whole(sub, 16, count),
                whole(count, width),
                pl.BlockSpec((1, 1, width, cols), lambda i, g: (0, g[0], 0, 0)),
                whole(8, width),
                *[whole(count, width)] * sub,
                *[whole(cols, count)] * sub,
            ],
            out_specs=whole(*shape),
        ),
        out_shape=jax.ShapeDtypeStruct(shape, BF16),
        compiler_params=pltpu.CompilerParams(vmem_limit_bytes=VMEM_LIMIT),
        cost_estimate=pl.CostEstimate(flops=1 << 20, bytes_accessed=1 << 10, transcendentals=0),
        name="last_grads",
    )(group, masks, ga, w_qkv, small, *parts, *grads)


def attend_forward(qkv, far_dist, slopes, sub):
    length, width = qkv.shape
    cols = width // 3
    heads = cols // HEAD_DIM
    count = length // sub
    block = 256
    per = count // block

    def body(slope_ref, qkv_ref, dist_ref, *refs):
        ctx_refs, lse_ref, held_ref = refs[:sub], refs[sub], refs[sub + 1]
        step = pl.program_id(0)
        at = pl.ds(pl.multiple_of(step * block, block), block)
        dist = dist_ref[...]
        for h in range(heads):
            q = qkv_ref[at, h * 64 : h * 64 + 64]
            k = qkv_ref[:, cols + h * 64 : cols + h * 64 + 64]
            v = qkv_ref[:, 2 * cols + h * 64 : 2 * cols + h * 64 + 64]
            s = dot(k, q, NT) * SCALE - dist * slope_ref[h]
            top = jnp.max(s, axis=0, keepdims=True)
            e = jnp.exp(s - top)
            total = jnp.sum(e, axis=0, keepdims=True)
            ctx = dot(v, e.astype(BF16), TN) / total
            held_ref[h * 64 : h * 64 + 64, :] = ctx.astype(BF16)
            lse_ref[h : h + 1, :] = top + jnp.log(total)
        for i in range(length // block):

            @pl.when(step == i)
            def _():
                first = i % per * block
                ctx_refs[i // per][:, first : first + block] = held_ref[...]

    return pl.pallas_call(
        body,
        grid=(length // block,),
        in_specs=[
            pl.BlockSpec(memory_space=pltpu.SMEM),
            pl.BlockSpec((length, width), lambda i: (0, 0)),
            pl.BlockSpec((length, block), lambda i: (0, i)),
        ],
        out_specs=[
            *[pl.BlockSpec((cols, count), lambda i: (0, 0))] * sub,
            pl.BlockSpec((heads, block), lambda i: (0, i)),
        ],
        out_shape=[
            *[jax.ShapeDtypeStruct((cols, count), BF16)] * sub,
            jax.ShapeDtypeStruct((heads, length), F32),
        ],
        scratch_shapes=[pltpu.VMEM((cols, block), BF16)],
        compiler_params=pltpu.CompilerParams(vmem_limit_bytes=VMEM_LIMIT),
        cost_estimate=cost(
            flops=16 * heads * length * length * HEAD_DIM,
            bytes_accessed=4 * length * length,
            transcendentals=heads * length * length,
        ),
        name="attend_forward",
    )(slopes, qkv, far_dist)


def attend_backward(qkv, ctx, ctx_grad, lse, far_dist, slopes):
    length, width = qkv.shape
    sub = len(ctx)
    cols = width // 3
    heads = cols // HEAD_DIM
    count = length // sub
    block = 256
    per = count // block

    def body(slope_ref, qkv_ref, lse_ref, dist_ref, *refs):
        ctx_refs, g_refs, out_refs = refs[:sub], refs[sub : 2 * sub], refs[2 * sub : 3 * sub]
        dk_ref, dv_ref, dq_ref, held_ref, inner_ref = refs[3 * sub :]
        step = pl.program_id(0)
        at = pl.ds(pl.multiple_of(step * block, block), block)

        @pl.when(step == 0)
        def _():
            dk_ref[...] = jnp.zeros_like(dk_ref)
            dv_ref[...] = jnp.zeros_like(dv_ref)
            for r in range(sub):
                g = g_refs[r][...]
                both = g.astype(F32) * ctx_refs[r][...].astype(F32)
                for p in range(per):
                    of = slice(p * block, p * block + block)
                    held_ref[r * per + p] = g[:, of]
                    for h in range(heads):
                        inner_ref[r * per + p, h : h + 1, :] = jnp.sum(
                            both[h * 64 : h * 64 + 64, of], axis=0, keepdims=True
                        )

        dist = dist_ref[...]
        for h in range(heads):
            mine = slice(h * 64, h * 64 + 64)
            q = qkv_ref[at, mine]
            k = qkv_ref[:, cols + h * 64 : cols + h * 64 + 64]
            v = qkv_ref[:, 2 * cols + h * 64 : 2 * cols + h * 64 + 64]
            g = held_ref[step, mine, :]
            s = dot(k, q, NT) * SCALE - dist * slope_ref[h]
            p = jnp.exp(s - lse_ref[h : h + 1, :])
            gp = dot(v, g, NN)
            gs = (p * (gp - inner_ref[step, h : h + 1, :])).astype(BF16)
            dv_ref[:, mine] += dot(p.astype(BF16), g, NT)
            dk_ref[:, mine] += dot(gs, q, NN)
            dq_ref[step, mine, :] = (dot(k, gs, TN) * SCALE).astype(BF16)

        @pl.when(step == pl.num_programs(0) - 1)
        def _():
            for r in range(sub):
                of = slice(r * count, r * count + count)
                for p in range(per):
                    out_refs[r][:cols, p * block : p * block + block] = dq_ref[r * per + p]
                out_refs[r][cols : 2 * cols, :] = (dk_ref[of, :] * SCALE).T.astype(BF16)
                out_refs[r][2 * cols :, :] = dv_ref[of, :].T.astype(BF16)

    return pl.pallas_call(
        body,
        grid=(length // block,),
        in_specs=[
            pl.BlockSpec(memory_space=pltpu.SMEM),
            pl.BlockSpec((length, width), lambda i: (0, 0)),
            pl.BlockSpec((heads, block), lambda i: (0, i)),
            pl.BlockSpec((length, block), lambda i: (0, i)),
            *[pl.BlockSpec((cols, count), lambda i: (0, 0))] * (2 * sub),
        ],
        out_specs=[pl.BlockSpec((width, count), lambda i: (0, 0))] * sub,
        out_shape=[jax.ShapeDtypeStruct((width, count), BF16)] * sub,
        scratch_shapes=[
            pltpu.VMEM((length, cols), F32),
            pltpu.VMEM((length, cols), F32),
            pltpu.VMEM((length // block, cols, block), BF16),
            pltpu.VMEM((length // block, cols, block), BF16),
            pltpu.VMEM((length // block, heads, block), F32),
        ],
        compiler_params=pltpu.CompilerParams(vmem_limit_bytes=VMEM_LIMIT),
        cost_estimate=cost(
            flops=8 * heads * length * length * HEAD_DIM,
            bytes_accessed=4 * length * length,
            transcendentals=heads * length * length,
        ),
        name="attend_backward",
    )(slopes, qkv, lse, far_dist, *ctx, *ctx_grad)


def pack_columns(*values):
    rows = [value.shape[-2] for value in values]
    blocks = [value.shape[-1] // PACK for value in values]
    lead = values[0].shape[:-2]
    total = sum(r * n for r, n in zip(rows, blocks))
    if any(r % 8 for r in rows):
        parts = []
        for value in values:
            parts += [value[..., i : i + PACK] for i in range(0, value.shape[-1], PACK)]
        return jnp.concatenate(parts, axis=-2)

    def body(*refs):
        out_ref = refs[-1]
        for i in range(math.prod(lead)):
            at = 0
            for ref, r, n in zip(refs, rows, blocks):
                value = ref[i].astype(F32) if r % 16 else ref[i]
                for j in range(n):
                    out_ref[i, at : at + r, :] = value[:, j * PACK : j * PACK + PACK].astype(BF16)
                    at += r

    flat = [value.reshape(math.prod(lead), *value.shape[-2:]) for value in values]
    return pl.pallas_call(
        body,
        out_shape=jax.ShapeDtypeStruct((math.prod(lead), total, PACK), BF16),
        compiler_params=pltpu.CompilerParams(vmem_limit_bytes=VMEM_LIMIT),
cost_estimate=pl.CostEstimate(flops=1 << 20, bytes_accessed=1 << 10, transcendentals=0),
        name="pack_columns",
    )(*flat).reshape(*lead, total, PACK)


def unpack_plan(width, ff, tok_devices, dp_devices):
    far = dp_devices // 2
    half = width // 2
    row_out, row_down = width // tok_devices, ff // tok_devices
    few = row_out // dp_devices
    plan = [[], [], []]
    for device in range(dp_devices):
        at, core = device // 2, device % 2
        first_cols = ff - far * PACK
        firsts, lasts, heads = [], [], []
        for layer in range(LAYERS):
            firsts.append(
                [
                    (2, layer, 0, core * ff + at * (first_cols // far) + i, row_out)
                    for i in range(0, first_cols // far, PACK)
                ]
            )
            lasts.append(
                [
                    (3, layer, at * (row_down // far), core * half, row_down // far),
                    (1, layer, at * (row_out // far), core * half, row_out // far),
                    (2, layer, 0, core * ff + first_cols + at * PACK, row_out),
                ]
            )
        for i in range(0, 3 * width, PACK):
            for layer in range(LAYERS):
                heads.append((0, layer, device * few, i, few))
        plan[0].append(firsts[0])
        gap = [(None, 0, 0, 0, 8)]
        plan[1].append(lasts[0] + gap + heads)
        plan[2].append(firsts[1] + lasts[1])
    return plan


def assemble(packed, width, ff, tok_devices, dp_devices):
    row_out, row_down = width // tok_devices, ff // tok_devices
    plan = unpack_plan(width, ff, tok_devices, dp_devices)
    shapes = [
        (row_out, LAYERS, 3 * width),
        (row_out, LAYERS, width),
        (row_out, LAYERS, 2 * ff),
        (row_down, LAYERS, width),
    ]
    if row_out // dp_devices % 8:
        outs = [jnp.zeros(shape, F32) for shape in shapes]
        for array, pieces in zip(packed, plan):
            for device in range(dp_devices):
                row = 0
                for out, n, to_row, to_col, count in pieces[device]:
                    if out is not None:
                        piece = array[device, row : row + count].astype(F32)
                        outs[out] = (
                            outs[out].at[to_row : to_row + count, n, to_col : to_col + PACK]
                        ).set(piece)
                    row += count
        return outs

    def body(*refs):
        in_refs, out_refs = refs[: len(plan)], refs[len(plan) :]
        for ref, pieces in zip(in_refs, plan):
            for device in range(dp_devices):
                row = 0
                for out, n, to_row, to_col, count in pieces[device]:
                    if out is not None:
                        piece = ref[device, row : row + count, :].astype(F32)
                        out_refs[out][to_row : to_row + count, n, to_col : to_col + PACK] = piece
                    row += count

    return pl.pallas_call(
        body,
        out_shape=[jax.ShapeDtypeStruct(shape, F32) for shape in shapes],
        compiler_params=pltpu.CompilerParams(vmem_limit_bytes=VMEM_LIMIT),
        name="assemble",
    )(*packed)


def swap(value, axis, bit):
    return lax.ppermute(value, axis, [(i, i ^ (1 << bit)) for i in range(lax.axis_size(axis))])


def bit_of(axis, bit):
    return (lax.axis_index(axis) >> bit) & 1


def bits_of(axis):
    return lax.axis_size(axis).bit_length() - 1


def add_up(*values):
    total = values[0].astype(F32)
    for value in values[1:]:
        total = total + value.astype(F32)
    return total.astype(BF16)


def reduce_half(value, axis, bit, dim):
    mine = bit_of(axis, bit)
    half = value.shape[dim] // 2
    kept = lax.dynamic_slice_in_dim(value, mine * half, half, dim)
    sent = lax.dynamic_slice_in_dim(value, (1 - mine) * half, half, dim)
    return add_up(kept, swap(sent, axis, bit))


def gather_pair(value, axis, bit, dim):
    mine = bit_of(axis, bit)
    other = swap(value, axis, bit)
    low = jnp.where(mine == 0, value, other)
    high = jnp.where(mine == 0, other, value)
    return jnp.stack((low, high), axis=dim)


def pin(*values):
    return lax.optimization_barrier(values)


def far_bits(sub):
    return [bit for bit in reversed(range(bits_of("tok"))) if (1 << bit) >= sub]


def per_device(
    tokens, mask, segments, replacement, w_qkv, w_out, w_in, w_down, ln_gain, ln_bias, cotangent
):
    tok_devices = lax.axis_size("tok")
    dp_devices = lax.axis_size("dp")
    seq_count, local_len, width = tokens.shape
    ff = w_down.shape[0]
    sub = tok_devices // seq_count
    per_group = HEADS // sub
    cols = per_group * HEAD_DIM
    tok_count = seq_count * local_len
    full_len = local_len * tok_devices
    tok_place = lax.axis_index("tok")
    group = tok_place % sub
    place_of = group.reshape(1)
    core = bit_of("dp", 0).reshape(1)
    side = bit_of("dp", bits_of("dp") - 1).reshape(1)
    near = [[j + sub * k for j in range(sub)] for k in range(seq_count)]
    apart = [[j + sub * k for k in range(seq_count)] for j in range(sub)]

    def regroup(value):
        place = tok_place // sub
        parts = [lax.dynamic_index_in_dim(value, place, 0, False)]
        for r in range(1, seq_count):
            part = lax.dynamic_index_in_dim(value, place ^ r, 0, False)
            to = [(i, i ^ (r * sub)) for i in range(tok_devices)]
            parts.append(lax.ppermute(part, "tok", to))
        if seq_count == 2:
            low = jnp.where(place == 0, parts[0], parts[1])
            return jnp.stack((low, jnp.where(place == 0, parts[1], parts[0])))
        return jnp.stack(parts)[jnp.arange(seq_count) ^ place]

    def spread(value):
        return lax.all_to_all(value, "tok", 0, 0, axis_index_groups=near)

    near_pairs = [[(i, i ^ r) for i in range(tok_devices)] for r in range(1, sub)]

    def deal(parts):
        return [
            parts[0],
            *(lax.ppermute(p, "tok", to) for p, to in zip(parts[1:], near_pairs)),
        ]

    extra = jnp.zeros((seq_count, local_len, LANES), BF16)
    code = (mask == 1).astype(jnp.int32) + 2 * segments
    extra = extra.at[:, :, 0].set(code.astype(BF16))
    mixed = regroup(jnp.concatenate((tokens, extra), axis=-1)).reshape(tok_count, -1)
    wq = split_layers_by_group(w_qkv, sub)
    wo = split_layers(w_out)
    mixed, wq, wo, w_in = pin(mixed, wq, wo, w_in)
    flags = mixed[:, width:]
    masked = flags[:, :1].astype(jnp.int32) % 2 == 1
    current = jnp.where(masked, replacement[None, :], mixed[:, :width].astype(F32))
    flat_in = current.astype(BF16)

    wi = split_layers(w_in)
    slopes = lax.dynamic_slice_in_dim(alibi_slopes(HEADS), group * per_group, per_group, 0)
    order = jnp.arange(sub, dtype=jnp.int32) ^ group
    place = (
        (jnp.arange(seq_count, dtype=jnp.int32)[None, :, None] * sub + order[:, None, None])
        * local_len
        + jnp.arange(local_len, dtype=jnp.int32)[None, None, :]
    ).reshape(full_len)
    far_dist = None
    stored = []
    for layer in range(LAYERS):
        sent = jnp.concatenate((flat_in, flags), axis=-1) if layer == 0 else flat_in
        parts = deal([sent] * sub)
        if layer == 0:
            *parts, wi, w_down = pin(*parts, wi, w_down)
            wd = split_layers(w_down)
            codes = jnp.concatenate([p[:, width] for p in parts]).astype(jnp.int32)
            labels = codes // 2
            masks = (codes % 2).astype(BF16).reshape(sub, 1, tok_count)
            masks = jnp.broadcast_to(masks, (sub, 16, tok_count))
            far_dist = jnp.where(
                labels[:, None] == labels[None, :],
                jnp.abs(place[:, None] - place[None, :]).astype(F32),
                FAR,
            )
        else:
            *parts, stored[0]["lhs_other"] = pin(*parts, stored[0]["lhs_other"])
        qkv = project(layer, place_of, parts, wq)
        *ctx_here, lse = attend_forward(qkv, far_dist, slopes, sub)
        ctx = deal(ctx_here)
        if layer == 0:
            *ctx, wd, cot = pin(*ctx, wd, regroup(cotangent))
        lhs, a, b, summed, z, current, flat_in = feed_forward(
            layer, place_of, current, ctx, wo, wi, wd, ln_gain, ln_bias
        )
        stored.append(
            {
                "attend": (parts, qkv, ctx_here, lse),
                "feed": (z, summed, a, b),
                "lhs": lhs,
                "lhs_other": swap(lhs, "dp", 0),
            }
        )
    layer_out = flat_in.reshape(seq_count, local_len, width)
    gradient = cot.reshape(tok_count, width).astype(F32)
    small = []
    row_out = width // tok_devices
    row_down = ff // tok_devices
    half = width // 2
    x_bits = list(reversed(range(1, bits_of("dp"))))
    far = dp_devices // 2

    def near_sum(parts):
        return add_up(*deal(parts))

    def x_sum(keep, send, parts):
        total = add_up(keep, swap(send, "dp", x_bits[0]))
        for bit in x_bits[1:]:
            at = bit_of("dp", bit)
            picked = []
            for choice in (at, 1 - at):
                begin, slices = 0, []
                for rows in parts:
                    slices.append(
                        lax.dynamic_slice_in_dim(
                            total, begin + choice * (rows // 2), rows // 2, 1
                        )
                    )
                    begin += rows
                picked.append(jnp.concatenate(slices, axis=1))
            total = add_up(picked[0], swap(picked[1], "dp", bit))
            parts = [rows // 2 for rows in parts]
        return total

    def x_sum_down(keep, send):
        return x_sum(keep, send, [row_down // 2, row_out // 2])

    def x_sum_in(keep, send):
        shape = (tok_devices, -1, PACK)
        return x_sum(keep.reshape(shape), send.reshape(shape), [far // 2 * row_out])

    def x_sum_columns(value):
        for bit in x_bits:
            value = reduce_half(value, "dp", bit, value.ndim - 1)
        return value

    def far_sum(value):
        for bit in far_bits(sub):
            value = reduce_half(value, "tok", bit, 0)
        return value[0]

    def by_place(value):
        return value.reshape(seq_count, sub, *value.shape[1:]).swapaxes(0, 1)

    def spread_sum(value):
        return add_up(*spread(by_place(value)))

    def deal_sum(value):
        value = by_place(value)
        return near_sum(
            [lax.dynamic_index_in_dim(value, group ^ r, 0, False) for r in range(sub)]
        )

    def dp_sum(value):
        return add_up(*lax.all_to_all(value, "dp", 0, 0))

    def by_head(value):
        few = row_out // dp_devices
        value = spread(by_place(value))
        extra = jnp.sum(value[:, :, few : few + 8, :PACK].astype(F32), axis=0).astype(BF16)
        value = jnp.concatenate((value[:, :, :few], value[:, :, few + 8 :]), axis=2)
        value = value.reshape(sub, seq_count, -1, 3, cols)
        return extra, value.transpose(1, 2, 3, 0, 4).reshape(seq_count, -1, 3 * width)

    before = None
    for layer in reversed(range(LAYERS)):
        parts, qkv, ctx_here, lse = stored[layer]["attend"]
        z, summed, a, b = stored[layer]["feed"]
        lhs, lhs_other = stored[layer]["lhs"], stored[layer]["lhs_other"]
        fed = feed_backward(
            layer, core, place_of, gradient, z, summed, a, b, wo, wi, wd, ln_gain, sub
        )
        if before is None:
            *fed, lhs_other, layer_out = pin(*fed, lhs_other, regroup(layer_out))
        else:
            send = fed[1]
            *fed, late, down = pin(
                *fed, near_sum(before["late"]), x_sum_down(*before["down"])
            )
            fed[1] = send
            first = jnp.concatenate((before["early"], late), axis=2)
            last = jnp.concatenate((down, before["last"]), axis=1)
        mine, send, ga, small_part, *gctx = fed
        small.insert(0, small_part)
        other = swap(send, "dp", 0)
        ctx_grad = deal(gctx)
        if before is not None:
            other, first, last = pin(other, first, last)
        *g_first, keep, sent, keep_in, sent_in = pair_grads(
            place_of, side, lhs, lhs_other, mine, other, ff, tok_devices, sub, far, before is None
        )
        done = (*ctx_grad, keep, sent, keep_in, sent_in, *g_first)
        if before is not None:
            done += (x_sum_columns(first), spread_sum(last))
        done = pin(*done)
        ctx_grad, (keep, sent, keep_in, sent_in) = done[:sub], done[sub : sub + 4]
        done = done[sub + 4 :]
        head_grad = attend_backward(qkv, ctx_here, ctx_grad, lse, far_dist, slopes)
        if before is None:
            both = pin(
                *head_grad, near_sum(done[:sub]), x_sum_in(keep_in, sent_in), keep, sent, *done[sub:]
            )
            head_grad, (early, last, keep, sent, *late) = both[:sub], both[sub:]
            g_qkv = dp_sum(qkv_grad(parts, head_grad, width, tok_devices, dp_devices))
            both = pin(*deal(head_grad), g_qkv, keep, sent, *late)
            back, (g_qkv, keep, sent, *late) = both[:sub], both[sub:]
            before = {
                "early": early,
                "late": late,
                "last": last,
                "down": (keep, sent),
                "qkv": g_qkv,
            }
        else:
            g_first, (first, last) = done[:sub], done[sub:]
            g_qkv = last_grads(
                place_of, jnp.concatenate(small, axis=0), masks, parts, head_grad, ga, wq,
                tok_devices, dp_devices,
            )
            both = pin(
                *head_grad,
                g_qkv,
                near_sum(g_first),
                x_sum_in(keep_in, sent_in),
                x_sum_down(keep, sent),
                pack_columns(first, last),
            )
            head_grad, (g_qkv, g_first, g_last, g_down, before_all) = both[:sub], both[sub:]
            g_last = deal_sum(jnp.concatenate((g_down, g_last), axis=1))
            g_qkv = jnp.concatenate((dp_sum(g_qkv), before["qkv"]), axis=1)
            both = pin(
                *head_grad,
                *by_head(g_qkv),
                far_sum(pack_columns(x_sum_columns(g_first))),
                g_last,
                lax.psum_scatter(
                    before_all, "tok", scatter_dimension=0, axis_index_groups=apart
                ),
            )
            head_grad, (*g_qkv, g_first, g_last, before_all) = both[:sub], both[sub:]
            back = deal(head_grad)
            packed = [
                g_first,
                far_sum(pack_columns(g_last, *g_qkv)),
                lax.all_gather(before_all, "dp"),
            ]
        gradient = input_grad(layer, place_of, ga, back, wq)
    packed[0] = packed[0][None]
    for bit in x_bits:
        packed[0] = gather_pair(packed[0], "dp", bit, 1)
        packed[0] = packed[0].reshape(-1, *packed[0].shape[2:])
    gradient, *packed = pin(gradient, *packed)
    grad_tokens = jnp.where(masked, 0.0, gradient).astype(BF16)
    grad_tokens = regroup(grad_tokens.reshape(seq_count, local_len, width))
    value = packed[1][None]
    for bit in x_bits:
        value = gather_pair(value, "dp", bit, 1)
        value = value.reshape(-1, *value.shape[2:])
    value, packed[0], grad_tokens = pin(value, gather_pair(packed[0], "dp", 0, 1), grad_tokens)
    grad_tokens = grad_tokens.astype(F32)
    packed[1] = gather_pair(value, "dp", 0, 1)
    packed[:2] = [v.reshape(dp_devices, *v.shape[2:]) for v in packed[:2]]
    begin = (row_down + row_out) // far + row_out
    few = row_out // dp_devices
    small = packed[1][:, begin : begin + 8].astype(F32)
    small = jnp.concatenate((small[:, :, :few], small[:, :1, LANES : LANES + few]), axis=1)
    small = small.transpose(1, 0, 2).reshape(-1, row_out)
    by_layer = small[: 4 * LAYERS].reshape(LAYERS, 2, 2, row_out)
    return (
        layer_out,
        grad_tokens,
        small[-1],
        *assemble(packed, width, ff, tok_devices, dp_devices),
        by_layer[:, 0],
        by_layer[:, 1],
    )


def solution(mesh):
    in_specs = (
        P("dp", "tok", None),
        P("dp", "tok"),
        P("dp", "tok"),
        P(),
        P(),
        P(),
        P(),
        P(),
        P(),
        P(),
        P("dp", "tok", None),
    )
    out_specs = (
        P("dp", "tok", None),
        P("dp", "tok", None),
        P("tok"),
        P("tok", None, None),
        P("tok", None, None),
        P("tok", None, None),
        P("tok", None, None),
        P(None, None, "tok"),
        P(None, None, "tok"),
    )
    return jax.shard_map(
        per_device, mesh=mesh, in_specs=in_specs, out_specs=out_specs, check_vma=False
    )
```

```python
import functools
import math

import jax
import jax.numpy as jnp
from jax import lax
from jax.experimental import pallas as pl
from jax.experimental.pallas import tpu as pltpu
from jax.sharding import PartitionSpec as P

HEADS = 12
HEAD_DIM = 64
LAYERS = 2
LANES = 128
PACK = 384
SCALE = 1.0 / math.sqrt(HEAD_DIM)
FAR = 1e30
BF16 = jnp.bfloat16
F32 = jnp.float32
VMEM_LIMIT = 56 << 20
COST_TIMES = 4


def alibi_slopes(head_count):
    head_index = jnp.arange(head_count, dtype=jnp.float32)
    return jnp.exp2(jnp.where(head_index < 8.0, -(head_index + 1.0), 7.5 - head_index))


def dot(a, b, dims):
    return lax.dot_general(a, b, (dims, ((), ())), preferred_element_type=F32)


def cost(flops, bytes_accessed, transcendentals):
    return pl.CostEstimate(
        flops=COST_TIMES * flops,
        bytes_accessed=bytes_accessed,
        transcendentals=transcendentals,
    )


NN = ((1,), (0,))
NT = ((1,), (1,))
TN = ((0,), (0,))


def split_layers(weight):
    rows, _, cols = weight.shape
    row_block = 256
    col_block = next(c for c in (3072, 2304, 1152, 768) if cols % c == 0)

    def body(in_ref, out_ref):
        to_row = lax.broadcasted_iota(jnp.int32, (256, 256), 0)
        from_row = lax.broadcasted_iota(jnp.int32, (256, 256), 1)
        wanted = jnp.where(to_row < 128, 2 * to_row, 2 * to_row - 255)
        pick = jnp.where(from_row == wanted, 1.0, 0.0).astype(BF16)
        for part in range(row_block // 128):
            at = slice(part * 128, part * 128 + 128)
            mixed = in_ref[at].reshape(256, col_block)
            picked = dot(pick, mixed, NN).astype(BF16)
            out_ref[0, at] = picked[:128]
            out_ref[1, at] = picked[128:]

    return pl.pallas_call(
        body,
        grid=(rows // row_block, cols // col_block),
        in_specs=[pl.BlockSpec((row_block, 2, col_block), lambda i, j: (i, 0, j))],
        out_specs=pl.BlockSpec((2, row_block, col_block), lambda i, j: (0, i, j)),
        out_shape=jax.ShapeDtypeStruct((2, rows, cols), BF16),
        compiler_params=pltpu.CompilerParams(vmem_limit_bytes=VMEM_LIMIT),
        cost_estimate=cost(
            flops=2 * 512 * rows * cols, bytes_accessed=8 * rows * cols, transcendentals=0
        ),
        name="split_layers",
    )(weight)


def split_layers_by_group(weight, sub):
    rows, _, cols = weight.shape
    row_block = 256
    group_cols = cols // sub // 3

    def body(in_ref, out_ref):
        to_row = lax.broadcasted_iota(jnp.int32, (256, 256), 0)
        from_row = lax.broadcasted_iota(jnp.int32, (256, 256), 1)
        wanted = jnp.where(to_row < 128, 2 * to_row, 2 * to_row - 255)
        pick = jnp.where(from_row == wanted, 1.0, 0.0).astype(BF16)
        for part in range(row_block // 128):
            at = slice(part * 128, part * 128 + 128)
            picked = dot(pick, in_ref[at].reshape(256, cols), NN).astype(BF16)
            for j in range(sub):
                for n in range(3):
                    first = (n * sub + j) * group_cols
                    block = picked[:, first : first + group_cols]
                    to = slice(n * group_cols, n * group_cols + group_cols)
                    out_ref[0, j, at, to] = block[:128]
                    out_ref[1, j, at, to] = block[128:]

    return pl.pallas_call(
        body,
        grid=(rows // row_block,),
        in_specs=[pl.BlockSpec((row_block, 2, cols), lambda i: (i, 0, 0))],
        out_specs=pl.BlockSpec((2, sub, row_block, 3 * group_cols), lambda i: (0, 0, i, 0)),
        out_shape=jax.ShapeDtypeStruct((2, sub, rows, 3 * group_cols), BF16),
        compiler_params=pltpu.CompilerParams(vmem_limit_bytes=VMEM_LIMIT),
        cost_estimate=cost(
            flops=2 * 512 * rows * cols, bytes_accessed=8 * rows * cols, transcendentals=0
        ),
        name="split_qkv",
    )(weight)


def norm_parts(value):
    center = jnp.mean(value, axis=-1, keepdims=True)
    shifted = value - center
    inverse = lax.rsqrt(jnp.mean(shifted * shifted, axis=-1, keepdims=True) + 1e-12)
    return shifted * inverse, inverse


def norm_grad(grad, value, gain):
    normed, inverse = norm_parts(value)
    scaled = grad * gain
    one = jnp.mean(scaled, axis=-1, keepdims=True)
    two = jnp.mean(scaled * normed, axis=-1, keepdims=True)
    in_grad = inverse * (scaled - one - normed * two)
    gain_grad = jnp.sum(grad * normed, axis=0, keepdims=True)
    bias_grad = jnp.sum(grad, axis=0, keepdims=True)
    return in_grad, gain_grad, bias_grad


def feed_forward(layer, group, current, ctx, w_out, w_in, w_down, gain, bias):
    count, width = current.shape
    sub, cols = len(ctx), ctx[0].shape[0]
    ff = w_down.shape[1]
    chunk = 768
    steps = ff // chunk

    def body(group_ref, *refs):
        ctx_refs = refs[:sub]
        cur_ref, wo_ref, wg_ref, wu_ref, wd_ref, gain_ref, bias_ref = refs[sub : sub + 7]
        lhs_ref, a_ref, b_ref, sum_ref, z_ref, next_ref, low_ref = refs[sub + 7 : sub + 14]
        y1l_ref, acc_ref, held_ref = refs[sub + 14 :]
        step = pl.program_id(0)

        @pl.when(step == 0)
        def _():
            branch = jnp.zeros((count, width), F32)
            for r in range(sub):
                held_ref[jnp.bitwise_xor(group_ref[0], r)] = ctx_refs[r][...]
            for j in range(sub):
                part = held_ref[j]
                to = slice(j * cols, j * cols + cols)
                lhs_ref[:, width + ff + j * cols : width + ff + j * cols + cols] = (
                    part.astype(F32).T.astype(BF16)
                )
                branch += dot(part, wo_ref[0, to, :], TN)
            summed = cur_ref[...] + branch
            sum_ref[...] = summed
            normed, _ = norm_parts(summed)
            y1 = normed * gain_ref[layer, 0:1, :] + bias_ref[layer, 0:1, :]
            acc_ref[...] = y1
            y1l_ref[...] = y1.astype(BF16)
            lhs_ref[:, :width] = y1.astype(BF16)

        y1l = y1l_ref[...]
        gate = dot(y1l, wg_ref[0], NN)
        up = dot(y1l, wu_ref[0], NN)
        cdf = 0.5 * (1.0 + lax.erf(gate * (0.5**0.5)))
        density = jnp.exp(-0.5 * gate * gate) * (1.0 / math.sqrt(2.0 * math.pi))
        gelu = gate * cdf
        hidden = (gelu * up).astype(BF16)
        a_ref[...] = gelu.astype(BF16)
        b_ref[...] = (up * (cdf + gate * density)).astype(BF16)
        lhs_ref[:, pl.ds(pl.multiple_of(width + step * chunk, 128), chunk)] = hidden
        acc_ref[...] += dot(hidden, wd_ref[0], NN)

        @pl.when(step == steps - 1)
        def _():
            z = acc_ref[...]
            z_ref[...] = z
            normed, _ = norm_parts(z)
            out = normed * gain_ref[layer, 1:2, :] + bias_ref[layer, 1:2, :]
            next_ref[...] = out
            low_ref[...] = out.astype(BF16)

    whole = lambda *shape: pl.BlockSpec(shape, lambda i: (0,) * len(shape))
    return pl.pallas_call(
        body,
        grid=(steps,),
        in_specs=[
            pl.BlockSpec(memory_space=pltpu.SMEM),
            *[whole(cols, count)] * sub,
            whole(count, width),
            pl.BlockSpec((1, width, width), lambda i: (layer, 0, 0)),
            pl.BlockSpec((1, width, chunk), lambda i: (layer, 0, i)),
            pl.BlockSpec((1, width, chunk), lambda i: (layer, 0, steps + i)),
            pl.BlockSpec((1, chunk, width), lambda i: (layer, i, 0)),
            whole(*gain.shape),
            whole(*bias.shape),
        ],
        out_specs=[
            whole(count, ff + 2 * width),
            pl.BlockSpec((count, chunk), lambda i: (0, i)),
            pl.BlockSpec((count, chunk), lambda i: (0, i)),
            whole(count, width),
            whole(count, width),
            whole(count, width),
            whole(count, width),
        ],
        out_shape=[
            jax.ShapeDtypeStruct((count, ff + 2 * width), BF16),
            jax.ShapeDtypeStruct((count, ff), BF16),
            jax.ShapeDtypeStruct((count, ff), BF16),
            jax.ShapeDtypeStruct((count, width), F32),
            jax.ShapeDtypeStruct((count, width), F32),
            jax.ShapeDtypeStruct((count, width), F32),
            jax.ShapeDtypeStruct((count, width), BF16),
        ],
        scratch_shapes=[
            pltpu.VMEM((count, width), BF16),
            pltpu.VMEM((count, width), F32),
            pltpu.VMEM((sub, cols, count), BF16),
        ],
        compiler_params=pltpu.CompilerParams(vmem_limit_bytes=VMEM_LIMIT),
        cost_estimate=cost(
            flops=2 * count * width * (width + 3 * ff),
            bytes_accessed=6 * width * ff + 2 * width * width + count * (20 * width + 6 * ff),
            transcendentals=2 * count * ff,
        ),
        name="feed_forward",
    )(group, *ctx, current, w_out, w_in, w_in, w_down, gain, bias)


def feed_backward(layer, core, group, grad, z, summed, a, b, w_out, w_in, w_down, gain, sub):
    count, width = grad.shape
    ff = w_down.shape[1]
    cols = width // sub
    half = width // 2
    chunk = 768
    steps = ff // chunk

    def body(
        core_ref, group_ref, grad_ref, z_ref, sum_ref, a_ref, b_ref,
        wo_ref, wg_ref, wu_ref, wd_ref, gain_ref, mine_ref, send_ref, ga_ref, small_ref, *refs,
    ):
        gctx_refs = refs[:sub]
        gzl_ref, acc_ref, held_ref = refs[sub:]
        step = pl.program_id(0)
        first = core_ref[0] == 0

        def store(to, low, high):
            mine_ref[:, to] = jnp.where(first, low, high)
            send_ref[:, to] = jnp.where(first, high, low)

        @pl.when(step == 0)
        def _():
            gz, gain_grad, bias_grad = norm_grad(grad_ref[...], z_ref[...], gain_ref[layer, 1:2, :])
            small_ref[1:2, :] = gain_grad
            small_ref[3:4, :] = bias_grad
            acc_ref[...] = gz
            gzl = gz.astype(BF16)
            gzl_ref[...] = gzl
            store(slice(ff, ff + half), gz[:, :half].astype(BF16), gz[:, half:].astype(BF16))

        gzl = gzl_ref[...]
        ghid = dot(gzl, wd_ref[0], NT)
        ggate = (ghid * b_ref[...].astype(F32)).astype(BF16)
        gup = (ghid * a_ref[...].astype(F32)).astype(BF16)
        store(pl.ds(pl.multiple_of(step * chunk, 128), chunk), ggate, gup)
        acc_ref[...] += dot(ggate, wg_ref[0], NT) + dot(gup, wu_ref[0], NT)

        @pl.when(step == steps - 1)
        def _():
            ga, gain_grad, bias_grad = norm_grad(
                acc_ref[...], sum_ref[...], gain_ref[layer, 0:1, :]
            )
            small_ref[0:1, :] = gain_grad
            small_ref[2:3, :] = bias_grad
            ga_ref[...] = ga
            gal = ga.astype(BF16)
            store(slice(ff + half, ff + width), gal[:, :half], gal[:, half:])
            for j in range(sub):
                to = slice(j * cols, j * cols + cols)
                held_ref[j] = dot(wo_ref[0, to, :], gal, NT).astype(BF16)
            for r in range(sub):
                gctx_refs[r][...] = held_ref[jnp.bitwise_xor(group_ref[0], r)]

    whole = lambda *shape: pl.BlockSpec(shape, lambda i: (0,) * len(shape))
    return pl.pallas_call(
        body,
        grid=(steps,),
        in_specs=[
            pl.BlockSpec(memory_space=pltpu.SMEM),
            pl.BlockSpec(memory_space=pltpu.SMEM),
            whole(count, width),
            whole(count, width),
            whole(count, width),
            pl.BlockSpec((count, chunk), lambda i: (0, i)),
            pl.BlockSpec((count, chunk), lambda i: (0, i)),
            pl.BlockSpec((1, width, width), lambda i: (layer, 0, 0)),
            pl.BlockSpec((1, width, chunk), lambda i: (layer, 0, i)),
            pl.BlockSpec((1, width, chunk), lambda i: (layer, 0, steps + i)),
            pl.BlockSpec((1, chunk, width), lambda i: (layer, i, 0)),
            whole(*gain.shape),
        ],
        out_specs=[
            whole(count, ff + width),
            whole(count, ff + width),
            whole(count, width),
            whole(4, width),
            *[whole(cols, count)] * sub,
        ],
        out_shape=[
            jax.ShapeDtypeStruct((count, ff + width), BF16),
            jax.ShapeDtypeStruct((count, ff + width), BF16),
            jax.ShapeDtypeStruct((count, width), F32),
            jax.ShapeDtypeStruct((4, width), F32),
            *[jax.ShapeDtypeStruct((cols, count), BF16)] * sub,
        ],
        scratch_shapes=[
            pltpu.VMEM((count, width), BF16),
            pltpu.VMEM((count, width), F32),
            pltpu.VMEM((sub, cols, count), BF16),
        ],
        compiler_params=pltpu.CompilerParams(vmem_limit_bytes=VMEM_LIMIT),
        cost_estimate=cost(
            flops=2 * count * width * (width + 3 * ff),
            bytes_accessed=6 * width * ff + 2 * width * width + count * (24 * width + 8 * ff),
            transcendentals=0,
        ),
        name="feed_backward",
    )(core, group, grad, z, summed, a, b, w_out, w_in, w_in, w_down, gain)


def pair_grads(group, side, lhs, lhs_other, rhs, rhs_other, ff, tok_devices, sub, far, early):
    count = lhs.shape[0]
    width = rhs.shape[1] - ff
    half = width // 2
    rows, rows_down = width // tok_devices, ff // tok_devices
    seqs = tok_devices // sub
    chunk = 2 * PACK
    steps_in, steps_down = ff // chunk, ff // chunk
    first_steps = steps_in - far * PACK // chunk
    ends = [0, 1, first_steps] if early else [0, first_steps]
    spans = list(zip(ends[:-1], ends[1:]))
    split = far // 2
    half_down, half_out = rows_down // 2, rows // 2

    def body(group_ref, side_ref, l1_ref, l2_ref, r1_ref, r2_ref, h1_ref, h2_ref, *refs):
        out_refs = refs[: len(spans) * sub]
        keep_ref, send_ref, keep_in_ref, send_in_ref, held_ref = refs[len(spans) * sub :]
        step = pl.program_id(0)
        low_side = side_ref[0] == 0

        def store(t, at, low, high):
            keep_ref[t, at] = jnp.where(low_side, low, high).astype(BF16)
            send_ref[t, at] = jnp.where(low_side, high, low).astype(BF16)

        @pl.when(step < steps_in)
        def _():
            out = dot(l1_ref[...], r1_ref[...], TN) + dot(l2_ref[...], r2_ref[...], TN)

            @pl.when(step < first_steps)
            def _():
                for t in range(tok_devices):
                    held_ref[t % sub, t // sub] = out[t * rows : t * rows + rows].astype(BF16)

            for n, (begin, end) in enumerate(spans):

                @pl.when((step >= begin) & (step < end))
                def _():
                    for r in range(sub):
                        out_refs[n * sub + r][...] = held_ref[jnp.bitwise_xor(group_ref[0], r)]

            for f in range(2):
                block = 2 * (step - first_steps) + f
                here = block // split == side_ref[0]
                to = block % split
                for wanted, ref in ((here, keep_in_ref), (jnp.logical_not(here), send_in_ref)):

                    @pl.when((step >= first_steps) & wanted)
                    def _():
                        for t in range(tok_devices):
                            part = out[t * rows : t * rows + rows, f * PACK : f * PACK + PACK]
                            ref[t, to] = part.astype(BF16)

        @pl.when(step >= steps_in)
        def _():
            out = dot(l1_ref[...], h1_ref[...], TN) + dot(l2_ref[...], h2_ref[...], TN)
            each = chunk // rows_down

            @pl.when(step < steps_in + steps_down)
            def _():
                for i in range(each):
                    low = out[i * rows_down : i * rows_down + half_down]
                    high = out[i * rows_down + half_down : (i + 1) * rows_down]
                    store((step - steps_in) * each + i, slice(0, half_down), low, high)

            @pl.when(step == steps_in + steps_down)
            def _():
                for t in range(tok_devices):
                    low = out[t * rows : t * rows + half_out]
                    high = out[t * rows + half_out : (t + 1) * rows]
                    store(t, slice(half_down, half_down + half_out), low, high)

    left = pl.BlockSpec((count, chunk), lambda i: (0, jnp.maximum(i - steps_in + 1, 0)))
    right = pl.BlockSpec((count, chunk), lambda i: (0, jnp.minimum(i, steps_in - 1)))
    halves = pl.BlockSpec(
        (count, half), lambda i: (0, ff // half + jnp.where(i < steps_in + steps_down, 0, 1))
    )
    kept = (tok_devices, half_down + half_out, half)
    kept_in = (tok_devices, split, rows, PACK)
    whole = lambda *shape: pl.BlockSpec(shape, lambda i: (0,) * len(shape))
    return pl.pallas_call(
        body,
        grid=(steps_in + steps_down + 1,),
        in_specs=[
            pl.BlockSpec(memory_space=pltpu.SMEM),
            pl.BlockSpec(memory_space=pltpu.SMEM),
            left,
            left,
            right,
            right,
            halves,
            halves,
        ],
        out_specs=[
            *[
                pl.BlockSpec(
                    (seqs, rows, chunk),
                    functools.partial(
                        lambda begin, end, i: (0, 0, jnp.clip(i - begin, 0, end - begin - 1)),
                        begin,
                        end,
                    ),
                )
                for begin, end in spans
                for _ in range(sub)
            ],
            whole(*kept),
            whole(*kept),
            whole(*kept_in),
            whole(*kept_in),
        ],
        out_shape=[
            *[
                jax.ShapeDtypeStruct((seqs, rows, (end - begin) * chunk), BF16)
                for begin, end in spans
                for _ in range(sub)
            ],
            jax.ShapeDtypeStruct(kept, BF16),
            jax.ShapeDtypeStruct(kept, BF16),
            jax.ShapeDtypeStruct(kept_in, BF16),
            jax.ShapeDtypeStruct(kept_in, BF16),
        ],
        scratch_shapes=[pltpu.VMEM((sub, seqs, rows, chunk), BF16)],
        compiler_params=pltpu.CompilerParams(vmem_limit_bytes=VMEM_LIMIT),
        cost_estimate=cost(
            flops=8 * count * width * ff,
            bytes_accessed=4 * width * ff + 8 * count * (width + ff),
            transcendentals=0,
        ),
        name="pair_grads",
    )(group, side, lhs, lhs_other, rhs, rhs_other, rhs, rhs_other)


def input_grad(layer, group, ga, back, w_qkv):
    sub = len(back)
    cols, count = back[0].shape
    width = ga.shape[1]

    def body(group_ref, ga_ref, w_ref, *refs):
        back_refs, out_ref, acc_ref = refs[:sub], refs[sub], refs[sub + 1]
        step = pl.program_id(0)

        @pl.when(step == 0)
        def _():
            acc_ref[...] = jnp.zeros_like(acc_ref)

        for r in range(sub):

            @pl.when(step == r)
            def _():
                acc_ref[...] += dot(w_ref[0, 0], back_refs[r][...], NN)

        @pl.when(step == sub - 1)
        def _():
            out_ref[...] = ga_ref[...] + acc_ref[...].T

    return pl.pallas_call(
        body,
        grid_spec=pltpu.PrefetchScalarGridSpec(
            num_scalar_prefetch=1,
            grid=(sub,),
            in_specs=[
                pl.BlockSpec((count, width), lambda i, g: (0, 0)),
                pl.BlockSpec(
                    (1, 1, width, cols), lambda i, g: (layer, jnp.bitwise_xor(g[0], i), 0, 0)
                ),
                *[pl.BlockSpec((cols, count), lambda i, g: (0, 0))] * sub,
            ],
            out_specs=pl.BlockSpec((count, width), lambda i, g: (0, 0)),
            scratch_shapes=[pltpu.VMEM((width, count), F32)],
        ),
        out_shape=jax.ShapeDtypeStruct((count, width), F32),
        compiler_params=pltpu.CompilerParams(vmem_limit_bytes=VMEM_LIMIT),
        cost_estimate=cost(
            flops=2 * count * width * cols * sub,
            bytes_accessed=2 * sub * cols * (width + count) + 8 * count * width,
            transcendentals=0,
        ),
        name="input_grad",
    )(group, ga, w_qkv, *back)


def project(layer, group, parts, w_qkv):
    sub = len(parts)
    count = parts[0].shape[0]
    width, cols = w_qkv.shape[2:]

    def body(group_ref, w_ref, *refs):
        out_ref = refs[sub]
        for r in range(sub):
            out_ref[r * count : r * count + count, :] = dot(
                refs[r][...], w_ref[0, 0], NN
            ).astype(BF16)

    return pl.pallas_call(
        body,
        grid_spec=pltpu.PrefetchScalarGridSpec(
            num_scalar_prefetch=1,
            grid=(1,),
            in_specs=[
                pl.BlockSpec((1, 1, width, cols), lambda i, g: (layer, g[0], 0, 0)),
                *[pl.BlockSpec((count, width), lambda i, g: (0, 0))] * sub,
            ],
            out_specs=pl.BlockSpec((sub * count, cols), lambda i, g: (0, 0)),
        ),
        out_shape=jax.ShapeDtypeStruct((sub * count, cols), BF16),
        compiler_params=pltpu.CompilerParams(vmem_limit_bytes=VMEM_LIMIT),
        cost_estimate=cost(
            flops=2 * sub * count * width * cols,
            bytes_accessed=2 * (width * cols + sub * count * (width + cols)),
            transcendentals=0,
        ),
        name="project",
    )(group, w_qkv, *parts)


def qkv_grad(parts, grads, width, tok_devices, dp_devices):
    sub = len(parts)
    count = parts[0].shape[0]
    cols = grads[0].shape[0]
    rows = width // tok_devices
    few = rows // dp_devices

    def body(*refs):
        qkv_grad_body(refs[:sub], refs[sub : 2 * sub], refs[2 * sub], rows, few)

    shape = (dp_devices, tok_devices, few, cols)
    return pl.pallas_call(
        body,
        grid=(1,),
        in_specs=[
            *[pl.BlockSpec((count, width), lambda i: (0, 0))] * sub,
            *[pl.BlockSpec((cols, count), lambda i: (0, 0))] * sub,
        ],
        out_specs=pl.BlockSpec(shape, lambda i: (0, 0, 0, 0)),
        out_shape=jax.ShapeDtypeStruct(shape, BF16),
        compiler_params=pltpu.CompilerParams(vmem_limit_bytes=VMEM_LIMIT),
        cost_estimate=pl.CostEstimate(flops=1 << 20, bytes_accessed=1 << 10, transcendentals=0),
        name="qkv_grad",
    )(*parts, *grads)


def qkv_grad_body(part_refs, grad_refs, out_ref, rows, few):
    cols, width = grad_refs[0].shape[0], part_refs[0].shape[1]
    acc = jnp.zeros((cols, width), F32)
    for part_ref, grad_ref in zip(part_refs, grad_refs):
        acc += dot(grad_ref[...], part_ref[...], NN)
    acc = acc.T
    dp_devices, tok_devices = out_ref.shape[:2]
    for t in range(tok_devices):
        for q in range(dp_devices):
            first = t * rows + q * few
            out_ref[q, t, :few, :] = acc[first : first + few].astype(BF16)


def last_grads(group, small, masks, parts, grads, ga, w_qkv, tok_devices, dp_devices):
    sub = len(grads)
    cols, count = grads[0].shape
    width = ga.shape[1]
    rows = width // tok_devices
    few = rows // dp_devices

    def twice(value):
        high = value.astype(BF16)
        return high, (value - high.astype(F32)).astype(BF16)

    def body(group_ref, mask_ref, ga_ref, w_ref, *refs):
        small_refs, refs = refs[:LAYERS], refs[LAYERS:]
        part_refs, grad_refs, out_ref = refs[:sub], refs[sub : 2 * sub], refs[2 * sub]
        qkv_grad_body(part_refs, grad_refs, out_ref, rows, few)
        total = jnp.zeros((16, cols), F32)
        for r in range(sub):
            total += dot(mask_ref[r], grad_refs[r][...], NT)
        mask_sum = jnp.zeros((16, width), F32)
        for part in twice(total):
            mask_sum += dot(part, w_ref[0, 0], NT)
        for part in twice(ga_ref[...]):
            mask_sum += dot(mask_ref[0], part, NN)
        values = jnp.concatenate([ref[...] for ref in small_refs], axis=0)
        for t in range(tok_devices):
            for q in range(dp_devices):
                of = slice(t * rows + q * few, t * rows + q * few + few)
                row = jnp.concatenate(
                    (
                        jnp.pad(values[:, of], ((0, 0), (0, LANES - few))),
                        jnp.pad(mask_sum[:8, of], ((0, 0), (0, cols - LANES - few))),
                    ),
                    axis=1,
                )
                out_ref[q, t, few:, :] = row.astype(BF16)

    whole = lambda *shape: pl.BlockSpec(shape, lambda i, g: (0,) * len(shape))
    shape = (dp_devices, tok_devices, few + 8, cols)
    return pl.pallas_call(
        body,
        grid_spec=pltpu.PrefetchScalarGridSpec(
            num_scalar_prefetch=1,
            grid=(1,),
            in_specs=[
                whole(sub, 16, count),
                whole(count, width),
                pl.BlockSpec((1, 1, width, cols), lambda i, g: (0, g[0], 0, 0)),
                *[whole(8 // LAYERS, width)] * LAYERS,
                *[whole(count, width)] * sub,
                *[whole(cols, count)] * sub,
            ],
            out_specs=whole(*shape),
        ),
        out_shape=jax.ShapeDtypeStruct(shape, BF16),
        compiler_params=pltpu.CompilerParams(vmem_limit_bytes=VMEM_LIMIT),
        cost_estimate=pl.CostEstimate(flops=1 << 20, bytes_accessed=1 << 10, transcendentals=0),
        name="last_grads",
    )(group, masks, ga, w_qkv, *small, *parts, *grads)


def attend_forward(qkv, far_dist, slopes, sub):
    length, width = qkv.shape
    cols = width // 3
    heads = cols // HEAD_DIM
    count = length // sub
    block = 256
    per = count // block

    def body(slope_ref, qkv_ref, dist_ref, *refs):
        ctx_refs, lse_ref, held_ref = refs[:sub], refs[sub], refs[sub + 1]
        step = pl.program_id(0)
        at = pl.ds(pl.multiple_of(step * block, block), block)
        dist = dist_ref[...]
        for h in range(heads):
            q = qkv_ref[at, h * 64 : h * 64 + 64]
            k = qkv_ref[:, cols + h * 64 : cols + h * 64 + 64]
            v = qkv_ref[:, 2 * cols + h * 64 : 2 * cols + h * 64 + 64]
            s = dot(k, q, NT) * SCALE - dist * slope_ref[h]
            top = jnp.max(s, axis=0, keepdims=True)
            e = jnp.exp(s - top)
            total = jnp.sum(e, axis=0, keepdims=True)
            ctx = dot(v, e.astype(BF16), TN) / total
            held_ref[h * 64 : h * 64 + 64, :] = ctx.astype(BF16)
            lse_ref[h : h + 1, :] = top + jnp.log(total)
        for i in range(length // block):

            @pl.when(step == i)
            def _():
                first = i % per * block
                ctx_refs[i // per][:, first : first + block] = held_ref[...]

    return pl.pallas_call(
        body,
        grid=(length // block,),
        in_specs=[
            pl.BlockSpec(memory_space=pltpu.SMEM),
            pl.BlockSpec((length, width), lambda i: (0, 0)),
            pl.BlockSpec((length, block), lambda i: (0, i)),
        ],
        out_specs=[
            *[pl.BlockSpec((cols, count), lambda i: (0, 0))] * sub,
            pl.BlockSpec((heads, block), lambda i: (0, i)),
        ],
        out_shape=[
            *[jax.ShapeDtypeStruct((cols, count), BF16)] * sub,
            jax.ShapeDtypeStruct((heads, length), F32),
        ],
        scratch_shapes=[pltpu.VMEM((cols, block), BF16)],
        compiler_params=pltpu.CompilerParams(vmem_limit_bytes=VMEM_LIMIT),
        cost_estimate=cost(
            flops=16 * heads * length * length * HEAD_DIM,
            bytes_accessed=4 * length * length,
            transcendentals=heads * length * length,
        ),
        name="attend_forward",
    )(slopes, qkv, far_dist)


def attend_backward(qkv, ctx, ctx_grad, lse, far_dist, slopes):
    length, width = qkv.shape
    sub = len(ctx)
    cols = width // 3
    heads = cols // HEAD_DIM
    count = length // sub
    block = 256
    per = count // block

    def body(slope_ref, qkv_ref, lse_ref, dist_ref, *refs):
        ctx_refs, g_refs, out_refs = refs[:sub], refs[sub : 2 * sub], refs[2 * sub : 3 * sub]
        dk_ref, dv_ref, dq_ref, held_ref, inner_ref = refs[3 * sub :]
        step = pl.program_id(0)
        at = pl.ds(pl.multiple_of(step * block, block), block)

        @pl.when(step == 0)
        def _():
            dk_ref[...] = jnp.zeros_like(dk_ref)
            dv_ref[...] = jnp.zeros_like(dv_ref)
            for r in range(sub):
                g = g_refs[r][...]
                both = g.astype(F32) * ctx_refs[r][...].astype(F32)
                for p in range(per):
                    of = slice(p * block, p * block + block)
                    held_ref[r * per + p] = g[:, of]
                    for h in range(heads):
                        inner_ref[r * per + p, h : h + 1, :] = jnp.sum(
                            both[h * 64 : h * 64 + 64, of], axis=0, keepdims=True
                        )

        dist = dist_ref[...]
        for h in range(heads):
            mine = slice(h * 64, h * 64 + 64)
            q = qkv_ref[at, mine]
            k = qkv_ref[:, cols + h * 64 : cols + h * 64 + 64]
            v = qkv_ref[:, 2 * cols + h * 64 : 2 * cols + h * 64 + 64]
            g = held_ref[step, mine, :]
            s = dot(k, q, NT) * SCALE - dist * slope_ref[h]
            p = jnp.exp(s - lse_ref[h : h + 1, :])
            gp = dot(v, g, NN)
            gs = (p * (gp - inner_ref[step, h : h + 1, :])).astype(BF16)
            dv_ref[:, mine] += dot(p.astype(BF16), g, NT)
            dk_ref[:, mine] += dot(gs, q, NN)
            dq_ref[step, mine, :] = (dot(k, gs, TN) * SCALE).astype(BF16)

        @pl.when(step == pl.num_programs(0) - 1)
        def _():
            for r in range(sub):
                of = slice(r * count, r * count + count)
                for p in range(per):
                    out_refs[r][:cols, p * block : p * block + block] = dq_ref[r * per + p]
                out_refs[r][cols : 2 * cols, :] = (dk_ref[of, :] * SCALE).T.astype(BF16)
                out_refs[r][2 * cols :, :] = dv_ref[of, :].T.astype(BF16)

    return pl.pallas_call(
        body,
        grid=(length // block,),
        in_specs=[
            pl.BlockSpec(memory_space=pltpu.SMEM),
            pl.BlockSpec((length, width), lambda i: (0, 0)),
            pl.BlockSpec((heads, block), lambda i: (0, i)),
            pl.BlockSpec((length, block), lambda i: (0, i)),
            *[pl.BlockSpec((cols, count), lambda i: (0, 0))] * (2 * sub),
        ],
        out_specs=[pl.BlockSpec((width, count), lambda i: (0, 0))] * sub,
        out_shape=[jax.ShapeDtypeStruct((width, count), BF16)] * sub,
        scratch_shapes=[
            pltpu.VMEM((length, cols), F32),
            pltpu.VMEM((length, cols), F32),
            pltpu.VMEM((length // block, cols, block), BF16),
            pltpu.VMEM((length // block, cols, block), BF16),
            pltpu.VMEM((length // block, heads, block), F32),
        ],
        compiler_params=pltpu.CompilerParams(vmem_limit_bytes=VMEM_LIMIT),
        cost_estimate=cost(
            flops=8 * heads * length * length * HEAD_DIM,
            bytes_accessed=4 * length * length,
            transcendentals=heads * length * length,
        ),
        name="attend_backward",
    )(slopes, qkv, lse, far_dist, *ctx, *ctx_grad)


def pack_columns(*values):
    rows = [value.shape[-2] for value in values]
    blocks = [value.shape[-1] // PACK for value in values]
    lead = values[0].shape[:-2]
    total = sum(r * n for r, n in zip(rows, blocks))
    if any(r % 8 for r in rows):
        parts = []
        for value in values:
            parts += [value[..., i : i + PACK] for i in range(0, value.shape[-1], PACK)]
        return jnp.concatenate(parts, axis=-2)

    def body(*refs):
        out_ref = refs[-1]
        for i in range(math.prod(lead)):
            at = 0
            for ref, r, n in zip(refs, rows, blocks):
                value = ref[i].astype(F32) if r % 16 else ref[i]
                for j in range(n):
                    out_ref[i, at : at + r, :] = value[:, j * PACK : j * PACK + PACK].astype(BF16)
                    at += r

    flat = [value.reshape(math.prod(lead), *value.shape[-2:]) for value in values]
    return pl.pallas_call(
        body,
        out_shape=jax.ShapeDtypeStruct((math.prod(lead), total, PACK), BF16),
        compiler_params=pltpu.CompilerParams(vmem_limit_bytes=VMEM_LIMIT),
cost_estimate=pl.CostEstimate(flops=1 << 20, bytes_accessed=1 << 10, transcendentals=0),
        name="pack_columns",
    )(*flat).reshape(*lead, total, PACK)


def unpack_plan(width, ff, tok_devices, dp_devices):
    far = dp_devices // 2
    half = width // 2
    row_out, row_down = width // tok_devices, ff // tok_devices
    few = row_out // dp_devices
    plan = [[], [], []]
    for device in range(dp_devices):
        at, core = device // 2, device % 2
        first_cols = ff - far * PACK
        firsts, lasts, heads = [], [], []
        for layer in range(LAYERS):
            firsts.append(
                [
                    (2, layer, 0, core * ff + at * (first_cols // far) + i, row_out)
                    for i in range(0, first_cols // far, PACK)
                ]
            )
            lasts.append(
                [
                    (3, layer, at * (row_down // far), core * half, row_down // far),
                    (1, layer, at * (row_out // far), core * half, row_out // far),
                    (2, layer, 0, core * ff + first_cols + at * PACK, row_out),
                ]
            )
        for i in range(0, 3 * width, PACK):
            for layer in range(LAYERS):
                heads.append((0, layer, device * few, i, few))
        plan[0].append(firsts[0])
        gap = [(None, 0, 0, 0, 8)]
        plan[1].append(lasts[0] + gap + heads)
        plan[2].append(firsts[1] + lasts[1])
    return plan


def assemble(packed, width, ff, tok_devices, dp_devices):
    row_out, row_down = width // tok_devices, ff // tok_devices
    plan = unpack_plan(width, ff, tok_devices, dp_devices)
    shapes = [
        (row_out, LAYERS, 3 * width),
        (row_out, LAYERS, width),
        (row_out, LAYERS, 2 * ff),
        (row_down, LAYERS, width),
    ]
    if row_out // dp_devices % 8:
        outs = [jnp.zeros(shape, F32) for shape in shapes]
        for array, pieces in zip(packed, plan):
            for device in range(dp_devices):
                row = 0
                for out, n, to_row, to_col, count in pieces[device]:
                    if out is not None:
                        piece = array[device, row : row + count].astype(F32)
                        outs[out] = (
                            outs[out].at[to_row : to_row + count, n, to_col : to_col + PACK]
                        ).set(piece)
                    row += count
        return outs

    def body(*refs):
        in_refs, out_refs = refs[: len(plan)], refs[len(plan) :]
        for step in range(2):

            @pl.when(pl.program_id(0) == step)
            def _():
                for ref, pieces in zip(in_refs, plan):
                    for device in range(dp_devices):
                        row = 0
                        for out, n, to_row, to_col, count in pieces[device]:
                            if out is not None:
                                half = shapes[out][0] // 2
                                begin = max(to_row, step * half)
                                end = min(to_row + count, step * half + half)
                                if begin < end:
                                    piece = ref[device, row + begin - to_row : row + end - to_row, :]
                                    out_refs[out][
                                        begin - step * half : end - step * half,
                                        n,
                                        to_col : to_col + PACK,
                                    ] = piece.astype(F32)
                            row += count

    return pl.pallas_call(
        body,
        grid=(2,),
        in_specs=[pl.BlockSpec(v.shape, lambda i: (0, 0, 0)) for v in packed],
        out_specs=[
            pl.BlockSpec((rows // 2, layers, cols), lambda i: (i, 0, 0))
            for rows, layers, cols in shapes
        ],
        out_shape=[jax.ShapeDtypeStruct(shape, F32) for shape in shapes],
        compiler_params=pltpu.CompilerParams(vmem_limit_bytes=VMEM_LIMIT),
        name="assemble",
    )(*packed)


def swap(value, axis, bit):
    return lax.ppermute(value, axis, [(i, i ^ (1 << bit)) for i in range(lax.axis_size(axis))])


def bit_of(axis, bit):
    return (lax.axis_index(axis) >> bit) & 1


def bits_of(axis):
    return lax.axis_size(axis).bit_length() - 1


def add_up(*values):
    total = values[0].astype(F32)
    for value in values[1:]:
        total = total + value.astype(F32)
    return total.astype(BF16)


def reduce_half(value, axis, bit, dim):
    mine = bit_of(axis, bit)
    half = value.shape[dim] // 2
    kept = lax.dynamic_slice_in_dim(value, mine * half, half, dim)
    sent = lax.dynamic_slice_in_dim(value, (1 - mine) * half, half, dim)
    return add_up(kept, swap(sent, axis, bit))


def gather_pair(value, axis, bit, dim):
    mine = bit_of(axis, bit)
    other = swap(value, axis, bit)
    low = jnp.where(mine == 0, value, other)
    high = jnp.where(mine == 0, other, value)
    return jnp.stack((low, high), axis=dim)


def pin(*values):
    return lax.optimization_barrier(values)


def far_bits(sub):
    return [bit for bit in reversed(range(bits_of("tok"))) if (1 << bit) >= sub]


def per_device(
    tokens, mask, segments, replacement, w_qkv, w_out, w_in, w_down, ln_gain, ln_bias, cotangent
):
    tok_devices = lax.axis_size("tok")
    dp_devices = lax.axis_size("dp")
    seq_count, local_len, width = tokens.shape
    ff = w_down.shape[0]
    sub = tok_devices // seq_count
    per_group = HEADS // sub
    cols = per_group * HEAD_DIM
    tok_count = seq_count * local_len
    full_len = local_len * tok_devices
    tok_place = lax.axis_index("tok")
    group = tok_place % sub
    place_of = group.reshape(1)
    core = bit_of("dp", 0).reshape(1)
    side = bit_of("dp", bits_of("dp") - 1).reshape(1)
    near = [[j + sub * k for j in range(sub)] for k in range(seq_count)]
    apart = [[j + sub * k for k in range(seq_count)] for j in range(sub)]

    def regroup(value):
        place = tok_place // sub
        parts = [lax.dynamic_index_in_dim(value, place, 0, False)]
        for r in range(1, seq_count):
            part = lax.dynamic_index_in_dim(value, place ^ r, 0, False)
            to = [(i, i ^ (r * sub)) for i in range(tok_devices)]
            parts.append(lax.ppermute(part, "tok", to))
        if seq_count == 2:
            low = jnp.where(place == 0, parts[0], parts[1])
            return jnp.stack((low, jnp.where(place == 0, parts[1], parts[0])))
        return jnp.stack(parts)[jnp.arange(seq_count) ^ place]

    def spread(value):
        return lax.all_to_all(value, "tok", 0, 0, axis_index_groups=near)

    near_pairs = [[(i, i ^ r) for i in range(tok_devices)] for r in range(1, sub)]

    def deal(parts):
        return [
            parts[0],
            *(lax.ppermute(p, "tok", to) for p, to in zip(parts[1:], near_pairs)),
        ]

    extra = jnp.zeros((seq_count, local_len, LANES), BF16)
    code = (mask == 1).astype(jnp.int32) + 2 * segments
    extra = extra.at[:, :, 0].set(code.astype(BF16))
    mixed = regroup(jnp.concatenate((tokens, extra), axis=-1)).reshape(tok_count, -1)
    wq = split_layers_by_group(w_qkv, sub)
    wo = split_layers(w_out)
    mixed, wq, wo, w_in = pin(mixed, wq, wo, w_in)
    flags = mixed[:, width:]
    masked = flags[:, :1].astype(jnp.int32) % 2 == 1
    current = jnp.where(masked, replacement[None, :], mixed[:, :width].astype(F32))
    flat_in = current.astype(BF16)

    wi = split_layers(w_in)
    slopes = lax.dynamic_slice_in_dim(alibi_slopes(HEADS), group * per_group, per_group, 0)
    order = jnp.arange(sub, dtype=jnp.int32) ^ group
    place = (
        (jnp.arange(seq_count, dtype=jnp.int32)[None, :, None] * sub + order[:, None, None])
        * local_len
        + jnp.arange(local_len, dtype=jnp.int32)[None, None, :]
    ).reshape(full_len)
    far_dist = None
    stored = []
    for layer in range(LAYERS):
        sent = jnp.concatenate((flat_in, flags), axis=-1) if layer == 0 else flat_in
        parts = deal([sent] * sub)
        if layer == 0:
            *parts, wi, w_down = pin(*parts, wi, w_down)
            wd = split_layers(w_down)
            codes = jnp.concatenate([p[:, width] for p in parts]).astype(jnp.int32)
            labels = codes // 2
            masks = (codes % 2).astype(BF16).reshape(sub, 1, tok_count)
            masks = jnp.broadcast_to(masks, (sub, 16, tok_count))
            far_dist = jnp.where(
                labels[:, None] == labels[None, :],
                jnp.abs(place[:, None] - place[None, :]).astype(F32),
                FAR,
            )
        else:
            *parts, stored[0]["lhs_other"] = pin(*parts, stored[0]["lhs_other"])
        qkv = project(layer, place_of, parts, wq)
        *ctx_here, lse = attend_forward(qkv, far_dist, slopes, sub)
        ctx = deal(ctx_here)
        if layer == 0:
            *ctx, wd, cot = pin(*ctx, wd, regroup(cotangent))
        lhs, a, b, summed, z, current, flat_in = feed_forward(
            layer, place_of, current, ctx, wo, wi, wd, ln_gain, ln_bias
        )
        stored.append(
            {
                "attend": (parts, qkv, ctx_here, lse),
                "feed": (z, summed, a, b),
                "lhs": lhs,
                "lhs_other": swap(lhs, "dp", 0),
            }
        )
    layer_out = flat_in.reshape(seq_count, local_len, width)
    gradient = cot.reshape(tok_count, width).astype(F32)
    small = []
    row_out = width // tok_devices
    row_down = ff // tok_devices
    half = width // 2
    x_bits = list(reversed(range(1, bits_of("dp"))))
    far = dp_devices // 2

    def near_sum(parts):
        return add_up(*deal(parts))

    def x_sum(keep, send, parts):
        total = add_up(keep, swap(send, "dp", x_bits[0]))
        for bit in x_bits[1:]:
            at = bit_of("dp", bit)
            picked = []
            for choice in (at, 1 - at):
                begin, slices = 0, []
                for rows in parts:
                    slices.append(
                        lax.dynamic_slice_in_dim(
                            total, begin + choice * (rows // 2), rows // 2, 1
                        )
                    )
                    begin += rows
                picked.append(jnp.concatenate(slices, axis=1))
            total = add_up(picked[0], swap(picked[1], "dp", bit))
            parts = [rows // 2 for rows in parts]
        return total

    def x_sum_down(keep, send):
        return x_sum(keep, send, [row_down // 2, row_out // 2])

    def x_sum_in(keep, send):
        shape = (tok_devices, -1, PACK)
        return x_sum(keep.reshape(shape), send.reshape(shape), [far // 2 * row_out])

    def x_sum_columns(value):
        for bit in x_bits:
            value = reduce_half(value, "dp", bit, value.ndim - 1)
        return value

    def far_sum(value):
        for bit in far_bits(sub):
            value = reduce_half(value, "tok", bit, 0)
        return value[0]

    def by_place(value):
        return value.reshape(seq_count, sub, *value.shape[1:]).swapaxes(0, 1)

    def spread_sum(value):
        return add_up(*spread(by_place(value)))

    def deal_sum(value):
        value = by_place(value)
        return near_sum(
            [lax.dynamic_index_in_dim(value, group ^ r, 0, False) for r in range(sub)]
        )

    def dp_sum(value):
        return add_up(*lax.all_to_all(value, "dp", 0, 0))

    def by_head(value):
        few = row_out // dp_devices
        value = spread(by_place(value))
        extra = jnp.sum(value[:, :, few : few + 8, :PACK].astype(F32), axis=0).astype(BF16)
        value = jnp.concatenate((value[:, :, :few], value[:, :, few + 8 :]), axis=2)
        value = value.reshape(sub, seq_count, -1, 3, cols)
        return extra, value.transpose(1, 2, 3, 0, 4).reshape(seq_count, -1, 3 * width)

    before = None
    for layer in reversed(range(LAYERS)):
        parts, qkv, ctx_here, lse = stored[layer]["attend"]
        z, summed, a, b = stored[layer]["feed"]
        lhs, lhs_other = stored[layer]["lhs"], stored[layer]["lhs_other"]
        fed = feed_backward(
            layer, core, place_of, gradient, z, summed, a, b, wo, wi, wd, ln_gain, sub
        )
        if before is None:
            *fed, lhs_other = pin(*fed, lhs_other)
        else:
            send = fed[1]
            *fed, late, down, layer_out = pin(
                *fed, near_sum(before["late"]), x_sum_down(*before["down"]), regroup(layer_out)
            )
            fed[1] = send
            first = jnp.concatenate((before["early"], late), axis=2)
            last = jnp.concatenate((down, before["last"]), axis=1)
        mine, send, ga, small_part, *gctx = fed
        small.insert(0, small_part)
        other = swap(send, "dp", 0)
        ctx_grad = deal(gctx)
        if before is not None:
            other, first, last = pin(other, first, last)
        *g_first, keep, sent, keep_in, sent_in = pair_grads(
            place_of, side, lhs, lhs_other, mine, other, ff, tok_devices, sub, far, before is None
        )
        done = (*ctx_grad, keep, sent, keep_in, sent_in, *g_first)
        if before is not None:
            done += (x_sum_columns(first), spread_sum(last))
        done = pin(*done)
        ctx_grad, (keep, sent, keep_in, sent_in) = done[:sub], done[sub : sub + 4]
        done = done[sub + 4 :]
        head_grad = attend_backward(qkv, ctx_here, ctx_grad, lse, far_dist, slopes)
        if before is None:
            both = pin(
                *head_grad, near_sum(done[:sub]), x_sum_in(keep_in, sent_in), keep, sent, *done[sub:]
            )
            head_grad, (early, last, keep, sent, *late) = both[:sub], both[sub:]
            g_qkv = dp_sum(qkv_grad(parts, head_grad, width, tok_devices, dp_devices))
            both = pin(*deal(head_grad), g_qkv, keep, sent, *late)
            back, (g_qkv, keep, sent, *late) = both[:sub], both[sub:]
            before = {
                "early": early,
                "late": late,
                "last": last,
                "down": (keep, sent),
                "qkv": g_qkv,
            }
        else:
            g_first, (first, last) = done[:sub], done[sub:]
            g_qkv = last_grads(
                place_of, small, masks, parts, head_grad, ga, wq,
                tok_devices, dp_devices,
            )
            both = pin(
                *head_grad,
                g_qkv,
                near_sum(g_first),
                x_sum_in(keep_in, sent_in),
                x_sum_down(keep, sent),
                lax.psum_scatter(
                    pack_columns(first, last), "tok", scatter_dimension=0, axis_index_groups=apart
                ),
            )
            head_grad, (g_qkv, g_first, g_last, g_down, before_all) = both[:sub], both[sub:]
            g_last = deal_sum(jnp.concatenate((g_down, g_last), axis=1))
            *head_grad, g_last = pin(*head_grad, g_last)
            g_qkv = jnp.concatenate((dp_sum(g_qkv), before["qkv"]), axis=1)
            both = pin(
                *deal(head_grad),
                *by_head(g_qkv),
                far_sum(pack_columns(x_sum_columns(g_first))),
                g_last,
                before_all,
            )
            back, (*g_qkv, g_first, g_last, before_all) = both[:sub], both[sub:]
            packed = [
                g_first,
                far_sum(pack_columns(g_last, *g_qkv)),
                lax.all_gather(before_all, "dp"),
            ]
        gradient = input_grad(layer, place_of, ga, back, wq)
    packed[0] = packed[0][None]
    for bit in x_bits:
        packed[0] = gather_pair(packed[0], "dp", bit, 1)
        packed[0] = packed[0].reshape(-1, *packed[0].shape[2:])
    gradient, *packed = pin(gradient, *packed)
    grad_tokens = jnp.where(masked, 0.0, gradient).astype(BF16)
    grad_tokens = regroup(grad_tokens.reshape(seq_count, local_len, width))
    value = packed[1][None]
    for bit in x_bits:
        value = gather_pair(value, "dp", bit, 1)
        value = value.reshape(-1, *value.shape[2:])
    value, packed[0], grad_tokens = pin(value, gather_pair(packed[0], "dp", 0, 1), grad_tokens)
    grad_tokens = grad_tokens.astype(F32)
    packed[1] = gather_pair(value, "dp", 0, 1)
    packed[:2] = [v.reshape(dp_devices, *v.shape[2:]) for v in packed[:2]]
    begin = (row_down + row_out) // far + row_out
    few = row_out // dp_devices
    small = packed[1][:, begin : begin + 8].astype(F32)
    small = jnp.concatenate((small[:, :, :few], small[:, :1, LANES : LANES + few]), axis=1)
    small = small.transpose(1, 0, 2).reshape(-1, row_out)
    by_layer = small[: 4 * LAYERS].reshape(LAYERS, 2, 2, row_out)
    return (
        layer_out,
        grad_tokens,
        small[-1],
        *assemble(packed, width, ff, tok_devices, dp_devices),
        by_layer[:, 0],
        by_layer[:, 1],
    )


def solution(mesh):
    in_specs = (
        P("dp", "tok", None),
        P("dp", "tok"),
        P("dp", "tok"),
        P(),
        P(),
        P(),
        P(),
        P(),
        P(),
        P(),
        P("dp", "tok", None),
    )
    out_specs = (
        P("dp", "tok", None),
        P("dp", "tok", None),
        P("tok"),
        P("tok", None, None),
        P("tok", None, None),
        P("tok", None, None),
        P("tok", None, None),
        P(None, None, "tok"),
        P(None, None, "tok"),
    )
    return jax.shard_map(
        per_device, mesh=mesh, in_specs=in_specs, out_specs=out_specs, check_vma=False
    )
```

```python
import functools
import math

import jax
import jax.numpy as jnp
from jax import lax
from jax.experimental import pallas as pl
from jax.experimental.pallas import tpu as pltpu
from jax.sharding import PartitionSpec as P

HEADS = 12
HEAD_DIM = 64
LAYERS = 2
LANES = 128
PACK = 384
SCALE = 1.0 / math.sqrt(HEAD_DIM)
FAR = 1e30
BF16 = jnp.bfloat16
F32 = jnp.float32
VMEM_LIMIT = 56 << 20
COST_TIMES = 4


def alibi_slopes(head_count):
    head_index = jnp.arange(head_count, dtype=jnp.float32)
    return jnp.exp2(jnp.where(head_index < 8.0, -(head_index + 1.0), 7.5 - head_index))


def dot(a, b, dims):
    return lax.dot_general(a, b, (dims, ((), ())), preferred_element_type=F32)


def cost(flops, bytes_accessed, transcendentals):
    return pl.CostEstimate(
        flops=COST_TIMES * flops,
        bytes_accessed=bytes_accessed,
        transcendentals=transcendentals,
    )


NN = ((1,), (0,))
NT = ((1,), (1,))
TN = ((0,), (0,))


def split_layers(weight):
    rows, _, cols = weight.shape
    row_block = 256
    col_block = next(c for c in (3072, 2304, 1152, 768) if cols % c == 0)

    def body(in_ref, out_ref):
        to_row = lax.broadcasted_iota(jnp.int32, (256, 256), 0)
        from_row = lax.broadcasted_iota(jnp.int32, (256, 256), 1)
        wanted = jnp.where(to_row < 128, 2 * to_row, 2 * to_row - 255)
        pick = jnp.where(from_row == wanted, 1.0, 0.0).astype(BF16)
        for part in range(row_block // 128):
            at = slice(part * 128, part * 128 + 128)
            mixed = in_ref[at].reshape(256, col_block)
            picked = dot(pick, mixed, NN).astype(BF16)
            out_ref[0, at] = picked[:128]
            out_ref[1, at] = picked[128:]

    return pl.pallas_call(
        body,
        grid=(rows // row_block, cols // col_block),
        in_specs=[pl.BlockSpec((row_block, 2, col_block), lambda i, j: (i, 0, j))],
        out_specs=pl.BlockSpec((2, row_block, col_block), lambda i, j: (0, i, j)),
        out_shape=jax.ShapeDtypeStruct((2, rows, cols), BF16),
        compiler_params=pltpu.CompilerParams(vmem_limit_bytes=VMEM_LIMIT),
        cost_estimate=cost(
            flops=2 * 512 * rows * cols, bytes_accessed=8 * rows * cols, transcendentals=0
        ),
        name="split_layers",
    )(weight)


def split_layers_by_group(weight, sub):
    rows, _, cols = weight.shape
    row_block = 256
    group_cols = cols // sub // 3

    def body(in_ref, out_ref):
        to_row = lax.broadcasted_iota(jnp.int32, (256, 256), 0)
        from_row = lax.broadcasted_iota(jnp.int32, (256, 256), 1)
        wanted = jnp.where(to_row < 128, 2 * to_row, 2 * to_row - 255)
        pick = jnp.where(from_row == wanted, 1.0, 0.0).astype(BF16)
        for part in range(row_block // 128):
            at = slice(part * 128, part * 128 + 128)
            picked = dot(pick, in_ref[at].reshape(256, cols), NN).astype(BF16)
            for j in range(sub):
                for n in range(3):
                    first = (n * sub + j) * group_cols
                    block = picked[:, first : first + group_cols]
                    to = slice(n * group_cols, n * group_cols + group_cols)
                    out_ref[0, j, at, to] = block[:128]
                    out_ref[1, j, at, to] = block[128:]

    return pl.pallas_call(
        body,
        grid=(rows // row_block,),
        in_specs=[pl.BlockSpec((row_block, 2, cols), lambda i: (i, 0, 0))],
        out_specs=pl.BlockSpec((2, sub, row_block, 3 * group_cols), lambda i: (0, 0, i, 0)),
        out_shape=jax.ShapeDtypeStruct((2, sub, rows, 3 * group_cols), BF16),
        compiler_params=pltpu.CompilerParams(vmem_limit_bytes=VMEM_LIMIT),
        cost_estimate=cost(
            flops=2 * 512 * rows * cols, bytes_accessed=8 * rows * cols, transcendentals=0
        ),
        name="split_qkv",
    )(weight)


def norm_parts(value):
    center = jnp.mean(value, axis=-1, keepdims=True)
    shifted = value - center
    inverse = lax.rsqrt(jnp.mean(shifted * shifted, axis=-1, keepdims=True) + 1e-12)
    return shifted * inverse, inverse


def norm_grad(grad, value, gain):
    normed, inverse = norm_parts(value)
    scaled = grad * gain
    one = jnp.mean(scaled, axis=-1, keepdims=True)
    two = jnp.mean(scaled * normed, axis=-1, keepdims=True)
    in_grad = inverse * (scaled - one - normed * two)
    gain_grad = jnp.sum(grad * normed, axis=0, keepdims=True)
    bias_grad = jnp.sum(grad, axis=0, keepdims=True)
    return in_grad, gain_grad, bias_grad


def feed_forward(layer, group, current, ctx, w_out, w_in, w_down, gain, bias):
    count, width = current.shape
    sub, cols = len(ctx), ctx[0].shape[0]
    ff = w_down.shape[1]
    chunk = 768
    steps = ff // chunk

    def body(group_ref, *refs):
        ctx_refs = refs[:sub]
        cur_ref, wo_ref, wg_ref, wu_ref, wd_ref, gain_ref, bias_ref = refs[sub : sub + 7]
        lhs_ref, a_ref, b_ref, sum_ref, z_ref, next_ref, low_ref = refs[sub + 7 : sub + 14]
        y1l_ref, acc_ref, held_ref = refs[sub + 14 :]
        step = pl.program_id(0)

        @pl.when(step == 0)
        def _():
            branch = jnp.zeros((count, width), F32)
            for r in range(sub):
                held_ref[jnp.bitwise_xor(group_ref[0], r)] = ctx_refs[r][...]
            for j in range(sub):
                part = held_ref[j]
                to = slice(j * cols, j * cols + cols)
                lhs_ref[:, width + ff + j * cols : width + ff + j * cols + cols] = (
                    part.astype(F32).T.astype(BF16)
                )
                branch += dot(part, wo_ref[0, to, :], TN)
            summed = cur_ref[...] + branch
            sum_ref[...] = summed
            normed, _ = norm_parts(summed)
            y1 = normed * gain_ref[layer, 0:1, :] + bias_ref[layer, 0:1, :]
            acc_ref[...] = y1
            y1l_ref[...] = y1.astype(BF16)
            lhs_ref[:, :width] = y1.astype(BF16)

        y1l = y1l_ref[...]
        gate = dot(y1l, wg_ref[0], NN)
        up = dot(y1l, wu_ref[0], NN)
        cdf = 0.5 * (1.0 + lax.erf(gate * (0.5**0.5)))
        density = jnp.exp(-0.5 * gate * gate) * (1.0 / math.sqrt(2.0 * math.pi))
        gelu = gate * cdf
        hidden = (gelu * up).astype(BF16)
        a_ref[...] = gelu.astype(BF16)
        b_ref[...] = (up * (cdf + gate * density)).astype(BF16)
        lhs_ref[:, pl.ds(pl.multiple_of(width + step * chunk, 128), chunk)] = hidden
        acc_ref[...] += dot(hidden, wd_ref[0], NN)

        @pl.when(step == steps - 1)
        def _():
            z = acc_ref[...]
            z_ref[...] = z
            normed, _ = norm_parts(z)
            out = normed * gain_ref[layer, 1:2, :] + bias_ref[layer, 1:2, :]
            next_ref[...] = out
            low_ref[...] = out.astype(BF16)

    whole = lambda *shape: pl.BlockSpec(shape, lambda i: (0,) * len(shape))
    return pl.pallas_call(
        body,
        grid=(steps,),
        in_specs=[
            pl.BlockSpec(memory_space=pltpu.SMEM),
            *[whole(cols, count)] * sub,
            whole(count, width),
            pl.BlockSpec((1, width, width), lambda i: (layer, 0, 0)),
            pl.BlockSpec((1, width, chunk), lambda i: (layer, 0, i)),
            pl.BlockSpec((1, width, chunk), lambda i: (layer, 0, steps + i)),
            pl.BlockSpec((1, chunk, width), lambda i: (layer, i, 0)),
            whole(*gain.shape),
            whole(*bias.shape),
        ],
        out_specs=[
            whole(count, ff + 2 * width),
            pl.BlockSpec((count, chunk), lambda i: (0, i)),
            pl.BlockSpec((count, chunk), lambda i: (0, i)),
            whole(count, width),
            whole(count, width),
            whole(count, width),
            whole(count, width),
        ],
        out_shape=[
            jax.ShapeDtypeStruct((count, ff + 2 * width), BF16),
            jax.ShapeDtypeStruct((count, ff), BF16),
            jax.ShapeDtypeStruct((count, ff), BF16),
            jax.ShapeDtypeStruct((count, width), F32),
            jax.ShapeDtypeStruct((count, width), F32),
            jax.ShapeDtypeStruct((count, width), F32),
            jax.ShapeDtypeStruct((count, width), BF16),
        ],
        scratch_shapes=[
            pltpu.VMEM((count, width), BF16),
            pltpu.VMEM((count, width), F32),
            pltpu.VMEM((sub, cols, count), BF16),
        ],
        compiler_params=pltpu.CompilerParams(vmem_limit_bytes=VMEM_LIMIT),
        cost_estimate=cost(
            flops=2 * count * width * (width + 3 * ff),
            bytes_accessed=6 * width * ff + 2 * width * width + count * (20 * width + 6 * ff),
            transcendentals=2 * count * ff,
        ),
        name="feed_forward",
    )(group, *ctx, current, w_out, w_in, w_in, w_down, gain, bias)


def feed_backward(layer, core, group, grad, z, summed, a, b, w_out, w_in, w_down, gain, sub):
    count, width = grad.shape
    ff = w_down.shape[1]
    cols = width // sub
    half = width // 2
    chunk = 768
    steps = ff // chunk

    def body(
        core_ref, group_ref, grad_ref, z_ref, sum_ref, a_ref, b_ref,
        wo_ref, wg_ref, wu_ref, wd_ref, gain_ref, mine_ref, send_ref, ga_ref, small_ref, *refs,
    ):
        gctx_refs = refs[:sub]
        gzl_ref, acc_ref, held_ref = refs[sub:]
        step = pl.program_id(0)
        first = core_ref[0] == 0

        def store(to, low, high):
            mine_ref[:, to] = jnp.where(first, low, high)
            send_ref[:, to] = jnp.where(first, high, low)

        @pl.when(step == 0)
        def _():
            gz, gain_grad, bias_grad = norm_grad(grad_ref[...], z_ref[...], gain_ref[layer, 1:2, :])
            small_ref[1:2, :] = gain_grad
            small_ref[3:4, :] = bias_grad
            acc_ref[...] = gz
            gzl = gz.astype(BF16)
            gzl_ref[...] = gzl
            store(slice(ff, ff + half), gz[:, :half].astype(BF16), gz[:, half:].astype(BF16))

        gzl = gzl_ref[...]
        ghid = dot(gzl, wd_ref[0], NT)
        ggate = (ghid * b_ref[...].astype(F32)).astype(BF16)
        gup = (ghid * a_ref[...].astype(F32)).astype(BF16)
        store(pl.ds(pl.multiple_of(step * chunk, 128), chunk), ggate, gup)
        acc_ref[...] += dot(ggate, wg_ref[0], NT) + dot(gup, wu_ref[0], NT)

        @pl.when(step == steps - 1)
        def _():
            ga, gain_grad, bias_grad = norm_grad(
                acc_ref[...], sum_ref[...], gain_ref[layer, 0:1, :]
            )
            small_ref[0:1, :] = gain_grad
            small_ref[2:3, :] = bias_grad
            ga_ref[...] = ga
            gal = ga.astype(BF16)
            store(slice(ff + half, ff + width), gal[:, :half], gal[:, half:])
            for j in range(sub):
                to = slice(j * cols, j * cols + cols)
                held_ref[j] = dot(wo_ref[0, to, :], gal, NT).astype(BF16)
            for r in range(sub):
                gctx_refs[r][...] = held_ref[jnp.bitwise_xor(group_ref[0], r)]

    whole = lambda *shape: pl.BlockSpec(shape, lambda i: (0,) * len(shape))
    return pl.pallas_call(
        body,
        grid=(steps,),
        in_specs=[
            pl.BlockSpec(memory_space=pltpu.SMEM),
            pl.BlockSpec(memory_space=pltpu.SMEM),
            whole(count, width),
            whole(count, width),
            whole(count, width),
            pl.BlockSpec((count, chunk), lambda i: (0, i)),
            pl.BlockSpec((count, chunk), lambda i: (0, i)),
            pl.BlockSpec((1, width, width), lambda i: (layer, 0, 0)),
            pl.BlockSpec((1, width, chunk), lambda i: (layer, 0, i)),
            pl.BlockSpec((1, width, chunk), lambda i: (layer, 0, steps + i)),
            pl.BlockSpec((1, chunk, width), lambda i: (layer, i, 0)),
            whole(*gain.shape),
        ],
        out_specs=[
            whole(count, ff + width),
            whole(count, ff + width),
            whole(count, width),
            whole(4, width),
            *[whole(cols, count)] * sub,
        ],
        out_shape=[
            jax.ShapeDtypeStruct((count, ff + width), BF16),
            jax.ShapeDtypeStruct((count, ff + width), BF16),
            jax.ShapeDtypeStruct((count, width), F32),
            jax.ShapeDtypeStruct((4, width), F32),
            *[jax.ShapeDtypeStruct((cols, count), BF16)] * sub,
        ],
        scratch_shapes=[
            pltpu.VMEM((count, width), BF16),
            pltpu.VMEM((count, width), F32),
            pltpu.VMEM((sub, cols, count), BF16),
        ],
        compiler_params=pltpu.CompilerParams(vmem_limit_bytes=VMEM_LIMIT),
        cost_estimate=cost(
            flops=2 * count * width * (width + 3 * ff),
            bytes_accessed=6 * width * ff + 2 * width * width + count * (24 * width + 8 * ff),
            transcendentals=0,
        ),
        name="feed_backward",
    )(core, group, grad, z, summed, a, b, w_out, w_in, w_in, w_down, gain)


def pair_grads(group, side, lhs, lhs_other, rhs, rhs_other, ff, tok_devices, sub, far, early):
    count = lhs.shape[0]
    width = rhs.shape[1] - ff
    half = width // 2
    rows, rows_down = width // tok_devices, ff // tok_devices
    seqs = tok_devices // sub
    chunk = 2 * PACK
    steps_in, steps_down = ff // chunk, ff // chunk
    first_steps = steps_in - far * PACK // chunk
    ends = [0, 1, first_steps] if early else [0, first_steps]
    spans = list(zip(ends[:-1], ends[1:]))
    split = far // 2
    half_down, half_out = rows_down // 2, rows // 2

    def body(group_ref, side_ref, l1_ref, l2_ref, r1_ref, r2_ref, h1_ref, h2_ref, *refs):
        out_refs = refs[: len(spans) * sub]
        keep_ref, send_ref, keep_in_ref, send_in_ref, held_ref = refs[len(spans) * sub :]
        step = pl.program_id(0)
        low_side = side_ref[0] == 0

        def store(t, at, low, high):
            keep_ref[t, at] = jnp.where(low_side, low, high).astype(BF16)
            send_ref[t, at] = jnp.where(low_side, high, low).astype(BF16)

        @pl.when(step < steps_in)
        def _():
            out = dot(l1_ref[...], r1_ref[...], TN) + dot(l2_ref[...], r2_ref[...], TN)

            @pl.when(step < first_steps)
            def _():
                for t in range(tok_devices):
                    held_ref[t % sub, t // sub] = out[t * rows : t * rows + rows].astype(BF16)

            for n, (begin, end) in enumerate(spans):

                @pl.when((step >= begin) & (step < end))
                def _():
                    for r in range(sub):
                        out_refs[n * sub + r][...] = held_ref[jnp.bitwise_xor(group_ref[0], r)]

            for f in range(2):
                block = 2 * (step - first_steps) + f
                here = block // split == side_ref[0]
                to = block % split
                for wanted, ref in ((here, keep_in_ref), (jnp.logical_not(here), send_in_ref)):

                    @pl.when((step >= first_steps) & wanted)
                    def _():
                        for t in range(tok_devices):
                            part = out[t * rows : t * rows + rows, f * PACK : f * PACK + PACK]
                            ref[t, to] = part.astype(BF16)

        @pl.when(step >= steps_in)
        def _():
            out = dot(l1_ref[...], h1_ref[...], TN) + dot(l2_ref[...], h2_ref[...], TN)
            each = chunk // rows_down

            @pl.when(step < steps_in + steps_down)
            def _():
                for i in range(each):
                    low = out[i * rows_down : i * rows_down + half_down]
                    high = out[i * rows_down + half_down : (i + 1) * rows_down]
                    store((step - steps_in) * each + i, slice(0, half_down), low, high)

            @pl.when(step == steps_in + steps_down)
            def _():
                for t in range(tok_devices):
                    low = out[t * rows : t * rows + half_out]
                    high = out[t * rows + half_out : (t + 1) * rows]
                    store(t, slice(half_down, half_down + half_out), low, high)

    left = pl.BlockSpec((count, chunk), lambda i: (0, jnp.maximum(i - steps_in + 1, 0)))
    right = pl.BlockSpec((count, chunk), lambda i: (0, jnp.minimum(i, steps_in - 1)))
    halves = pl.BlockSpec(
        (count, half), lambda i: (0, ff // half + jnp.where(i < steps_in + steps_down, 0, 1))
    )
    kept = (tok_devices, half_down + half_out, half)
    kept_in = (tok_devices, split, rows, PACK)
    whole = lambda *shape: pl.BlockSpec(shape, lambda i: (0,) * len(shape))
    return pl.pallas_call(
        body,
        grid=(steps_in + steps_down + 1,),
        in_specs=[
            pl.BlockSpec(memory_space=pltpu.SMEM),
            pl.BlockSpec(memory_space=pltpu.SMEM),
            left,
            left,
            right,
            right,
            halves,
            halves,
        ],
        out_specs=[
            *[
                pl.BlockSpec(
                    (seqs, rows, chunk),
                    functools.partial(
                        lambda begin, end, i: (0, 0, jnp.clip(i - begin, 0, end - begin - 1)),
                        begin,
                        end,
                    ),
                )
                for begin, end in spans
                for _ in range(sub)
            ],
            whole(*kept),
            whole(*kept),
            whole(*kept_in),
            whole(*kept_in),
        ],
        out_shape=[
            *[
                jax.ShapeDtypeStruct((seqs, rows, (end - begin) * chunk), BF16)
                for begin, end in spans
                for _ in range(sub)
            ],
            jax.ShapeDtypeStruct(kept, BF16),
            jax.ShapeDtypeStruct(kept, BF16),
            jax.ShapeDtypeStruct(kept_in, BF16),
            jax.ShapeDtypeStruct(kept_in, BF16),
        ],
        scratch_shapes=[pltpu.VMEM((sub, seqs, rows, chunk), BF16)],
        compiler_params=pltpu.CompilerParams(vmem_limit_bytes=VMEM_LIMIT),
        cost_estimate=cost(
            flops=8 * count * width * ff,
            bytes_accessed=4 * width * ff + 8 * count * (width + ff),
            transcendentals=0,
        ),
        name="pair_grads",
    )(group, side, lhs, lhs_other, rhs, rhs_other, rhs, rhs_other)


def input_grad(layer, group, ga, back, w_qkv):
    sub = len(back)
    cols, count = back[0].shape
    width = ga.shape[1]

    def body(group_ref, ga_ref, w_ref, *refs):
        back_refs, out_ref, acc_ref = refs[:sub], refs[sub], refs[sub + 1]
        step = pl.program_id(0)

        @pl.when(step == 0)
        def _():
            acc_ref[...] = jnp.zeros_like(acc_ref)

        for r in range(sub):

            @pl.when(step == r)
            def _():
                acc_ref[...] += dot(w_ref[0, 0], back_refs[r][...], NN)

        @pl.when(step == sub - 1)
        def _():
            out_ref[...] = ga_ref[...] + acc_ref[...].T

    return pl.pallas_call(
        body,
        grid_spec=pltpu.PrefetchScalarGridSpec(
            num_scalar_prefetch=1,
            grid=(sub,),
            in_specs=[
                pl.BlockSpec((count, width), lambda i, g: (0, 0)),
                pl.BlockSpec(
                    (1, 1, width, cols), lambda i, g: (layer, jnp.bitwise_xor(g[0], i), 0, 0)
                ),
                *[pl.BlockSpec((cols, count), lambda i, g: (0, 0))] * sub,
            ],
            out_specs=pl.BlockSpec((count, width), lambda i, g: (0, 0)),
            scratch_shapes=[pltpu.VMEM((width, count), F32)],
        ),
        out_shape=jax.ShapeDtypeStruct((count, width), F32),
        compiler_params=pltpu.CompilerParams(vmem_limit_bytes=VMEM_LIMIT),
        cost_estimate=cost(
            flops=2 * count * width * cols * sub,
            bytes_accessed=2 * sub * cols * (width + count) + 8 * count * width,
            transcendentals=0,
        ),
        name="input_grad",
    )(group, ga, w_qkv, *back)


def qkv_grad(parts, grads, width, tok_devices, dp_devices):
    sub = len(parts)
    count = parts[0].shape[0]
    cols = grads[0].shape[0]
    rows = width // tok_devices
    few = rows // dp_devices

    def body(*refs):
        qkv_grad_body(refs[:sub], refs[sub : 2 * sub], refs[2 * sub], rows, few)

    shape = (dp_devices, tok_devices, few, cols)
    return pl.pallas_call(
        body,
        grid=(1,),
        in_specs=[
            *[pl.BlockSpec((count, width), lambda i: (0, 0))] * sub,
            *[pl.BlockSpec((cols, count), lambda i: (0, 0))] * sub,
        ],
        out_specs=pl.BlockSpec(shape, lambda i: (0, 0, 0, 0)),
        out_shape=jax.ShapeDtypeStruct(shape, BF16),
        compiler_params=pltpu.CompilerParams(vmem_limit_bytes=VMEM_LIMIT),
        cost_estimate=pl.CostEstimate(flops=1 << 20, bytes_accessed=1 << 10, transcendentals=0),
        name="qkv_grad",
    )(*parts, *grads)


def qkv_grad_body(part_refs, grad_refs, out_ref, rows, few):
    cols, width = grad_refs[0].shape[0], part_refs[0].shape[1]
    acc = jnp.zeros((cols, width), F32)
    for part_ref, grad_ref in zip(part_refs, grad_refs):
        acc += dot(grad_ref[...], part_ref[...], NN)
    acc = acc.T
    dp_devices, tok_devices = out_ref.shape[:2]
    for t in range(tok_devices):
        for q in range(dp_devices):
            first = t * rows + q * few
            out_ref[q, t, :few, :] = acc[first : first + few].astype(BF16)


def last_grads(group, small, masks, parts, grads, ga, w_qkv, tok_devices, dp_devices):
    sub = len(grads)
    cols, count = grads[0].shape
    width = ga.shape[1]
    rows = width // tok_devices
    few = rows // dp_devices

    def twice(value):
        high = value.astype(BF16)
        return high, (value - high.astype(F32)).astype(BF16)

    def body(group_ref, mask_ref, ga_ref, w_ref, *refs):
        small_refs, refs = refs[:LAYERS], refs[LAYERS:]
        part_refs, grad_refs, out_ref = refs[:sub], refs[sub : 2 * sub], refs[2 * sub]
        qkv_grad_body(part_refs, grad_refs, out_ref, rows, few)
        total = jnp.zeros((16, cols), F32)
        for r in range(sub):
            total += dot(mask_ref[r], grad_refs[r][...], NT)
        mask_sum = jnp.zeros((16, width), F32)
        for part in twice(total):
            mask_sum += dot(part, w_ref[0, 0], NT)
        for part in twice(ga_ref[...]):
            mask_sum += dot(mask_ref[0], part, NN)
        values = jnp.concatenate([ref[...] for ref in small_refs], axis=0)
        for t in range(tok_devices):
            for q in range(dp_devices):
                of = slice(t * rows + q * few, t * rows + q * few + few)
                row = jnp.concatenate(
                    (
                        jnp.pad(values[:, of], ((0, 0), (0, LANES - few))),
                        jnp.pad(mask_sum[:8, of], ((0, 0), (0, cols - LANES - few))),
                    ),
                    axis=1,
                )
                out_ref[q, t, few:, :] = row.astype(BF16)

    whole = lambda *shape: pl.BlockSpec(shape, lambda i, g: (0,) * len(shape))
    shape = (dp_devices, tok_devices, few + 8, cols)
    return pl.pallas_call(
        body,
        grid_spec=pltpu.PrefetchScalarGridSpec(
            num_scalar_prefetch=1,
            grid=(1,),
            in_specs=[
                whole(sub, 16, count),
                whole(count, width),
                pl.BlockSpec((1, 1, width, cols), lambda i, g: (0, g[0], 0, 0)),
                *[whole(8 // LAYERS, width)] * LAYERS,
                *[whole(count, width)] * sub,
                *[whole(cols, count)] * sub,
            ],
            out_specs=whole(*shape),
        ),
        out_shape=jax.ShapeDtypeStruct(shape, BF16),
        compiler_params=pltpu.CompilerParams(vmem_limit_bytes=VMEM_LIMIT),
        cost_estimate=pl.CostEstimate(flops=1 << 20, bytes_accessed=1 << 10, transcendentals=0),
        name="last_grads",
    )(group, masks, ga, w_qkv, *small, *parts, *grads)


def attend_forward(layer, group, parts, w_qkv, far_dist, slopes):
    sub = len(parts)
    count, length = parts[0].shape[0], far_dist.shape[0]
    model_width, width = w_qkv.shape[2:]
    cols = width // 3
    heads = cols // HEAD_DIM
    block = 256
    per = count // block

    def body(group_ref, slope_ref, dist_ref, w_ref, *refs):
        part_refs, (qkv_ref, lse_ref) = refs[:sub], refs[sub : sub + 2]
        ctx_refs, held_ref = refs[sub + 2 : 2 * sub + 2], refs[2 * sub + 2]
        step = pl.program_id(0)

        @pl.when(step == 0)
        def _():
            for r in range(sub):
                qkv_ref[r * count : r * count + count, :] = dot(
                    part_refs[r][...], w_ref[0, 0], NN
                ).astype(BF16)

        at = pl.ds(pl.multiple_of(step * block, block), block)
        dist = dist_ref[...]
        for h in range(heads):
            q = qkv_ref[at, h * 64 : h * 64 + 64]
            k = qkv_ref[:, cols + h * 64 : cols + h * 64 + 64]
            v = qkv_ref[:, 2 * cols + h * 64 : 2 * cols + h * 64 + 64]
            s = dot(k, q, NT) * SCALE - dist * slope_ref[h]
            top = jnp.max(s, axis=0, keepdims=True)
            e = jnp.exp(s - top)
            total = jnp.sum(e, axis=0, keepdims=True)
            ctx = dot(v, e.astype(BF16), TN) / total
            held_ref[h * 64 : h * 64 + 64, :] = ctx.astype(BF16)
            lse_ref[h : h + 1, :] = top + jnp.log(total)
        for i in range(length // block):

            @pl.when(step == i)
            def _():
                first = i % per * block
                ctx_refs[i // per][:, first : first + block] = held_ref[...]

    return pl.pallas_call(
        body,
        grid_spec=pltpu.PrefetchScalarGridSpec(
            num_scalar_prefetch=1,
            grid=(length // block,),
            in_specs=[
                pl.BlockSpec(memory_space=pltpu.SMEM),
                pl.BlockSpec((length, block), lambda i, g: (0, i)),
                pl.BlockSpec((1, 1, model_width, width), lambda i, g: (layer, g[0], 0, 0)),
                *[pl.BlockSpec((count, model_width), lambda i, g: (0, 0))] * sub,
            ],
            out_specs=[
                pl.BlockSpec((length, width), lambda i, g: (0, 0)),
                pl.BlockSpec((heads, block), lambda i, g: (0, i)),
                *[pl.BlockSpec((cols, count), lambda i, g: (0, 0))] * sub,
            ],
            scratch_shapes=[pltpu.VMEM((cols, block), BF16)],
        ),
        out_shape=[
            jax.ShapeDtypeStruct((length, width), BF16),
            jax.ShapeDtypeStruct((heads, length), F32),
            *[jax.ShapeDtypeStruct((cols, count), BF16)] * sub,
        ],
        compiler_params=pltpu.CompilerParams(vmem_limit_bytes=VMEM_LIMIT),
        cost_estimate=cost(
            flops=16 * heads * length * length * HEAD_DIM + 2 * length * model_width * width,
            bytes_accessed=4 * length * length,
            transcendentals=heads * length * length,
        ),
        name="attend_forward",
    )(group, slopes, far_dist, w_qkv, *parts)


def attend_backward(qkv, ctx, ctx_grad, lse, far_dist, slopes):
    length, width = qkv.shape
    sub = len(ctx)
    cols = width // 3
    heads = cols // HEAD_DIM
    count = length // sub
    block = 256
    per = count // block

    def body(slope_ref, qkv_ref, lse_ref, dist_ref, *refs):
        ctx_refs, g_refs, out_refs = refs[:sub], refs[sub : 2 * sub], refs[2 * sub : 3 * sub]
        dk_ref, dv_ref, dq_ref, held_ref, inner_ref = refs[3 * sub :]
        step = pl.program_id(0)
        at = pl.ds(pl.multiple_of(step * block, block), block)

        @pl.when(step == 0)
        def _():
            dk_ref[...] = jnp.zeros_like(dk_ref)
            dv_ref[...] = jnp.zeros_like(dv_ref)
            for r in range(sub):
                g = g_refs[r][...]
                both = g.astype(F32) * ctx_refs[r][...].astype(F32)
                for p in range(per):
                    of = slice(p * block, p * block + block)
                    held_ref[r * per + p] = g[:, of]
                    for h in range(heads):
                        inner_ref[r * per + p, h : h + 1, :] = jnp.sum(
                            both[h * 64 : h * 64 + 64, of], axis=0, keepdims=True
                        )

        dist = dist_ref[...]
        for h in range(heads):
            mine = slice(h * 64, h * 64 + 64)
            q = qkv_ref[at, mine]
            k = qkv_ref[:, cols + h * 64 : cols + h * 64 + 64]
            v = qkv_ref[:, 2 * cols + h * 64 : 2 * cols + h * 64 + 64]
            g = held_ref[step, mine, :]
            s = dot(k, q, NT) * SCALE - dist * slope_ref[h]
            p = jnp.exp(s - lse_ref[h : h + 1, :])
            gp = dot(v, g, NN)
            gs = (p * (gp - inner_ref[step, h : h + 1, :])).astype(BF16)
            dv_ref[:, mine] += dot(p.astype(BF16), g, NT)
            dk_ref[:, mine] += dot(gs, q, NN)
            dq_ref[step, mine, :] = (dot(k, gs, TN) * SCALE).astype(BF16)

        @pl.when(step == pl.num_programs(0) - 1)
        def _():
            for r in range(sub):
                of = slice(r * count, r * count + count)
                for p in range(per):
                    out_refs[r][:cols, p * block : p * block + block] = dq_ref[r * per + p]
                out_refs[r][cols : 2 * cols, :] = (dk_ref[of, :] * SCALE).T.astype(BF16)
                out_refs[r][2 * cols :, :] = dv_ref[of, :].T.astype(BF16)

    return pl.pallas_call(
        body,
        grid=(length // block,),
        in_specs=[
            pl.BlockSpec(memory_space=pltpu.SMEM),
            pl.BlockSpec((length, width), lambda i: (0, 0)),
            pl.BlockSpec((heads, block), lambda i: (0, i)),
            pl.BlockSpec((length, block), lambda i: (0, i)),
            *[pl.BlockSpec((cols, count), lambda i: (0, 0))] * (2 * sub),
        ],
        out_specs=[pl.BlockSpec((width, count), lambda i: (0, 0))] * sub,
        out_shape=[jax.ShapeDtypeStruct((width, count), BF16)] * sub,
        scratch_shapes=[
            pltpu.VMEM((length, cols), F32),
            pltpu.VMEM((length, cols), F32),
            pltpu.VMEM((length // block, cols, block), BF16),
            pltpu.VMEM((length // block, cols, block), BF16),
            pltpu.VMEM((length // block, heads, block), F32),
        ],
        compiler_params=pltpu.CompilerParams(vmem_limit_bytes=VMEM_LIMIT),
        cost_estimate=cost(
            flops=8 * heads * length * length * HEAD_DIM,
            bytes_accessed=4 * length * length,
            transcendentals=heads * length * length,
        ),
        name="attend_backward",
    )(slopes, qkv, lse, far_dist, *ctx, *ctx_grad)


def pack_columns(*values):
    rows = [value.shape[-2] for value in values]
    blocks = [value.shape[-1] // PACK for value in values]
    lead = values[0].shape[:-2]
    total = sum(r * n for r, n in zip(rows, blocks))
    if any(r % 8 for r in rows):
        parts = []
        for value in values:
            parts += [value[..., i : i + PACK] for i in range(0, value.shape[-1], PACK)]
        return jnp.concatenate(parts, axis=-2)

    def body(*refs):
        out_ref = refs[-1]
        for i in range(math.prod(lead)):
            at = 0
            for ref, r, n in zip(refs, rows, blocks):
                value = ref[i].astype(F32) if r % 16 else ref[i]
                for j in range(n):
                    out_ref[i, at : at + r, :] = value[:, j * PACK : j * PACK + PACK].astype(BF16)
                    at += r

    flat = [value.reshape(math.prod(lead), *value.shape[-2:]) for value in values]
    return pl.pallas_call(
        body,
        out_shape=jax.ShapeDtypeStruct((math.prod(lead), total, PACK), BF16),
        compiler_params=pltpu.CompilerParams(vmem_limit_bytes=VMEM_LIMIT),
cost_estimate=pl.CostEstimate(flops=1 << 20, bytes_accessed=1 << 10, transcendentals=0),
        name="pack_columns",
    )(*flat).reshape(*lead, total, PACK)


def unpack_plan(width, ff, tok_devices, dp_devices):
    far = dp_devices // 2
    half = width // 2
    row_out, row_down = width // tok_devices, ff // tok_devices
    few = row_out // dp_devices
    plan = [[], [], []]
    for device in range(dp_devices):
        at, core = device // 2, device % 2
        first_cols = ff - far * PACK
        firsts, lasts, heads = [], [], []
        for layer in range(LAYERS):
            firsts.append(
                [
                    (2, layer, 0, core * ff + at * (first_cols // far) + i, row_out)
                    for i in range(0, first_cols // far, PACK)
                ]
            )
            lasts.append(
                [
                    (3, layer, at * (row_down // far), core * half, row_down // far),
                    (1, layer, at * (row_out // far), core * half, row_out // far),
                    (2, layer, 0, core * ff + first_cols + at * PACK, row_out),
                ]
            )
        for i in range(0, 3 * width, PACK):
            for layer in range(LAYERS):
                heads.append((0, layer, device * few, i, few))
        plan[0].append(firsts[0])
        gap = [(None, 0, 0, 0, 8)]
        plan[1].append(lasts[0] + gap + heads)
        plan[2].append(firsts[1] + lasts[1])
    return plan


def assemble(packed, width, ff, tok_devices, dp_devices):
    row_out, row_down = width // tok_devices, ff // tok_devices
    plan = unpack_plan(width, ff, tok_devices, dp_devices)
    shapes = [
        (row_out, LAYERS, 3 * width),
        (row_out, LAYERS, width),
        (row_out, LAYERS, 2 * ff),
        (row_down, LAYERS, width),
    ]
    if row_out // dp_devices % 8:
        outs = [jnp.zeros(shape, F32) for shape in shapes]
        for array, pieces in zip(packed, plan):
            for device in range(dp_devices):
                row = 0
                for out, n, to_row, to_col, count in pieces[device]:
                    if out is not None:
                        piece = array[device, row : row + count].astype(F32)
                        outs[out] = (
                            outs[out].at[to_row : to_row + count, n, to_col : to_col + PACK]
                        ).set(piece)
                    row += count
        return outs

    def body(*refs):
        in_refs, out_refs = refs[: len(plan)], refs[len(plan) :]
        for step in range(2):

            @pl.when(pl.program_id(0) == step)
            def _():
                for ref, pieces in zip(in_refs, plan):
                    for device in range(dp_devices):
                        row = 0
                        for out, n, to_row, to_col, count in pieces[device]:
                            if out is not None:
                                half = shapes[out][0] // 2
                                begin = max(to_row, step * half)
                                end = min(to_row + count, step * half + half)
                                if begin < end:
                                    piece = ref[device, row + begin - to_row : row + end - to_row, :]
                                    out_refs[out][
                                        begin - step * half : end - step * half,
                                        n,
                                        to_col : to_col + PACK,
                                    ] = piece.astype(F32)
                            row += count

    return pl.pallas_call(
        body,
        grid=(2,),
        in_specs=[pl.BlockSpec(v.shape, lambda i: (0, 0, 0)) for v in packed],
        out_specs=[
            pl.BlockSpec((rows // 2, layers, cols), lambda i: (i, 0, 0))
            for rows, layers, cols in shapes
        ],
        out_shape=[jax.ShapeDtypeStruct(shape, F32) for shape in shapes],
        compiler_params=pltpu.CompilerParams(vmem_limit_bytes=VMEM_LIMIT),
        name="assemble",
    )(*packed)


def swap(value, axis, bit):
    return lax.ppermute(value, axis, [(i, i ^ (1 << bit)) for i in range(lax.axis_size(axis))])


def bit_of(axis, bit):
    return (lax.axis_index(axis) >> bit) & 1


def bits_of(axis):
    return lax.axis_size(axis).bit_length() - 1


def add_up(*values):
    total = values[0].astype(F32)
    for value in values[1:]:
        total = total + value.astype(F32)
    return total.astype(BF16)


def reduce_half(value, axis, bit, dim):
    mine = bit_of(axis, bit)
    half = value.shape[dim] // 2
    kept = lax.dynamic_slice_in_dim(value, mine * half, half, dim)
    sent = lax.dynamic_slice_in_dim(value, (1 - mine) * half, half, dim)
    return add_up(kept, swap(sent, axis, bit))


def gather_pair(value, axis, bit, dim):
    mine = bit_of(axis, bit)
    other = swap(value, axis, bit)
    low = jnp.where(mine == 0, value, other)
    high = jnp.where(mine == 0, other, value)
    return jnp.stack((low, high), axis=dim)


def pin(*values):
    return lax.optimization_barrier(values)


def far_bits(sub):
    return [bit for bit in reversed(range(bits_of("tok"))) if (1 << bit) >= sub]


def per_device(
    tokens, mask, segments, replacement, w_qkv, w_out, w_in, w_down, ln_gain, ln_bias, cotangent
):
    tok_devices = lax.axis_size("tok")
    dp_devices = lax.axis_size("dp")
    seq_count, local_len, width = tokens.shape
    ff = w_down.shape[0]
    sub = tok_devices // seq_count
    per_group = HEADS // sub
    cols = per_group * HEAD_DIM
    tok_count = seq_count * local_len
    full_len = local_len * tok_devices
    tok_place = lax.axis_index("tok")
    group = tok_place % sub
    place_of = group.reshape(1)
    core = bit_of("dp", 0).reshape(1)
    side = bit_of("dp", bits_of("dp") - 1).reshape(1)
    near = [[j + sub * k for j in range(sub)] for k in range(seq_count)]
    apart = [[j + sub * k for k in range(seq_count)] for j in range(sub)]

    def regroup(value):
        place = tok_place // sub
        parts = [lax.dynamic_index_in_dim(value, place, 0, False)]
        for r in range(1, seq_count):
            part = lax.dynamic_index_in_dim(value, place ^ r, 0, False)
            to = [(i, i ^ (r * sub)) for i in range(tok_devices)]
            parts.append(lax.ppermute(part, "tok", to))
        if seq_count == 2:
            low = jnp.where(place == 0, parts[0], parts[1])
            return jnp.stack((low, jnp.where(place == 0, parts[1], parts[0])))
        return jnp.stack(parts)[jnp.arange(seq_count) ^ place]

    def spread(value):
        return lax.all_to_all(value, "tok", 0, 0, axis_index_groups=near)

    near_pairs = [[(i, i ^ r) for i in range(tok_devices)] for r in range(1, sub)]

    def deal(parts):
        return [
            parts[0],
            *(lax.ppermute(p, "tok", to) for p, to in zip(parts[1:], near_pairs)),
        ]

    extra = jnp.zeros((seq_count, local_len, LANES), BF16)
    code = (mask == 1).astype(jnp.int32) + 2 * segments
    extra = extra.at[:, :, 0].set(code.astype(BF16))
    mixed = regroup(jnp.concatenate((tokens, extra), axis=-1)).reshape(tok_count, -1)
    wq = split_layers_by_group(w_qkv, sub)
    wo = split_layers(w_out)
    mixed, wq, wo, w_in = pin(mixed, wq, wo, w_in)
    flags = mixed[:, width:]
    masked = flags[:, :1].astype(jnp.int32) % 2 == 1
    current = jnp.where(masked, replacement[None, :], mixed[:, :width].astype(F32))
    flat_in = current.astype(BF16)

    wi = split_layers(w_in)
    slopes = lax.dynamic_slice_in_dim(alibi_slopes(HEADS), group * per_group, per_group, 0)
    order = jnp.arange(sub, dtype=jnp.int32) ^ group
    place = (
        (jnp.arange(seq_count, dtype=jnp.int32)[None, :, None] * sub + order[:, None, None])
        * local_len
        + jnp.arange(local_len, dtype=jnp.int32)[None, None, :]
    ).reshape(full_len)
    far_dist = None
    stored = []
    for layer in range(LAYERS):
        sent = jnp.concatenate((flat_in, flags), axis=-1) if layer == 0 else flat_in
        parts = deal([sent] * sub)
        if layer == 0:
            *parts, wi, w_down = pin(*parts, wi, w_down)
            wd = split_layers(w_down)
            codes = jnp.concatenate([p[:, width] for p in parts]).astype(jnp.int32)
            labels = codes // 2
            masks = (codes % 2).astype(BF16).reshape(sub, 1, tok_count)
            masks = jnp.broadcast_to(masks, (sub, 16, tok_count))
            far_dist = jnp.where(
                labels[:, None] == labels[None, :],
                jnp.abs(place[:, None] - place[None, :]).astype(F32),
                FAR,
            )
        else:
            *parts, stored[0]["lhs_other"] = pin(*parts, stored[0]["lhs_other"])
        qkv, lse, *ctx_here = attend_forward(layer, place_of, parts, wq, far_dist, slopes)
        ctx = deal(ctx_here)
        if layer == 0:
            *ctx, wd, cot = pin(*ctx, wd, regroup(cotangent))
        lhs, a, b, summed, z, current, flat_in = feed_forward(
            layer, place_of, current, ctx, wo, wi, wd, ln_gain, ln_bias
        )
        stored.append(
            {
                "attend": (parts, qkv, ctx_here, lse),
                "feed": (z, summed, a, b),
                "lhs": lhs,
                "lhs_other": swap(lhs, "dp", 0),
            }
        )
    layer_out = flat_in.reshape(seq_count, local_len, width)
    gradient = cot.reshape(tok_count, width).astype(F32)
    small = []
    row_out = width // tok_devices
    row_down = ff // tok_devices
    half = width // 2
    x_bits = list(reversed(range(1, bits_of("dp"))))
    far = dp_devices // 2

    def near_sum(parts):
        return add_up(*deal(parts))

    def x_sum(keep, send, parts):
        total = add_up(keep, swap(send, "dp", x_bits[0]))
        for bit in x_bits[1:]:
            at = bit_of("dp", bit)
            picked = []
            for choice in (at, 1 - at):
                begin, slices = 0, []
                for rows in parts:
                    slices.append(
                        lax.dynamic_slice_in_dim(
                            total, begin + choice * (rows // 2), rows // 2, 1
                        )
                    )
                    begin += rows
                picked.append(jnp.concatenate(slices, axis=1))
            total = add_up(picked[0], swap(picked[1], "dp", bit))
            parts = [rows // 2 for rows in parts]
        return total

    def x_sum_down(keep, send):
        return x_sum(keep, send, [row_down // 2, row_out // 2])

    def x_sum_in(keep, send):
        shape = (tok_devices, -1, PACK)
        return x_sum(keep.reshape(shape), send.reshape(shape), [far // 2 * row_out])

    def x_sum_columns(value):
        for bit in x_bits:
            value = reduce_half(value, "dp", bit, value.ndim - 1)
        return value

    def far_sum(value):
        for bit in far_bits(sub):
            value = reduce_half(value, "tok", bit, 0)
        return value[0]

    def by_place(value):
        return value.reshape(seq_count, sub, *value.shape[1:]).swapaxes(0, 1)

    def spread_sum(value):
        return add_up(*spread(by_place(value)))

    def deal_sum(value):
        value = by_place(value)
        return near_sum(
            [lax.dynamic_index_in_dim(value, group ^ r, 0, False) for r in range(sub)]
        )

    def dp_sum(value):
        return add_up(*lax.all_to_all(value, "dp", 0, 0))

    def by_head(value):
        few = row_out // dp_devices
        value = spread(by_place(value))
        extra = jnp.sum(value[:, :, few : few + 8, :PACK].astype(F32), axis=0).astype(BF16)
        value = jnp.concatenate((value[:, :, :few], value[:, :, few + 8 :]), axis=2)
        value = value.reshape(sub, seq_count, -1, 3, cols)
        return extra, value.transpose(1, 2, 3, 0, 4).reshape(seq_count, -1, 3 * width)

    before = None
    for layer in reversed(range(LAYERS)):
        parts, qkv, ctx_here, lse = stored[layer]["attend"]
        z, summed, a, b = stored[layer]["feed"]
        lhs, lhs_other = stored[layer]["lhs"], stored[layer]["lhs_other"]
        fed = feed_backward(
            layer, core, place_of, gradient, z, summed, a, b, wo, wi, wd, ln_gain, sub
        )
        if before is None:
            *fed, lhs_other = pin(*fed, lhs_other)
        else:
            send = fed[1]
            *fed, late, down, layer_out = pin(
                *fed, near_sum(before["late"]), x_sum_down(*before["down"]), regroup(layer_out)
            )
            fed[1] = send
            first = jnp.concatenate((before["early"], late), axis=2)
            last = jnp.concatenate((down, before["last"]), axis=1)
        mine, send, ga, small_part, *gctx = fed
        small.insert(0, small_part)
        other = swap(send, "dp", 0)
        ctx_grad = deal(gctx)
        if before is not None:
            other, first, last = pin(other, first, last)
        *g_first, keep, sent, keep_in, sent_in = pair_grads(
            place_of, side, lhs, lhs_other, mine, other, ff, tok_devices, sub, far, before is None
        )
        done = (*ctx_grad, keep, sent, keep_in, sent_in, *g_first)
        if before is not None:
            done += (x_sum_columns(first), spread_sum(last))
        done = pin(*done)
        ctx_grad, (keep, sent, keep_in, sent_in) = done[:sub], done[sub : sub + 4]
        done = done[sub + 4 :]
        head_grad = attend_backward(qkv, ctx_here, ctx_grad, lse, far_dist, slopes)
        if before is None:
            both = pin(
                *head_grad, near_sum(done[:sub]), x_sum_in(keep_in, sent_in), keep, sent, *done[sub:]
            )
            head_grad, (early, last, keep, sent, *late) = both[:sub], both[sub:]
            g_qkv = dp_sum(qkv_grad(parts, head_grad, width, tok_devices, dp_devices))
            both = pin(*deal(head_grad), g_qkv, keep, sent, *late)
            back, (g_qkv, keep, sent, *late) = both[:sub], both[sub:]
            before = {
                "early": early,
                "late": late,
                "last": last,
                "down": (keep, sent),
                "qkv": g_qkv,
            }
        else:
            g_first, (first, last) = done[:sub], done[sub:]
            g_qkv = last_grads(
                place_of, small, masks, parts, head_grad, ga, wq,
                tok_devices, dp_devices,
            )
            both = pin(
                *head_grad,
                g_qkv,
                near_sum(g_first),
                x_sum_in(keep_in, sent_in),
                x_sum_down(keep, sent),
                lax.psum_scatter(
                    pack_columns(first, last), "tok", scatter_dimension=0, axis_index_groups=apart
                ),
            )
            head_grad, (g_qkv, g_first, g_last, g_down, before_all) = both[:sub], both[sub:]
            g_last = deal_sum(jnp.concatenate((g_down, g_last), axis=1))
            *head_grad, g_last = pin(*head_grad, g_last)
            g_qkv = jnp.concatenate((dp_sum(g_qkv), before["qkv"]), axis=1)
            both = pin(
                *deal(head_grad),
                *by_head(g_qkv),
                far_sum(pack_columns(x_sum_columns(g_first))),
                g_last,
                before_all,
            )
            back, (*g_qkv, g_first, g_last, before_all) = both[:sub], both[sub:]
            packed = [
                g_first,
                far_sum(pack_columns(g_last, *g_qkv)),
                lax.all_gather(before_all, "dp"),
            ]
        gradient = input_grad(layer, place_of, ga, back, wq)
    packed[0] = packed[0][None]
    for bit in x_bits:
        packed[0] = gather_pair(packed[0], "dp", bit, 1)
        packed[0] = packed[0].reshape(-1, *packed[0].shape[2:])
    gradient, *packed = pin(gradient, *packed)
    grad_tokens = jnp.where(masked, 0.0, gradient).astype(BF16)
    grad_tokens = regroup(grad_tokens.reshape(seq_count, local_len, width))
    value = packed[1][None]
    for bit in x_bits:
        value = gather_pair(value, "dp", bit, 1)
        value = value.reshape(-1, *value.shape[2:])
    value, packed[0], grad_tokens = pin(value, gather_pair(packed[0], "dp", 0, 1), grad_tokens)
    grad_tokens = grad_tokens.astype(F32)
    packed[1] = gather_pair(value, "dp", 0, 1)
    packed[:2] = [v.reshape(dp_devices, *v.shape[2:]) for v in packed[:2]]
    begin = (row_down + row_out) // far + row_out
    few = row_out // dp_devices
    small = packed[1][:, begin : begin + 8].astype(F32)
    small = jnp.concatenate((small[:, :, :few], small[:, :1, LANES : LANES + few]), axis=1)
    small = small.transpose(1, 0, 2).reshape(-1, row_out)
    by_layer = small[: 4 * LAYERS].reshape(LAYERS, 2, 2, row_out)
    return (
        layer_out,
        grad_tokens,
        small[-1],
        *assemble(packed, width, ff, tok_devices, dp_devices),
        by_layer[:, 0],
        by_layer[:, 1],
    )


def solution(mesh):
    in_specs = (
        P("dp", "tok", None),
        P("dp", "tok"),
        P("dp", "tok"),
        P(),
        P(),
        P(),
        P(),
        P(),
        P(),
        P(),
        P("dp", "tok", None),
    )
    out_specs = (
        P("dp", "tok", None),
        P("dp", "tok", None),
        P("tok"),
        P("tok", None, None),
        P("tok", None, None),
        P("tok", None, None),
        P("tok", None, None),
        P(None, None, "tok"),
        P(None, None, "tok"),
    )
    return jax.shard_map(
        per_device, mesh=mesh, in_specs=in_specs, out_specs=out_specs, check_vma=False
    )
```

```python
import functools
import math

import jax
import jax.numpy as jnp
from jax import lax
from jax.experimental import pallas as pl
from jax.experimental.pallas import tpu as pltpu
from jax.sharding import PartitionSpec as P

HEADS = 12
HEAD_DIM = 64
LAYERS = 2
LANES = 128
PACK = 384
SCALE = 1.0 / math.sqrt(HEAD_DIM)
FAR = 1e30
BF16 = jnp.bfloat16
F32 = jnp.float32
VMEM_LIMIT = 56 << 20
COST_TIMES = 4


def alibi_slopes(head_count):
    head_index = jnp.arange(head_count, dtype=jnp.float32)
    return jnp.exp2(jnp.where(head_index < 8.0, -(head_index + 1.0), 7.5 - head_index))


def dot(a, b, dims):
    return lax.dot_general(a, b, (dims, ((), ())), preferred_element_type=F32)


def cost(flops, bytes_accessed, transcendentals):
    return pl.CostEstimate(
        flops=COST_TIMES * flops,
        bytes_accessed=bytes_accessed,
        transcendentals=transcendentals,
    )


NN = ((1,), (0,))
NT = ((1,), (1,))
TN = ((0,), (0,))


def split_layers(weight):
    rows, _, cols = weight.shape
    row_block = 256
    col_block = next(c for c in (3072, 2304, 1152, 768) if cols % c == 0)

    def body(in_ref, out_ref):
        to_row = lax.broadcasted_iota(jnp.int32, (256, 256), 0)
        from_row = lax.broadcasted_iota(jnp.int32, (256, 256), 1)
        wanted = jnp.where(to_row < 128, 2 * to_row, 2 * to_row - 255)
        pick = jnp.where(from_row == wanted, 1.0, 0.0).astype(BF16)
        for part in range(row_block // 128):
            at = slice(part * 128, part * 128 + 128)
            mixed = in_ref[at].reshape(256, col_block)
            picked = dot(pick, mixed, NN).astype(BF16)
            out_ref[0, at] = picked[:128]
            out_ref[1, at] = picked[128:]

    return pl.pallas_call(
        body,
        grid=(rows // row_block, cols // col_block),
        in_specs=[pl.BlockSpec((row_block, 2, col_block), lambda i, j: (i, 0, j))],
        out_specs=pl.BlockSpec((2, row_block, col_block), lambda i, j: (0, i, j)),
        out_shape=jax.ShapeDtypeStruct((2, rows, cols), BF16),
        compiler_params=pltpu.CompilerParams(vmem_limit_bytes=VMEM_LIMIT),
        cost_estimate=cost(
            flops=2 * 512 * rows * cols, bytes_accessed=8 * rows * cols, transcendentals=0
        ),
        name="split_layers",
    )(weight)


def split_layers_by_group(weight, sub):
    rows, _, cols = weight.shape
    row_block = 256
    group_cols = cols // sub // 3

    def body(in_ref, out_ref):
        to_row = lax.broadcasted_iota(jnp.int32, (256, 256), 0)
        from_row = lax.broadcasted_iota(jnp.int32, (256, 256), 1)
        wanted = jnp.where(to_row < 128, 2 * to_row, 2 * to_row - 255)
        pick = jnp.where(from_row == wanted, 1.0, 0.0).astype(BF16)
        for part in range(row_block // 128):
            at = slice(part * 128, part * 128 + 128)
            picked = dot(pick, in_ref[at].reshape(256, cols), NN).astype(BF16)
            for j in range(sub):
                for n in range(3):
                    first = (n * sub + j) * group_cols
                    block = picked[:, first : first + group_cols]
                    to = slice(n * group_cols, n * group_cols + group_cols)
                    out_ref[0, j, at, to] = block[:128]
                    out_ref[1, j, at, to] = block[128:]

    return pl.pallas_call(
        body,
        grid=(rows // row_block,),
        in_specs=[pl.BlockSpec((row_block, 2, cols), lambda i: (i, 0, 0))],
        out_specs=pl.BlockSpec((2, sub, row_block, 3 * group_cols), lambda i: (0, 0, i, 0)),
        out_shape=jax.ShapeDtypeStruct((2, sub, rows, 3 * group_cols), BF16),
        compiler_params=pltpu.CompilerParams(vmem_limit_bytes=VMEM_LIMIT),
        cost_estimate=cost(
            flops=2 * 512 * rows * cols, bytes_accessed=8 * rows * cols, transcendentals=0
        ),
        name="split_qkv",
    )(weight)


def norm_parts(value):
    center = jnp.mean(value, axis=-1, keepdims=True)
    shifted = value - center
    inverse = lax.rsqrt(jnp.mean(shifted * shifted, axis=-1, keepdims=True) + 1e-12)
    return shifted * inverse, inverse


def norm_grad(grad, value, gain):
    normed, inverse = norm_parts(value)
    scaled = grad * gain
    one = jnp.mean(scaled, axis=-1, keepdims=True)
    two = jnp.mean(scaled * normed, axis=-1, keepdims=True)
    in_grad = inverse * (scaled - one - normed * two)
    gain_grad = jnp.sum(grad * normed, axis=0, keepdims=True)
    bias_grad = jnp.sum(grad, axis=0, keepdims=True)
    return in_grad, gain_grad, bias_grad


def feed_forward(layer, group, current, ctx, w_out, w_in, w_down, gain, bias):
    count, width = current.shape
    sub, cols = len(ctx), ctx[0].shape[0]
    ff = w_down.shape[1]
    chunk = 1536
    steps = ff // chunk

    def body(group_ref, *refs):
        ctx_refs = refs[:sub]
        cur_ref, wo_ref, wg_ref, wu_ref, wd_ref, gain_ref, bias_ref = refs[sub : sub + 7]
        lhs_ref, a_ref, b_ref, sum_ref, z_ref, next_ref, low_ref = refs[sub + 7 : sub + 14]
        y1l_ref, acc_ref, held_ref = refs[sub + 14 :]
        step = pl.program_id(0)

        @pl.when(step == 0)
        def _():
            branch = jnp.zeros((count, width), F32)
            for r in range(sub):
                held_ref[jnp.bitwise_xor(group_ref[0], r)] = ctx_refs[r][...]
            for j in range(sub):
                part = held_ref[j]
                to = slice(j * cols, j * cols + cols)
                lhs_ref[:, width + ff + j * cols : width + ff + j * cols + cols] = (
                    part.astype(F32).T.astype(BF16)
                )
                branch += dot(part, wo_ref[0, to, :], TN)
            summed = cur_ref[...] + branch
            sum_ref[...] = summed
            normed, _ = norm_parts(summed)
            y1 = normed * gain_ref[layer, 0:1, :] + bias_ref[layer, 0:1, :]
            acc_ref[...] = y1
            y1l_ref[...] = y1.astype(BF16)
            lhs_ref[:, :width] = y1.astype(BF16)

        y1l = y1l_ref[...]
        gate = dot(y1l, wg_ref[0], NN)
        up = dot(y1l, wu_ref[0], NN)
        cdf = 0.5 * (1.0 + lax.erf(gate * (0.5**0.5)))
        density = jnp.exp(-0.5 * gate * gate) * (1.0 / math.sqrt(2.0 * math.pi))
        gelu = gate * cdf
        hidden = (gelu * up).astype(BF16)
        a_ref[...] = gelu.astype(BF16)
        b_ref[...] = (up * (cdf + gate * density)).astype(BF16)
        lhs_ref[:, pl.ds(pl.multiple_of(width + step * chunk, 128), chunk)] = hidden
        acc_ref[...] += dot(hidden, wd_ref[0], NN)

        @pl.when(step == steps - 1)
        def _():
            z = acc_ref[...]
            z_ref[...] = z
            normed, _ = norm_parts(z)
            out = normed * gain_ref[layer, 1:2, :] + bias_ref[layer, 1:2, :]
            next_ref[...] = out
            low_ref[...] = out.astype(BF16)

    whole = lambda *shape: pl.BlockSpec(shape, lambda i: (0,) * len(shape))
    return pl.pallas_call(
        body,
        grid=(steps,),
        in_specs=[
            pl.BlockSpec(memory_space=pltpu.SMEM),
            *[whole(cols, count)] * sub,
            whole(count, width),
            pl.BlockSpec((1, width, width), lambda i: (layer, 0, 0)),
            pl.BlockSpec((1, width, chunk), lambda i: (layer, 0, i)),
            pl.BlockSpec((1, width, chunk), lambda i: (layer, 0, steps + i)),
            pl.BlockSpec((1, chunk, width), lambda i: (layer, i, 0)),
            whole(*gain.shape),
            whole(*bias.shape),
        ],
        out_specs=[
            whole(count, ff + 2 * width),
            pl.BlockSpec((count, chunk), lambda i: (0, i)),
            pl.BlockSpec((count, chunk), lambda i: (0, i)),
            whole(count, width),
            whole(count, width),
            whole(count, width),
            whole(count, width),
        ],
        out_shape=[
            jax.ShapeDtypeStruct((count, ff + 2 * width), BF16),
            jax.ShapeDtypeStruct((count, ff), BF16),
            jax.ShapeDtypeStruct((count, ff), BF16),
            jax.ShapeDtypeStruct((count, width), F32),
            jax.ShapeDtypeStruct((count, width), F32),
            jax.ShapeDtypeStruct((count, width), F32),
            jax.ShapeDtypeStruct((count, width), BF16),
        ],
        scratch_shapes=[
            pltpu.VMEM((count, width), BF16),
            pltpu.VMEM((count, width), F32),
            pltpu.VMEM((sub, cols, count), BF16),
        ],
        compiler_params=pltpu.CompilerParams(vmem_limit_bytes=VMEM_LIMIT),
        cost_estimate=cost(
            flops=2 * count * width * (width + 3 * ff),
            bytes_accessed=6 * width * ff + 2 * width * width + count * (20 * width + 6 * ff),
            transcendentals=2 * count * ff,
        ),
        name="feed_forward",
    )(group, *ctx, current, w_out, w_in, w_in, w_down, gain, bias)


def feed_backward(layer, core, group, grad, z, summed, a, b, w_out, w_in, w_down, gain, sub):
    count, width = grad.shape
    ff = w_down.shape[1]
    cols = width // sub
    half = width // 2
    chunk = 768
    steps = ff // chunk

    def body(
        core_ref, group_ref, grad_ref, z_ref, sum_ref, a_ref, b_ref,
        wo_ref, wg_ref, wu_ref, wd_ref, gain_ref, mine_ref, send_ref, ga_ref, small_ref, *refs,
    ):
        gctx_refs = refs[:sub]
        gzl_ref, acc_ref, held_ref = refs[sub:]
        step = pl.program_id(0)
        first = core_ref[0] == 0

        def store(to, low, high):
            mine_ref[:, to] = jnp.where(first, low, high)
            send_ref[:, to] = jnp.where(first, high, low)

        @pl.when(step == 0)
        def _():
            gz, gain_grad, bias_grad = norm_grad(grad_ref[...], z_ref[...], gain_ref[layer, 1:2, :])
            small_ref[1:2, :] = gain_grad
            small_ref[3:4, :] = bias_grad
            acc_ref[...] = gz
            gzl = gz.astype(BF16)
            gzl_ref[...] = gzl
            store(slice(ff, ff + half), gz[:, :half].astype(BF16), gz[:, half:].astype(BF16))

        gzl = gzl_ref[...]
        ghid = dot(gzl, wd_ref[0], NT)
        ggate = (ghid * b_ref[...].astype(F32)).astype(BF16)
        gup = (ghid * a_ref[...].astype(F32)).astype(BF16)
        store(pl.ds(pl.multiple_of(step * chunk, 128), chunk), ggate, gup)
        acc_ref[...] += dot(ggate, wg_ref[0], NT) + dot(gup, wu_ref[0], NT)

        @pl.when(step == steps - 1)
        def _():
            ga, gain_grad, bias_grad = norm_grad(
                acc_ref[...], sum_ref[...], gain_ref[layer, 0:1, :]
            )
            small_ref[0:1, :] = gain_grad
            small_ref[2:3, :] = bias_grad
            ga_ref[...] = ga
            gal = ga.astype(BF16)
            store(slice(ff + half, ff + width), gal[:, :half], gal[:, half:])
            for j in range(sub):
                to = slice(j * cols, j * cols + cols)
                held_ref[j] = dot(wo_ref[0, to, :], gal, NT).astype(BF16)
            for r in range(sub):
                gctx_refs[r][...] = held_ref[jnp.bitwise_xor(group_ref[0], r)]

    whole = lambda *shape: pl.BlockSpec(shape, lambda i: (0,) * len(shape))
    return pl.pallas_call(
        body,
        grid=(steps,),
        in_specs=[
            pl.BlockSpec(memory_space=pltpu.SMEM),
            pl.BlockSpec(memory_space=pltpu.SMEM),
            whole(count, width),
            whole(count, width),
            whole(count, width),
            pl.BlockSpec((count, chunk), lambda i: (0, i)),
            pl.BlockSpec((count, chunk), lambda i: (0, i)),
            pl.BlockSpec((1, width, width), lambda i: (layer, 0, 0)),
            pl.BlockSpec((1, width, chunk), lambda i: (layer, 0, i)),
            pl.BlockSpec((1, width, chunk), lambda i: (layer, 0, steps + i)),
            pl.BlockSpec((1, chunk, width), lambda i: (layer, i, 0)),
            whole(*gain.shape),
        ],
        out_specs=[
            whole(count, ff + width),
            whole(count, ff + width),
            whole(count, width),
            whole(4, width),
            *[whole(cols, count)] * sub,
        ],
        out_shape=[
            jax.ShapeDtypeStruct((count, ff + width), BF16),
            jax.ShapeDtypeStruct((count, ff + width), BF16),
            jax.ShapeDtypeStruct((count, width), F32),
            jax.ShapeDtypeStruct((4, width), F32),
            *[jax.ShapeDtypeStruct((cols, count), BF16)] * sub,
        ],
        scratch_shapes=[
            pltpu.VMEM((count, width), BF16),
            pltpu.VMEM((count, width), F32),
            pltpu.VMEM((sub, cols, count), BF16),
        ],
        compiler_params=pltpu.CompilerParams(vmem_limit_bytes=VMEM_LIMIT),
        cost_estimate=cost(
            flops=2 * count * width * (width + 3 * ff),
            bytes_accessed=6 * width * ff + 2 * width * width + count * (24 * width + 8 * ff),
            transcendentals=0,
        ),
        name="feed_backward",
    )(core, group, grad, z, summed, a, b, w_out, w_in, w_in, w_down, gain)


def pair_grads(group, side, lhs, lhs_other, rhs, rhs_other, ff, tok_devices, sub, far, early):
    count = lhs.shape[0]
    width = rhs.shape[1] - ff
    half = width // 2
    rows, rows_down = width // tok_devices, ff // tok_devices
    seqs = tok_devices // sub
    chunk = 2 * PACK
    steps_in, steps_down = ff // chunk, ff // chunk
    first_steps = steps_in - far * PACK // chunk
    ends = [0, 1, first_steps] if early else [0, first_steps]
    spans = list(zip(ends[:-1], ends[1:]))
    split = far // 2
    half_down, half_out = rows_down // 2, rows // 2

    def body(group_ref, side_ref, l1_ref, l2_ref, r1_ref, r2_ref, h1_ref, h2_ref, *refs):
        out_refs = refs[: len(spans) * sub]
        keep_ref, send_ref, keep_in_ref, send_in_ref, held_ref = refs[len(spans) * sub :]
        step = pl.program_id(0)
        low_side = side_ref[0] == 0

        def store(t, at, low, high):
            keep_ref[t, at] = jnp.where(low_side, low, high).astype(BF16)
            send_ref[t, at] = jnp.where(low_side, high, low).astype(BF16)

        @pl.when(step < steps_in)
        def _():
            out = dot(l1_ref[...], r1_ref[...], TN) + dot(l2_ref[...], r2_ref[...], TN)

            @pl.when(step < first_steps)
            def _():
                for t in range(tok_devices):
                    held_ref[t % sub, t // sub] = out[t * rows : t * rows + rows].astype(BF16)

            for n, (begin, end) in enumerate(spans):

                @pl.when((step >= begin) & (step < end))
                def _():
                    for r in range(sub):
                        out_refs[n * sub + r][...] = held_ref[jnp.bitwise_xor(group_ref[0], r)]

            for f in range(2):
                block = 2 * (step - first_steps) + f
                here = block // split == side_ref[0]
                to = block % split
                for wanted, ref in ((here, keep_in_ref), (jnp.logical_not(here), send_in_ref)):

                    @pl.when((step >= first_steps) & wanted)
                    def _():
                        for t in range(tok_devices):
                            part = out[t * rows : t * rows + rows, f * PACK : f * PACK + PACK]
                            ref[t, to] = part.astype(BF16)

        @pl.when(step >= steps_in)
        def _():
            out = dot(l1_ref[...], h1_ref[...], TN) + dot(l2_ref[...], h2_ref[...], TN)
            each = chunk // rows_down

            @pl.when(step < steps_in + steps_down)
            def _():
                for i in range(each):
                    low = out[i * rows_down : i * rows_down + half_down]
                    high = out[i * rows_down + half_down : (i + 1) * rows_down]
                    store((step - steps_in) * each + i, slice(0, half_down), low, high)

            @pl.when(step == steps_in + steps_down)
            def _():
                for t in range(tok_devices):
                    low = out[t * rows : t * rows + half_out]
                    high = out[t * rows + half_out : (t + 1) * rows]
                    store(t, slice(half_down, half_down + half_out), low, high)

    left = pl.BlockSpec((count, chunk), lambda i: (0, jnp.maximum(i - steps_in + 1, 0)))
    right = pl.BlockSpec((count, chunk), lambda i: (0, jnp.minimum(i, steps_in - 1)))
    halves = pl.BlockSpec(
        (count, half), lambda i: (0, ff // half + jnp.where(i < steps_in + steps_down, 0, 1))
    )
    kept = (tok_devices, half_down + half_out, half)
    kept_in = (tok_devices, split, rows, PACK)
    whole = lambda *shape: pl.BlockSpec(shape, lambda i: (0,) * len(shape))
    return pl.pallas_call(
        body,
        grid=(steps_in + steps_down + 1,),
        in_specs=[
            pl.BlockSpec(memory_space=pltpu.SMEM),
            pl.BlockSpec(memory_space=pltpu.SMEM),
            left,
            left,
            right,
            right,
            halves,
            halves,
        ],
        out_specs=[
            *[
                pl.BlockSpec(
                    (seqs, rows, chunk),
                    functools.partial(
                        lambda begin, end, i: (0, 0, jnp.clip(i - begin, 0, end - begin - 1)),
                        begin,
                        end,
                    ),
                )
                for begin, end in spans
                for _ in range(sub)
            ],
            whole(*kept),
            whole(*kept),
            whole(*kept_in),
            whole(*kept_in),
        ],
        out_shape=[
            *[
                jax.ShapeDtypeStruct((seqs, rows, (end - begin) * chunk), BF16)
                for begin, end in spans
                for _ in range(sub)
            ],
            jax.ShapeDtypeStruct(kept, BF16),
            jax.ShapeDtypeStruct(kept, BF16),
            jax.ShapeDtypeStruct(kept_in, BF16),
            jax.ShapeDtypeStruct(kept_in, BF16),
        ],
        scratch_shapes=[pltpu.VMEM((sub, seqs, rows, chunk), BF16)],
        compiler_params=pltpu.CompilerParams(vmem_limit_bytes=VMEM_LIMIT),
        cost_estimate=cost(
            flops=8 * count * width * ff,
            bytes_accessed=4 * width * ff + 8 * count * (width + ff),
            transcendentals=0,
        ),
        name="pair_grads",
    )(group, side, lhs, lhs_other, rhs, rhs_other, rhs, rhs_other)


def input_grad(layer, group, ga, back, w_qkv):
    sub = len(back)
    cols, count = back[0].shape
    width = ga.shape[1]

    def body(group_ref, ga_ref, w_ref, *refs):
        back_refs, out_ref, acc_ref = refs[:sub], refs[sub], refs[sub + 1]
        step = pl.program_id(0)

        @pl.when(step == 0)
        def _():
            acc_ref[...] = jnp.zeros_like(acc_ref)

        for r in range(sub):

            @pl.when(step == r)
            def _():
                acc_ref[...] += dot(w_ref[0, 0], back_refs[r][...], NN)

        @pl.when(step == sub - 1)
        def _():
            out_ref[...] = ga_ref[...] + acc_ref[...].T

    return pl.pallas_call(
        body,
        grid_spec=pltpu.PrefetchScalarGridSpec(
            num_scalar_prefetch=1,
            grid=(sub,),
            in_specs=[
                pl.BlockSpec((count, width), lambda i, g: (0, 0)),
                pl.BlockSpec(
                    (1, 1, width, cols), lambda i, g: (layer, jnp.bitwise_xor(g[0], i), 0, 0)
                ),
                *[pl.BlockSpec((cols, count), lambda i, g: (0, 0))] * sub,
            ],
            out_specs=pl.BlockSpec((count, width), lambda i, g: (0, 0)),
            scratch_shapes=[pltpu.VMEM((width, count), F32)],
        ),
        out_shape=jax.ShapeDtypeStruct((count, width), F32),
        compiler_params=pltpu.CompilerParams(vmem_limit_bytes=VMEM_LIMIT),
        cost_estimate=cost(
            flops=2 * count * width * cols * sub,
            bytes_accessed=2 * sub * cols * (width + count) + 8 * count * width,
            transcendentals=0,
        ),
        name="input_grad",
    )(group, ga, w_qkv, *back)


def qkv_grad(parts, grads, width, tok_devices, dp_devices):
    sub = len(parts)
    count = parts[0].shape[0]
    cols = grads[0].shape[0]
    rows = width // tok_devices
    few = rows // dp_devices

    def body(*refs):
        qkv_grad_body(refs[:sub], refs[sub : 2 * sub], refs[2 * sub], rows, few)

    shape = (dp_devices, tok_devices, few, cols)
    return pl.pallas_call(
        body,
        grid=(1,),
        in_specs=[
            *[pl.BlockSpec((count, width), lambda i: (0, 0))] * sub,
            *[pl.BlockSpec((cols, count), lambda i: (0, 0))] * sub,
        ],
        out_specs=pl.BlockSpec(shape, lambda i: (0, 0, 0, 0)),
        out_shape=jax.ShapeDtypeStruct(shape, BF16),
        compiler_params=pltpu.CompilerParams(vmem_limit_bytes=VMEM_LIMIT),
        cost_estimate=pl.CostEstimate(flops=1 << 20, bytes_accessed=1 << 10, transcendentals=0),
        name="qkv_grad",
    )(*parts, *grads)


def qkv_grad_body(part_refs, grad_refs, out_ref, rows, few):
    cols, width = grad_refs[0].shape[0], part_refs[0].shape[1]
    acc = jnp.zeros((cols, width), F32)
    for part_ref, grad_ref in zip(part_refs, grad_refs):
        acc += dot(grad_ref[...], part_ref[...], NN)
    acc = acc.T
    dp_devices, tok_devices = out_ref.shape[:2]
    for t in range(tok_devices):
        for q in range(dp_devices):
            first = t * rows + q * few
            out_ref[q, t, :few, :] = acc[first : first + few].astype(BF16)


def last_grads(group, small, masks, parts, grads, ga, w_qkv, tok_devices, dp_devices):
    sub = len(grads)
    cols, count = grads[0].shape
    width = ga.shape[1]
    rows = width // tok_devices
    few = rows // dp_devices

    def twice(value):
        high = value.astype(BF16)
        return high, (value - high.astype(F32)).astype(BF16)

    def body(group_ref, mask_ref, ga_ref, w_ref, *refs):
        small_refs, refs = refs[:LAYERS], refs[LAYERS:]
        part_refs, grad_refs, out_ref = refs[:sub], refs[sub : 2 * sub], refs[2 * sub]
        qkv_grad_body(part_refs, grad_refs, out_ref, rows, few)
        total = jnp.zeros((16, cols), F32)
        for r in range(sub):
            total += dot(mask_ref[r], grad_refs[r][...], NT)
        mask_sum = jnp.zeros((16, width), F32)
        for part in twice(total):
            mask_sum += dot(part, w_ref[0, 0], NT)
        for part in twice(ga_ref[...]):
            mask_sum += dot(mask_ref[0], part, NN)
        values = jnp.concatenate([ref[...] for ref in small_refs], axis=0)
        for t in range(tok_devices):
            for q in range(dp_devices):
                of = slice(t * rows + q * few, t * rows + q * few + few)
                row = jnp.concatenate(
                    (
                        jnp.pad(values[:, of], ((0, 0), (0, LANES - few))),
                        jnp.pad(mask_sum[:8, of], ((0, 0), (0, cols - LANES - few))),
                    ),
                    axis=1,
                )
                out_ref[q, t, few:, :] = row.astype(BF16)

    whole = lambda *shape: pl.BlockSpec(shape, lambda i, g: (0,) * len(shape))
    shape = (dp_devices, tok_devices, few + 8, cols)
    return pl.pallas_call(
        body,
        grid_spec=pltpu.PrefetchScalarGridSpec(
            num_scalar_prefetch=1,
            grid=(1,),
            in_specs=[
                whole(sub, 16, count),
                whole(count, width),
                pl.BlockSpec((1, 1, width, cols), lambda i, g: (0, g[0], 0, 0)),
                *[whole(8 // LAYERS, width)] * LAYERS,
                *[whole(count, width)] * sub,
                *[whole(cols, count)] * sub,
            ],
            out_specs=whole(*shape),
        ),
        out_shape=jax.ShapeDtypeStruct(shape, BF16),
        compiler_params=pltpu.CompilerParams(vmem_limit_bytes=VMEM_LIMIT),
        cost_estimate=pl.CostEstimate(flops=1 << 20, bytes_accessed=1 << 10, transcendentals=0),
        name="last_grads",
    )(group, masks, ga, w_qkv, *small, *parts, *grads)


def attend_forward(layer, group, parts, w_qkv, far_dist, slopes):
    sub = len(parts)
    count, length = parts[0].shape[0], far_dist.shape[0]
    model_width, width = w_qkv.shape[2:]
    cols = width // 3
    heads = cols // HEAD_DIM
    block = 256
    per = count // block

    def body(group_ref, slope_ref, dist_ref, w_ref, *refs):
        part_refs, (qkv_ref, lse_ref) = refs[:sub], refs[sub : sub + 2]
        ctx_refs, held_ref = refs[sub + 2 : 2 * sub + 2], refs[2 * sub + 2]
        step = pl.program_id(0)

        @pl.when(step == 0)
        def _():
            for r in range(sub):
                qkv_ref[r * count : r * count + count, :] = dot(
                    part_refs[r][...], w_ref[0, 0], NN
                ).astype(BF16)

        at = pl.ds(pl.multiple_of(step * block, block), block)
        dist = dist_ref[...]
        for h in range(heads):
            q = qkv_ref[at, h * 64 : h * 64 + 64]
            k = qkv_ref[:, cols + h * 64 : cols + h * 64 + 64]
            v = qkv_ref[:, 2 * cols + h * 64 : 2 * cols + h * 64 + 64]
            s = dot(k, q, NT) * SCALE - dist * slope_ref[h]
            top = jnp.max(s, axis=0, keepdims=True)
            e = jnp.exp(s - top)
            total = jnp.sum(e, axis=0, keepdims=True)
            ctx = dot(v, e.astype(BF16), TN) / total
            held_ref[h * 64 : h * 64 + 64, :] = ctx.astype(BF16)
            lse_ref[h : h + 1, :] = top + jnp.log(total)
        for i in range(length // block):

            @pl.when(step == i)
            def _():
                first = i % per * block
                ctx_refs[i // per][:, first : first + block] = held_ref[...]

    return pl.pallas_call(
        body,
        grid_spec=pltpu.PrefetchScalarGridSpec(
            num_scalar_prefetch=1,
            grid=(length // block,),
            in_specs=[
                pl.BlockSpec(memory_space=pltpu.SMEM),
                pl.BlockSpec((length, block), lambda i, g: (0, i)),
                pl.BlockSpec((1, 1, model_width, width), lambda i, g: (layer, g[0], 0, 0)),
                *[pl.BlockSpec((count, model_width), lambda i, g: (0, 0))] * sub,
            ],
            out_specs=[
                pl.BlockSpec((length, width), lambda i, g: (0, 0)),
                pl.BlockSpec((heads, block), lambda i, g: (0, i)),
                *[pl.BlockSpec((cols, count), lambda i, g: (0, 0))] * sub,
            ],
            scratch_shapes=[pltpu.VMEM((cols, block), BF16)],
        ),
        out_shape=[
            jax.ShapeDtypeStruct((length, width), BF16),
            jax.ShapeDtypeStruct((heads, length), F32),
            *[jax.ShapeDtypeStruct((cols, count), BF16)] * sub,
        ],
        compiler_params=pltpu.CompilerParams(vmem_limit_bytes=VMEM_LIMIT),
        cost_estimate=cost(
            flops=16 * heads * length * length * HEAD_DIM + 2 * length * model_width * width,
            bytes_accessed=4 * length * length,
            transcendentals=heads * length * length,
        ),
        name="attend_forward",
    )(group, slopes, far_dist, w_qkv, *parts)


def attend_backward(qkv, ctx, ctx_grad, lse, far_dist, slopes):
    length, width = qkv.shape
    sub = len(ctx)
    cols = width // 3
    heads = cols // HEAD_DIM
    count = length // sub
    block = 256
    per = count // block

    def body(slope_ref, qkv_ref, lse_ref, dist_ref, *refs):
        ctx_refs, g_refs, out_refs = refs[:sub], refs[sub : 2 * sub], refs[2 * sub : 3 * sub]
        dk_ref, dv_ref, dq_ref, held_ref, inner_ref = refs[3 * sub :]
        step = pl.program_id(0)
        at = pl.ds(pl.multiple_of(step * block, block), block)

        @pl.when(step == 0)
        def _():
            dk_ref[...] = jnp.zeros_like(dk_ref)
            dv_ref[...] = jnp.zeros_like(dv_ref)
            for r in range(sub):
                g = g_refs[r][...]
                both = g.astype(F32) * ctx_refs[r][...].astype(F32)
                for p in range(per):
                    of = slice(p * block, p * block + block)
                    held_ref[r * per + p] = g[:, of]
                    for h in range(heads):
                        inner_ref[r * per + p, h : h + 1, :] = jnp.sum(
                            both[h * 64 : h * 64 + 64, of], axis=0, keepdims=True
                        )

        dist = dist_ref[...]
        for h in range(heads):
            mine = slice(h * 64, h * 64 + 64)
            q = qkv_ref[at, mine]
            k = qkv_ref[:, cols + h * 64 : cols + h * 64 + 64]
            v = qkv_ref[:, 2 * cols + h * 64 : 2 * cols + h * 64 + 64]
            g = held_ref[step, mine, :]
            s = dot(k, q, NT) * SCALE - dist * slope_ref[h]
            p = jnp.exp(s - lse_ref[h : h + 1, :])
            gp = dot(v, g, NN)
            gs = (p * (gp - inner_ref[step, h : h + 1, :])).astype(BF16)
            dv_ref[:, mine] += dot(p.astype(BF16), g, NT)
            dk_ref[:, mine] += dot(gs, q, NN)
            dq_ref[step, mine, :] = (dot(k, gs, TN) * SCALE).astype(BF16)

        @pl.when(step == pl.num_programs(0) - 1)
        def _():
            for r in range(sub):
                of = slice(r * count, r * count + count)
                for p in range(per):
                    out_refs[r][:cols, p * block : p * block + block] = dq_ref[r * per + p]
                out_refs[r][cols : 2 * cols, :] = (dk_ref[of, :] * SCALE).T.astype(BF16)
                out_refs[r][2 * cols :, :] = dv_ref[of, :].T.astype(BF16)

    return pl.pallas_call(
        body,
        grid=(length // block,),
        in_specs=[
            pl.BlockSpec(memory_space=pltpu.SMEM),
            pl.BlockSpec((length, width), lambda i: (0, 0)),
            pl.BlockSpec((heads, block), lambda i: (0, i)),
            pl.BlockSpec((length, block), lambda i: (0, i)),
            *[pl.BlockSpec((cols, count), lambda i: (0, 0))] * (2 * sub),
        ],
        out_specs=[pl.BlockSpec((width, count), lambda i: (0, 0))] * sub,
        out_shape=[jax.ShapeDtypeStruct((width, count), BF16)] * sub,
        scratch_shapes=[
            pltpu.VMEM((length, cols), F32),
            pltpu.VMEM((length, cols), F32),
            pltpu.VMEM((length // block, cols, block), BF16),
            pltpu.VMEM((length // block, cols, block), BF16),
            pltpu.VMEM((length // block, heads, block), F32),
        ],
        compiler_params=pltpu.CompilerParams(vmem_limit_bytes=VMEM_LIMIT),
        cost_estimate=cost(
            flops=8 * heads * length * length * HEAD_DIM,
            bytes_accessed=4 * length * length,
            transcendentals=heads * length * length,
        ),
        name="attend_backward",
    )(slopes, qkv, lse, far_dist, *ctx, *ctx_grad)


def pack_columns(*values):
    rows = [value.shape[-2] for value in values]
    blocks = [value.shape[-1] // PACK for value in values]
    lead = values[0].shape[:-2]
    total = sum(r * n for r, n in zip(rows, blocks))
    if any(r % 8 for r in rows):
        parts = []
        for value in values:
            parts += [value[..., i : i + PACK] for i in range(0, value.shape[-1], PACK)]
        return jnp.concatenate(parts, axis=-2)

    def body(*refs):
        out_ref = refs[-1]
        for i in range(math.prod(lead)):
            at = 0
            for ref, r, n in zip(refs, rows, blocks):
                value = ref[i].astype(F32) if r % 16 else ref[i]
                for j in range(n):
                    out_ref[i, at : at + r, :] = value[:, j * PACK : j * PACK + PACK].astype(BF16)
                    at += r

    flat = [value.reshape(math.prod(lead), *value.shape[-2:]) for value in values]
    return pl.pallas_call(
        body,
        out_shape=jax.ShapeDtypeStruct((math.prod(lead), total, PACK), BF16),
        compiler_params=pltpu.CompilerParams(vmem_limit_bytes=VMEM_LIMIT),
cost_estimate=pl.CostEstimate(flops=1 << 20, bytes_accessed=1 << 10, transcendentals=0),
        name="pack_columns",
    )(*flat).reshape(*lead, total, PACK)


def unpack_plan(width, ff, tok_devices, dp_devices):
    far = dp_devices // 2
    half = width // 2
    row_out, row_down = width // tok_devices, ff // tok_devices
    few = row_out // dp_devices
    plan = [[], [], []]
    for device in range(dp_devices):
        at, core = device // 2, device % 2
        first_cols = ff - far * PACK
        firsts, lasts, heads = [], [], []
        for layer in range(LAYERS):
            firsts.append(
                [
                    (2, layer, 0, core * ff + at * (first_cols // far) + i, row_out)
                    for i in range(0, first_cols // far, PACK)
                ]
            )
            lasts.append(
                [
                    (3, layer, at * (row_down // far), core * half, row_down // far),
                    (1, layer, at * (row_out // far), core * half, row_out // far),
                    (2, layer, 0, core * ff + first_cols + at * PACK, row_out),
                ]
            )
        for i in range(0, 3 * width, PACK):
            for layer in range(LAYERS):
                heads.append((0, layer, device * few, i, few))
        plan[0].append(firsts[0])
        gap = [(None, 0, 0, 0, 8)]
        plan[1].append(lasts[0] + gap + heads)
        plan[2].append(firsts[1] + lasts[1])
    return plan


def assemble(packed, width, ff, tok_devices, dp_devices):
    row_out, row_down = width // tok_devices, ff // tok_devices
    plan = unpack_plan(width, ff, tok_devices, dp_devices)
    shapes = [
        (row_out, LAYERS, 3 * width),
        (row_out, LAYERS, width),
        (row_out, LAYERS, 2 * ff),
        (row_down, LAYERS, width),
    ]
    if row_out // dp_devices % 8:
        outs = [jnp.zeros(shape, F32) for shape in shapes]
        for array, pieces in zip(packed, plan):
            for device in range(dp_devices):
                row = 0
                for out, n, to_row, to_col, count in pieces[device]:
                    if out is not None:
                        piece = array[device, row : row + count].astype(F32)
                        outs[out] = (
                            outs[out].at[to_row : to_row + count, n, to_col : to_col + PACK]
                        ).set(piece)
                    row += count
        return outs

    def body(*refs):
        in_refs, out_refs = refs[: len(plan)], refs[len(plan) :]
        for step in range(2):

            @pl.when(pl.program_id(0) == step)
            def _():
                for ref, pieces in zip(in_refs, plan):
                    for device in range(dp_devices):
                        row = 0
                        for out, n, to_row, to_col, count in pieces[device]:
                            if out is not None:
                                half = shapes[out][0] // 2
                                begin = max(to_row, step * half)
                                end = min(to_row + count, step * half + half)
                                if begin < end:
                                    piece = ref[device, row + begin - to_row : row + end - to_row, :]
                                    out_refs[out][
                                        begin - step * half : end - step * half,
                                        n,
                                        to_col : to_col + PACK,
                                    ] = piece.astype(F32)
                            row += count

    return pl.pallas_call(
        body,
        grid=(2,),
        in_specs=[pl.BlockSpec(v.shape, lambda i: (0, 0, 0)) for v in packed],
        out_specs=[
            pl.BlockSpec((rows // 2, layers, cols), lambda i: (i, 0, 0))
            for rows, layers, cols in shapes
        ],
        out_shape=[jax.ShapeDtypeStruct(shape, F32) for shape in shapes],
        compiler_params=pltpu.CompilerParams(vmem_limit_bytes=VMEM_LIMIT),
        name="assemble",
    )(*packed)


def swap(value, axis, bit):
    return lax.ppermute(value, axis, [(i, i ^ (1 << bit)) for i in range(lax.axis_size(axis))])


def bit_of(axis, bit):
    return (lax.axis_index(axis) >> bit) & 1


def bits_of(axis):
    return lax.axis_size(axis).bit_length() - 1


def add_up(*values):
    total = values[0].astype(F32)
    for value in values[1:]:
        total = total + value.astype(F32)
    return total.astype(BF16)


def reduce_half(value, axis, bit, dim):
    mine = bit_of(axis, bit)
    half = value.shape[dim] // 2
    kept = lax.dynamic_slice_in_dim(value, mine * half, half, dim)
    sent = lax.dynamic_slice_in_dim(value, (1 - mine) * half, half, dim)
    return add_up(kept, swap(sent, axis, bit))


def gather_pair(value, axis, bit, dim):
    mine = bit_of(axis, bit)
    other = swap(value, axis, bit)
    low = jnp.where(mine == 0, value, other)
    high = jnp.where(mine == 0, other, value)
    return jnp.stack((low, high), axis=dim)


def pin(*values):
    return lax.optimization_barrier(values)


def far_bits(sub):
    return [bit for bit in reversed(range(bits_of("tok"))) if (1 << bit) >= sub]


def per_device(
    tokens, mask, segments, replacement, w_qkv, w_out, w_in, w_down, ln_gain, ln_bias, cotangent
):
    tok_devices = lax.axis_size("tok")
    dp_devices = lax.axis_size("dp")
    seq_count, local_len, width = tokens.shape
    ff = w_down.shape[0]
    sub = tok_devices // seq_count
    per_group = HEADS // sub
    cols = per_group * HEAD_DIM
    tok_count = seq_count * local_len
    full_len = local_len * tok_devices
    tok_place = lax.axis_index("tok")
    group = tok_place % sub
    place_of = group.reshape(1)
    core = bit_of("dp", 0).reshape(1)
    side = bit_of("dp", bits_of("dp") - 1).reshape(1)
    near = [[j + sub * k for j in range(sub)] for k in range(seq_count)]
    apart = [[j + sub * k for k in range(seq_count)] for j in range(sub)]

    def regroup(value):
        place = tok_place // sub
        parts = [lax.dynamic_index_in_dim(value, place, 0, False)]
        for r in range(1, seq_count):
            part = lax.dynamic_index_in_dim(value, place ^ r, 0, False)
            to = [(i, i ^ (r * sub)) for i in range(tok_devices)]
            parts.append(lax.ppermute(part, "tok", to))
        if seq_count == 2:
            low = jnp.where(place == 0, parts[0], parts[1])
            return jnp.stack((low, jnp.where(place == 0, parts[1], parts[0])))
        return jnp.stack(parts)[jnp.arange(seq_count) ^ place]

    def spread(value):
        return lax.all_to_all(value, "tok", 0, 0, axis_index_groups=near)

    near_pairs = [[(i, i ^ r) for i in range(tok_devices)] for r in range(1, sub)]

    def deal(parts):
        return [
            parts[0],
            *(lax.ppermute(p, "tok", to) for p, to in zip(parts[1:], near_pairs)),
        ]

    extra = jnp.zeros((seq_count, local_len, LANES), BF16)
    code = (mask == 1).astype(jnp.int32) + 2 * segments
    extra = extra.at[:, :, 0].set(code.astype(BF16))
    mixed = regroup(jnp.concatenate((tokens, extra), axis=-1)).reshape(tok_count, -1)
    wq = split_layers_by_group(w_qkv, sub)
    wo = split_layers(w_out)
    mixed, wq, wo, w_in = pin(mixed, wq, wo, w_in)
    flags = mixed[:, width:]
    masked = flags[:, :1].astype(jnp.int32) % 2 == 1
    current = jnp.where(masked, replacement[None, :], mixed[:, :width].astype(F32))
    flat_in = current.astype(BF16)

    wi = split_layers(w_in)
    slopes = lax.dynamic_slice_in_dim(alibi_slopes(HEADS), group * per_group, per_group, 0)
    order = jnp.arange(sub, dtype=jnp.int32) ^ group
    place = (
        (jnp.arange(seq_count, dtype=jnp.int32)[None, :, None] * sub + order[:, None, None])
        * local_len
        + jnp.arange(local_len, dtype=jnp.int32)[None, None, :]
    ).reshape(full_len)
    far_dist = None
    stored = []
    for layer in range(LAYERS):
        sent = jnp.concatenate((flat_in, flags), axis=-1) if layer == 0 else flat_in
        parts = deal([sent] * sub)
        if layer == 0:
            *parts, wi, w_down = pin(*parts, wi, w_down)
            wd = split_layers(w_down)
            codes = jnp.concatenate([p[:, width] for p in parts]).astype(jnp.int32)
            labels = codes // 2
            masks = (codes % 2).astype(BF16).reshape(sub, 1, tok_count)
            masks = jnp.broadcast_to(masks, (sub, 16, tok_count))
            far_dist = jnp.where(
                labels[:, None] == labels[None, :],
                jnp.abs(place[:, None] - place[None, :]).astype(F32),
                FAR,
            )
        else:
            *parts, stored[0]["lhs_other"] = pin(*parts, stored[0]["lhs_other"])
        qkv, lse, *ctx_here = attend_forward(layer, place_of, parts, wq, far_dist, slopes)
        ctx = deal(ctx_here)
        if layer == 0:
            *ctx, wd, cot = pin(*ctx, wd, regroup(cotangent))
        lhs, a, b, summed, z, current, flat_in = feed_forward(
            layer, place_of, current, ctx, wo, wi, wd, ln_gain, ln_bias
        )
        stored.append(
            {
                "attend": (parts, qkv, ctx_here, lse),
                "feed": (z, summed, a, b),
                "lhs": lhs,
                "lhs_other": swap(lhs, "dp", 0),
            }
        )
    layer_out = flat_in.reshape(seq_count, local_len, width)
    gradient = cot.reshape(tok_count, width).astype(F32)
    small = []
    row_out = width // tok_devices
    row_down = ff // tok_devices
    half = width // 2
    x_bits = list(reversed(range(1, bits_of("dp"))))
    far = dp_devices // 2

    def near_sum(parts):
        return add_up(*deal(parts))

    def x_sum(keep, send, parts):
        total = add_up(keep, swap(send, "dp", x_bits[0]))
        for bit in x_bits[1:]:
            at = bit_of("dp", bit)
            picked = []
            for choice in (at, 1 - at):
                begin, slices = 0, []
                for rows in parts:
                    slices.append(
                        lax.dynamic_slice_in_dim(
                            total, begin + choice * (rows // 2), rows // 2, 1
                        )
                    )
                    begin += rows
                picked.append(jnp.concatenate(slices, axis=1))
            total = add_up(picked[0], swap(picked[1], "dp", bit))
            parts = [rows // 2 for rows in parts]
        return total

    def x_sum_down(keep, send):
        return x_sum(keep, send, [row_down // 2, row_out // 2])

    def x_sum_in(keep, send):
        shape = (tok_devices, -1, PACK)
        return x_sum(keep.reshape(shape), send.reshape(shape), [far // 2 * row_out])

    def x_sum_columns(value):
        for bit in x_bits:
            value = reduce_half(value, "dp", bit, value.ndim - 1)
        return value

    def far_sum(value):
        for bit in far_bits(sub):
            value = reduce_half(value, "tok", bit, 0)
        return value[0]

    def by_place(value):
        return value.reshape(seq_count, sub, *value.shape[1:]).swapaxes(0, 1)

    def spread_sum(value):
        return add_up(*spread(by_place(value)))

    def deal_sum(value):
        value = by_place(value)
        return near_sum(
            [lax.dynamic_index_in_dim(value, group ^ r, 0, False) for r in range(sub)]
        )

    def dp_sum(value):
        return add_up(*lax.all_to_all(value, "dp", 0, 0))

    def by_head(value):
        few = row_out // dp_devices
        value = spread(by_place(value))
        extra = jnp.sum(value[:, :, few : few + 8, :PACK].astype(F32), axis=0).astype(BF16)
        value = jnp.concatenate((value[:, :, :few], value[:, :, few + 8 :]), axis=2)
        value = value.reshape(sub, seq_count, -1, 3, cols)
        return extra, value.transpose(1, 2, 3, 0, 4).reshape(seq_count, -1, 3 * width)

    before = None
    for layer in reversed(range(LAYERS)):
        parts, qkv, ctx_here, lse = stored[layer]["attend"]
        z, summed, a, b = stored[layer]["feed"]
        lhs, lhs_other = stored[layer]["lhs"], stored[layer]["lhs_other"]
        fed = feed_backward(
            layer, core, place_of, gradient, z, summed, a, b, wo, wi, wd, ln_gain, sub
        )
        if before is None:
            *fed, lhs_other = pin(*fed, lhs_other)
        else:
            send = fed[1]
            *fed, late, down, layer_out = pin(
                *fed, near_sum(before["late"]), x_sum_down(*before["down"]), regroup(layer_out)
            )
            fed[1] = send
            first = jnp.concatenate((before["early"], late), axis=2)
            last = jnp.concatenate((down, before["last"]), axis=1)
        mine, send, ga, small_part, *gctx = fed
        small.insert(0, small_part)
        other = swap(send, "dp", 0)
        ctx_grad = deal(gctx)
        if before is not None:
            other, first, last = pin(other, first, last)
        *g_first, keep, sent, keep_in, sent_in = pair_grads(
            place_of, side, lhs, lhs_other, mine, other, ff, tok_devices, sub, far, before is None
        )
        done = (*ctx_grad, keep, sent, keep_in, sent_in, *g_first)
        if before is not None:
            done += (x_sum_columns(first), spread_sum(last))
        done = pin(*done)
        ctx_grad, (keep, sent, keep_in, sent_in) = done[:sub], done[sub : sub + 4]
        done = done[sub + 4 :]
        head_grad = attend_backward(qkv, ctx_here, ctx_grad, lse, far_dist, slopes)
        if before is None:
            both = pin(
                *head_grad, near_sum(done[:sub]), x_sum_in(keep_in, sent_in), keep, sent, *done[sub:]
            )
            head_grad, (early, last, keep, sent, *late) = both[:sub], both[sub:]
            g_qkv = dp_sum(qkv_grad(parts, head_grad, width, tok_devices, dp_devices))
            both = pin(*deal(head_grad), g_qkv, keep, sent, *late)
            back, (g_qkv, keep, sent, *late) = both[:sub], both[sub:]
            before = {
                "early": early,
                "late": late,
                "last": last,
                "down": (keep, sent),
                "qkv": g_qkv,
            }
        else:
            g_first, (first, last) = done[:sub], done[sub:]
            g_qkv = last_grads(
                place_of, small, masks, parts, head_grad, ga, wq,
                tok_devices, dp_devices,
            )
            both = pin(
                *head_grad,
                g_qkv,
                near_sum(g_first),
                x_sum_in(keep_in, sent_in),
                x_sum_down(keep, sent),
                lax.psum_scatter(
                    pack_columns(first, last), "tok", scatter_dimension=0, axis_index_groups=apart
                ),
            )
            head_grad, (g_qkv, g_first, g_last, g_down, before_all) = both[:sub], both[sub:]
            g_last = deal_sum(jnp.concatenate((g_down, g_last), axis=1))
            *head_grad, g_last = pin(*head_grad, g_last)
            g_qkv = jnp.concatenate((dp_sum(g_qkv), before["qkv"]), axis=1)
            both = pin(
                *deal(head_grad),
                *by_head(g_qkv),
                far_sum(pack_columns(x_sum_columns(g_first))),
                g_last,
                before_all,
            )
            back, (*g_qkv, g_first, g_last, before_all) = both[:sub], both[sub:]
            packed = [
                g_first,
                far_sum(pack_columns(g_last, *g_qkv)),
                lax.all_gather(before_all, "dp"),
            ]
        gradient = input_grad(layer, place_of, ga, back, wq)
    packed[0] = packed[0][None]
    for bit in x_bits:
        packed[0] = gather_pair(packed[0], "dp", bit, 1)
        packed[0] = packed[0].reshape(-1, *packed[0].shape[2:])
    gradient, *packed = pin(gradient, *packed)
    grad_tokens = jnp.where(masked, 0.0, gradient).astype(BF16)
    grad_tokens = regroup(grad_tokens.reshape(seq_count, local_len, width))
    value = packed[1][None]
    for bit in x_bits:
        value = gather_pair(value, "dp", bit, 1)
        value = value.reshape(-1, *value.shape[2:])
    value, packed[0], grad_tokens = pin(value, gather_pair(packed[0], "dp", 0, 1), grad_tokens)
    grad_tokens = grad_tokens.astype(F32)
    packed[1] = gather_pair(value, "dp", 0, 1)
    packed[:2] = [v.reshape(dp_devices, *v.shape[2:]) for v in packed[:2]]
    begin = (row_down + row_out) // far + row_out
    few = row_out // dp_devices
    small = packed[1][:, begin : begin + 8].astype(F32)
    small = jnp.concatenate((small[:, :, :few], small[:, :1, LANES : LANES + few]), axis=1)
    small = small.transpose(1, 0, 2).reshape(-1, row_out)
    by_layer = small[: 4 * LAYERS].reshape(LAYERS, 2, 2, row_out)
    return (
        layer_out,
        grad_tokens,
        small[-1],
        *assemble(packed, width, ff, tok_devices, dp_devices),
        by_layer[:, 0],
        by_layer[:, 1],
    )


def solution(mesh):
    in_specs = (
        P("dp", "tok", None),
        P("dp", "tok"),
        P("dp", "tok"),
        P(),
        P(),
        P(),
        P(),
        P(),
        P(),
        P(),
        P("dp", "tok", None),
    )
    out_specs = (
        P("dp", "tok", None),
        P("dp", "tok", None),
        P("tok"),
        P("tok", None, None),
        P("tok", None, None),
        P("tok", None, None),
        P("tok", None, None),
        P(None, None, "tok"),
        P(None, None, "tok"),
    )
    return jax.shard_map(
        per_device, mesh=mesh, in_specs=in_specs, out_specs=out_specs, check_vma=False
    )
```
